32 devices in a mesh: dp: 32 (over z, y, x, core).
Axes of the slice: x: 2, y: 2, z: 4, core: 2. Of those that a mesh axis runs over, the one named last changes fastest.
Arguments:
- tokens: bfloat16 [8192, 1024], P('dp'), may hold values from -6 to 6
- memory: bfloat16 [65536, 1024], P('dp'), may hold values from -6 to 6
- target_lengths: int32 [32], P('dp'), may hold values from 128 to 256, as said below
- memory_lengths: int32 [32], P('dp'), may hold values from 1024 to 2048, as said below
- cotangent: bfloat16 [8192, 1024], P('dp'), may hold values from -6 to 6
- self_query: bfloat16 [1024, 1024], P('dp'), may hold values from -0.1875 to 0.1875
- self_key: bfloat16 [1024, 1024], P('dp'), may hold values from -0.1875 to 0.1875
- self_value: bfloat16 [1024, 1024], P('dp'), may hold values from -0.1875 to 0.1875
- self_output: bfloat16 [1024, 1024], P('dp'), may hold values from -0.75 to 0.75
- first_gain: bfloat16 [1024], P('dp'), may hold values from 0.5 to 1.5
- first_shift: bfloat16 [1024], P('dp'), may hold values from -3 to 3
- cross_query: bfloat16 [1024, 1024], P('dp'), may hold values from -0.1875 to 0.1875
- cross_key: bfloat16 [1024, 1024], P('dp'), may hold values from -0.1875 to 0.1875
- cross_value: bfloat16 [1024, 1024], P('dp'), may hold values from -0.1875 to 0.1875
- cross_output: bfloat16 [1024, 1024], P('dp'), may hold values from -1.5 to 1.5
- second_gain: bfloat16 [1024], P('dp'), may hold values from 0.5 to 1.5
- second_shift: bfloat16 [1024], P('dp'), may hold values from -3 to 3
- inner_weight: bfloat16 [1024, 4096], P('dp'), may hold values from -0.1875 to 0.1875
- outer_weight: bfloat16 [4096, 1024], P('dp'), may hold values from -0.09375 to 0.09375
- third_gain: bfloat16 [1024], P('dp'), may hold values from 0.5 to 1.5
- third_shift: bfloat16 [1024], P('dp'), may hold values from -3 to 3
Outputs:
- output: bfloat16 [8192, 1024], P('dp')
- tokens_grad: float32 [8192, 1024], P('dp')
- memory_grad: float32 [65536, 1024], P('dp')
- grad_self_query: float32 [1024, 1024], P('dp')
- grad_self_key: float32 [1024, 1024], P('dp')
- grad_self_value: float32 [1024, 1024], P('dp')
- grad_self_output: float32 [1024, 1024], P('dp')
- grad_first_gain: float32 [1024], P('dp')
- grad_first_shift: float32 [1024], P('dp')
- grad_cross_query: float32 [1024, 1024], P('dp')
- grad_cross_key: float32 [1024, 1024], P('dp')
- grad_cross_value: float32 [1024, 1024], P('dp')
- grad_cross_output: float32 [1024, 1024], P('dp')
- grad_second_gain: float32 [1024], P('dp')
- grad_second_shift: float32 [1024], P('dp')
- grad_inner_weight: float32 [1024, 4096], P('dp')
- grad_outer_weight: float32 [4096, 1024], P('dp')
- grad_third_gain: float32 [1024], P('dp')
- grad_third_shift: float32 [1024], P('dp')
The draws below stay inside these ranges and needn't reach their ends.
Inputs may be any that keep to these rules, and one draw needn't show every extreme that they name: `target_lengths`: some question has exactly 256 live target tokens. `memory_lengths`: some question has exactly 2048 live memory tokens.
All inputs are finite; a program needn't handle non-finite values.
Results may differ from the reference program's by a relative error of at most 0.02.
The reference program's roundings to bfloat16 on the way count: a program that leaves them out, or rounds other values in their place, can miss the bound.
Values may be sent and summed in bfloat16 or wider, within the bound.
A program may use at most 256 MiB of HBM per device.

```python
import math
from functools import partial
import jax
import jax.numpy as jnp
from jax import lax

D = 1024
HEADS = 16
HEAD = 64
FF = 4096
TGT = 256
MEM = 2048
QUESTIONS = 32
TOKENS = 8192
MEMORY = 65536


def draw_target_lengths(key, part):
    key = jax.random.fold_in(key, 11)
    first_key, second_key = jax.random.split(key)
    lengths = jax.random.randint(first_key, (QUESTIONS,), TGT // 2, TGT + 1)
    chosen = jax.random.randint(second_key, (), 0, QUESTIONS)
    return jnp.where(jnp.arange(QUESTIONS) == chosen, TGT, lengths).astype(jnp.int32)


def draw_memory_lengths(key, part):
    key = jax.random.fold_in(key, 23)
    first_key, second_key = jax.random.split(key)
    lengths = jax.random.randint(first_key, (QUESTIONS,), MEM // 2, MEM + 1)
    chosen = jax.random.randint(second_key, (), 0, QUESTIONS)
    return jnp.where(jnp.arange(QUESTIONS) == chosen, MEM, lengths).astype(jnp.int32)


def block_scale(rng, extent, cuts, smallest, top_value):
    level, own = 1.0, jax.random.fold_in(rng, 6)
    for axis_at, shards_of in cuts:
        heights = jnp.exp(jax.random.uniform(jax.random.fold_in(own, axis_at), (shards_of,), jnp.float32, smallest / len(cuts), top_value / len(cuts)))
        level = level * jnp.repeat(heights, extent[axis_at] // shards_of).reshape([-1 if axis == axis_at else 1 for axis in range(len(extent))])
    return level


def noise(own_key, dims, width, bound, cuts=(), held_as=jnp.bfloat16):
    level = block_scale(own_key, dims, cuts, -0.22, 0.18) if cuts else 1.0
    entries = jax.random.normal(own_key, dims, jnp.float32) * width * level
    return jnp.minimum(jnp.maximum(entries, -bound), bound).astype(held_as)


def setup_inputs(seed: int = 0) -> dict:
    key_list = jax.random.split(jax.random.key(seed), 22)
    tokens = noise(key_list[0], (TOKENS, D), 1.0, 6.0, ((0, 32),))
    memory = noise(key_list[1], (MEMORY, D), 1.0, 6.0, ((0, 32),))
    target_lengths = draw_target_lengths(jax.random.fold_in(key_list[21], 71), 0)
    memory_lengths = draw_memory_lengths(jax.random.fold_in(key_list[21], 71), 0)
    cotangent = noise(key_list[4], (TOKENS, D), 1.0, 6.0, ((0, 32),))
    self_query = noise(key_list[5], (D, D), D ** -0.5, 0.1875, ((0, 32),))
    self_key = noise(key_list[6], (D, D), D ** -0.5, 0.1875, ((0, 32),))
    self_value = noise(key_list[7], (D, D), D ** -0.5, 0.1875, ((0, 32),))
    self_output = noise(key_list[8], (D, D), (D // 16) ** -0.5, 0.75, ((0, 32),))
    first_gain = jnp.clip(1.0 + 0.1 * jax.random.normal(key_list[9], (D,), jnp.float32), 0.5, 1.5).astype(jnp.bfloat16)
    first_shift = noise(key_list[10], (D,), 0.5, 3.0, ((0, 32),))
    cross_query = noise(key_list[11], (D, D), D ** -0.5, 0.1875, ((0, 32),))
    cross_key = noise(key_list[12], (D, D), D ** -0.5, 0.1875, ((0, 32),))
    cross_value = noise(key_list[13], (D, D), D ** -0.5, 0.1875, ((0, 32),))
    cross_output = noise(key_list[14], (D, D), (D // 64) ** -0.5, 1.5, ((0, 32),))
    second_gain = jnp.clip(1.0 + 0.1 * jax.random.normal(key_list[15], (D,), jnp.float32), 0.5, 1.5).astype(jnp.bfloat16)
    second_shift = noise(key_list[16], (D,), 0.5, 3.0, ((0, 32),))
    inner_weight = noise(key_list[17], (D, FF), D ** -0.5, 0.1875, ((0, 32),))
    outer_weight = noise(key_list[18], (FF, D), FF ** -0.5, 0.09375, ((0, 32),))
    third_gain = jnp.clip(1.0 + 0.1 * jax.random.normal(key_list[19], (D,), jnp.float32), 0.5, 1.5).astype(jnp.bfloat16)
    third_shift = noise(key_list[20], (D,), 0.5, 3.0, ((0, 32),))
    return dict(tokens=tokens, memory=memory, target_lengths=target_lengths, memory_lengths=memory_lengths, cotangent=cotangent, self_query=self_query, self_key=self_key, self_value=self_value, self_output=self_output, first_gain=first_gain, first_shift=first_shift, cross_query=cross_query, cross_key=cross_key, cross_value=cross_value, cross_output=cross_output, second_gain=second_gain, second_shift=second_shift, inner_weight=inner_weight, outer_weight=outer_weight, third_gain=third_gain, third_shift=third_shift)


@jax.custom_vjp
def low(v):
    return lax.optimization_barrier(v.astype(jnp.bfloat16)).astype(jnp.float32)

@jax.custom_vjp
def low_back(v):
    return v

def low_keep(v):
    return (low(v), None)

def low_pass(kept, grad):
    return (grad,)

def back_keep(v):
    return (v, None)

def back_low(kept, grad):
    return (low(grad),)
low.defvjp(low_keep, low_pass)
low_back.defvjp(back_keep, back_low)

def matmul(operand, factor):
    return jnp.dot(operand, factor, precision=lax.Precision.HIGHEST, preferred_element_type=jnp.float32)

def rounded(values):
    return low_back(low(values))

def layer_norm(summed, norm_gain, norm_shift):
    average = lax.optimization_barrier(jnp.mean(summed, axis=-1, keepdims=True))
    centred = summed - average
    spread = lax.optimization_barrier(jnp.mean(centred * centred, axis=-1, keepdims=True))
    return centred * lax.rsqrt(spread + 1e-05) * norm_gain + norm_shift

def exact_gelu(inner_pre):
    return jax.nn.gelu(inner_pre, approximate=False)

def attention(query_rows, key_rows, value_rows, allowed):
    row_count = query_rows.shape[0]
    key_count = key_rows.shape[0]
    query_heads = query_rows.reshape(row_count, HEADS, HEAD)
    key_heads = key_rows.reshape(key_count, HEADS, HEAD)
    value_heads = value_rows.reshape(key_count, HEADS, HEAD)
    score_scale = 1.0 / math.sqrt(HEAD)
    scores = low_back(jnp.einsum('qhd,khd->hqk', query_heads, key_heads, precision=lax.Precision.HIGHEST) * score_scale)
    scores = jnp.where(allowed[None], scores, -1e+30)
    prob_rows = low(jax.nn.softmax(scores, axis=-1))
    mixture = jnp.einsum('hqk,khd->qhd', prob_rows, value_heads, precision=lax.Precision.HIGHEST)
    return rounded(mixture.reshape(row_count, HEADS * HEAD))

def self_question(pieces):
    query_rows, key_rows, value_rows, length = pieces
    positions = jnp.arange(TGT)
    allowed = (positions[None, :] <= positions[:, None]) & (positions[None, :] < length)
    return attention(query_rows, key_rows, value_rows, allowed)

def cross_question(pieces):
    query_rows, key_rows, value_rows, length = pieces
    allowed = jnp.broadcast_to(jnp.arange(MEM)[None, :] < length, (TGT, MEM))
    return attention(query_rows, key_rows, value_rows, allowed)

def forward(target_lengths, memory_lengths, tokens, memory, self_query, self_key, self_value, self_output, first_gain, first_shift, cross_query, cross_key, cross_value, cross_output, second_gain, second_shift, inner_weight, outer_weight, third_gain, third_shift):
    queries = rounded(matmul(tokens, self_query))
    key_rows = rounded(matmul(tokens, self_key))
    value_rows = rounded(matmul(tokens, self_value))
    self_mixture = lax.map(jax.checkpoint(self_question), (queries.reshape(QUESTIONS, TGT, D), key_rows.reshape(QUESTIONS, TGT, D), value_rows.reshape(QUESTIONS, TGT, D), target_lengths)).reshape(TOKENS, D)
    first_sum = tokens + low_back(matmul(self_mixture, self_output))
    first_out = layer_norm(first_sum, first_gain, first_shift)
    cross_queries = rounded(matmul(low(first_out), cross_query))
    cross_keys = rounded(matmul(memory, cross_key))
    cross_values = rounded(matmul(memory, cross_value))
    cross_mixture = lax.map(jax.checkpoint(cross_question), (cross_queries.reshape(QUESTIONS, TGT, D), cross_keys.reshape(QUESTIONS, MEM, D), cross_values.reshape(QUESTIONS, MEM, D), memory_lengths)).reshape(TOKENS, D)
    second_sum = first_out + low_back(matmul(cross_mixture, cross_output))
    second = layer_norm(second_sum, second_gain, second_shift)
    inner_pre = low_back(matmul(low(second), inner_weight))
    activated = low(exact_gelu(inner_pre))
    third_sum = second + low_back(matmul(activated, outer_weight))
    return layer_norm(third_sum, third_gain, third_shift)

def reference(tokens, memory, target_lengths, memory_lengths, cotangent, self_query, self_key, self_value, self_output, first_gain, first_shift, cross_query, cross_key, cross_value, cross_output, second_gain, second_shift, inner_weight, outer_weight, third_gain, third_shift):
    floats = tuple((operand.astype(jnp.float32) for operand in (tokens, memory, self_query, self_key, self_value, self_output, first_gain, first_shift, cross_query, cross_key, cross_value, cross_output, second_gain, second_shift, inner_weight, outer_weight, third_gain, third_shift)))
    output, pullback = jax.vjp(partial(forward, target_lengths, memory_lengths), *floats)
    gradients = pullback(cotangent.astype(jnp.float32))
    return (output.astype(jnp.bfloat16), gradients[0], gradients[1], gradients[2], gradients[3], gradients[4], gradients[5], gradients[6], gradients[7], gradients[8], gradients[9], gradients[10], gradients[11], gradients[12], gradients[13], gradients[14], gradients[15], gradients[16], gradients[17])
```

```python
import functools
import math

import jax
import jax.numpy as jnp
from jax import lax
from jax.experimental import pallas as pl
from jax.experimental.pallas import tpu as pltpu
from jax.sharding import PartitionSpec as P

HEAD = 64
EPS = 1e-05
SCALE = 1.0 / math.sqrt(HEAD)
LOG2E = 1.4426950408889634
BLOCKS = 32
MIB = 1024 * 1024
F32 = jnp.float32
BF16 = jnp.bfloat16


def nn(a, b):
    return jnp.dot(a, b, preferred_element_type=F32)


def nt(a, b):
    return lax.dot_general(a, b, (((1,), (1,)), ((), ())), preferred_element_type=F32)


def tn(a, b):
    return lax.dot_general(a, b, (((0,), (0,)), ((), ())), preferred_element_type=F32)


def whole(ref):
    return ref[...].reshape(-1, ref.shape[-1])


def call(body, name, out, grid=(), ins=None, outs=None, scratch=(), prefetch=0, limit=56, flops=0, moved=0):
    return pl.pallas_call(
        body,
        out_shape=out,
        grid_spec=pltpu.PrefetchScalarGridSpec(
            num_scalar_prefetch=prefetch,
            grid=grid,
            in_specs=ins,
            out_specs=outs,
            scratch_shapes=scratch,
        ),
        compiler_params=pltpu.CompilerParams(vmem_limit_bytes=limit * MIB),
        cost_estimate=pl.CostEstimate(flops=flops, bytes_accessed=moved, transcendentals=0),
        name=name,
    )


def full(shape):
    return pl.BlockSpec(shape, lambda *_: (0,) * len(shape))


def weight(at):
    return pl.BlockSpec((BLOCKS, 32, 1024), lambda *_: (0, at, 0))


def shape(dims, dtype):
    return jax.ShapeDtypeStruct(dims, dtype)


def norm_parts(summed):
    average = jnp.mean(summed, axis=-1, keepdims=True)
    centred = summed - average
    spread = jnp.mean(centred * centred, axis=-1, keepdims=True)
    scale = lax.rsqrt(spread + EPS)
    return centred * scale, scale


def norm_back(summed, gain, upstream):
    normal, scale = norm_parts(summed)
    grad_gain = jnp.sum(upstream * normal, axis=0, keepdims=True)
    grad_shift = jnp.sum(upstream, axis=0, keepdims=True)
    scaled = upstream * gain
    first = jnp.mean(scaled, axis=-1, keepdims=True)
    second = jnp.mean(scaled * normal, axis=-1, keepdims=True)
    return scale * (scaled - first - normal * second), grad_gain, grad_shift


def lanes(rows):
    return lax.broadcasted_iota(jnp.int32, (rows, 128), 1)


def stack_pair(rows):
    low = lanes(rows.shape[0]) < HEAD
    zero = jnp.zeros_like(rows)
    return jnp.concatenate([jnp.where(low, rows, zero), jnp.where(low, zero, rows)], axis=0)


def unstack_pair(stacked):
    half = stacked.shape[0] // 2
    return jnp.where(lanes(half) < HEAD, stacked[:half], stacked[half:])


def pair_forward(stacked, keys, values, mask):
    scores = nt(stacked, keys)
    if mask is not None:
        scores = mask(scores)
    peak = jnp.max(scores, axis=-1, keepdims=True)
    raised = jnp.exp2((scores - peak) * (SCALE * LOG2E))
    total = jnp.sum(raised, axis=-1, keepdims=True)
    mixed = nn(raised.astype(BF16), values) / total
    return mixed, peak * SCALE + jnp.log(total)


def pair_tile_back(q2, g2, keys, values, totals, inner, mask):
    scores = nt(keys, q2)
    probs = jnp.exp2(scores * (SCALE * LOG2E) - totals)
    if mask is not None:
        probs = mask(probs)
    grad_probs = nt(values, g2)
    grad_scores = (probs * (grad_probs - inner)).astype(BF16)
    grad_values = nn(probs.astype(BF16), g2)
    grad_keys = nn(grad_scores, q2) * SCALE
    grad_queries = tn(keys, grad_scores)
    return grad_queries, grad_keys, grad_values


def pair_inner(mixture, grad):
    product = mixture.astype(F32) * grad.astype(F32)
    half = jnp.where(
        (lax.broadcasted_iota(jnp.int32, (8, 128), 1) // HEAD)
        == lax.broadcasted_iota(jnp.int32, (8, 128), 0),
        1.0,
        0.0,
    ).astype(F32)
    sums = lax.dot_general(
        half, product, (((1,), (1,)), ((), ())),
        preferred_element_type=F32, precision=lax.Precision.HIGHEST,
    )
    return jnp.concatenate([sums[0:1], sums[1:2]], axis=1)


def join_grad_queries(grad):
    count = grad.shape[1] // 2
    joined = jnp.concatenate([grad[:HEAD, :count], grad[HEAD:, count:]], axis=0) * SCALE
    return joined.T.astype(BF16)


def kv_body(memory, wk, wv, keys, values):
    rows = memory[...]
    keys[...] = nn(rows, whole(wk)).astype(BF16)
    values[...] = nn(rows, whole(wv)).astype(BF16)


def kv_project(memory, stack, at_k, at_v):
    count, width = memory.shape
    tile = 512
    spec = pl.BlockSpec((tile, width), lambda i: (i, 0))
    return call(
        kv_body, "cross_kv", [shape(memory.shape, BF16)] * 2, (count // tile,),
        [spec, weight(at_k), weight(at_v)], [spec, spec],
        flops=4 * count * width * width, moved=12 * MIB + 4 * MIB,
    )(memory, stack, stack)


def self_body(length, tokens, wq, wk, wv, wo, wcq, vecs, q_o, k_o, v_o, mix_o, sum_o, first_o, low_o, cq_o, lse_o):
    rows = tokens[...]
    count, width = rows.shape
    q_o[...] = nn(rows, whole(wq)).astype(BF16)
    k_o[...] = nn(rows, whole(wk)).astype(BF16)
    v_o[...] = nn(rows, whole(wv)).astype(BF16)
    live = length[0]
    at_q = lax.rem(lax.broadcasted_iota(jnp.int32, (2 * count, count), 0), count)
    at_k = lax.broadcasted_iota(jnp.int32, (2 * count, count), 1)
    allowed = (at_k <= at_q) & (at_k < live)
    column = lanes(count)
    totals = jnp.zeros((count, 128), F32)
    for pair in range(width // 128):
        cut = slice(pair * 128, pair * 128 + 128)
        mixed, log_total = pair_forward(
            stack_pair(q_o[:, cut]), k_o[:, cut], v_o[:, cut],
            lambda scores: jnp.where(allowed, scores, -1e30),
        )
        mix_o[:, cut] = unstack_pair(mixed).astype(BF16)
        totals = jnp.where(column == 2 * pair, log_total[:count], totals)
        totals = jnp.where(column == 2 * pair + 1, log_total[count:], totals)
    lse_o[...] = totals.T
    summed = rows.astype(F32) + nn(mix_o[...], whole(wo))
    sum_o[...] = summed
    normal, _ = norm_parts(summed)
    first = normal * vecs[0:1] + vecs[1:2]
    first_o[...] = first
    low = first.astype(BF16)
    low_o[...] = low
    cq_o[...] = nn(low, whole(wcq)).astype(BF16)


def self_forward(length, tokens, stack, at, vecs):
    count, width = tokens.shape
    low = shape(tokens.shape, BF16)
    wide = shape(tokens.shape, F32)
    spec = full(tokens.shape)
    return call(
        self_body, "self_forward",
        [low, low, low, low, wide, wide, low, low, shape((128, count), F32)], (1,),
        [spec] + [weight(k) for k in at] + [full(vecs.shape)],
        [spec] * 8 + [full((128, count))], prefetch=1,
        flops=10 * count * width * width, moved=16 * MIB,
    )(length, tokens, stack, stack, stack, stack, stack, vecs)


def cross_body(length, q, k, v, mix_o, lse_o):
    count = q.shape[0]
    slots = k.shape[0]
    live = length[0]
    q2 = stack_pair(q[...])
    keys = k[...]
    values = v[...]
    half = slots // 2
    tile = 128
    column = lax.broadcasted_iota(jnp.int32, (tile, slots - half), 1) + half

    def mask(scores):
        upper = jnp.where(column < live, scores[:, half:], -1e30)
        return jnp.concatenate([scores[:, :half], upper], axis=1)

    mixes, logs = [], []
    for at in range(0, 2 * count, tile):
        mixed, log_total = pair_forward(q2[at : at + tile], keys, values, mask)
        mixes.append(mixed)
        logs.append(log_total)
    mix_o[...] = unstack_pair(jnp.concatenate(mixes, axis=0)).astype(BF16)
    logs = jnp.concatenate(logs, axis=0)
    column = lanes(count)
    totals = jnp.where(column == 0, logs[:count], jnp.where(column == 1, logs[count:], 0.0))
    lse_o[0] = totals.T[:8]


def cross_forward(length, q, k, v):
    count, width = q.shape
    slots = k.shape[0]
    pairs = width // 128
    return call(
        cross_body, "cross_forward",
        [shape(q.shape, BF16), shape((pairs, 8, count), F32)], (pairs,),
        [pl.BlockSpec((count, 128), lambda i, _: (0, i))]
        + [pl.BlockSpec((slots, 128), lambda i, _: (0, i))] * 2,
        [pl.BlockSpec((count, 128), lambda i, _: (0, i)), pl.BlockSpec((1, 8, count), lambda i, _: (i, 0, 0))],
        prefetch=1, flops=16 * count * slots * width, moved=10 * MIB,
    )(length, q, k, v)


def second_body(mixture, wo, first, vecs, sum_o, second_o, low_o):
    summed = first[...] + nn(mixture[...], whole(wo))
    sum_o[...] = summed
    normal, _ = norm_parts(summed)
    second = normal * vecs[2:3] + vecs[3:4]
    second_o[...] = second
    low_o[...] = second.astype(BF16)


def second_norm(mixture, stack, at, first, vecs):
    spec = full(mixture.shape)
    return call(
        second_body, "second_norm",
        [shape(mixture.shape, F32), shape(mixture.shape, F32), shape(mixture.shape, BF16)], (1,),
        [spec, weight(at), spec, full(vecs.shape)], [spec] * 3,
        flops=MIB * 512, moved=6 * MIB,
    )(mixture, stack, first, vecs)


def erf(x):
    return lax.erf(x)


def ffn_body(low, second, inner, outer, cot, vecs, act_o, slope_o, out_o, gts_o, go_o, grads_o, total):
    step = pl.program_id(0)
    pre = nn(low[...], whole(inner))
    half = 0.5 * (1.0 + erf(pre * math.sqrt(0.5)))
    active = (pre * half).astype(BF16)
    act_o[...] = active
    slope_o[...] = half + pre * (jnp.exp(-0.5 * pre * pre) * (1.0 / math.sqrt(2.0 * math.pi)))
    part = nn(active, whole(outer))

    @pl.when(step == 0)
    def _():
        total[...] = second[...] + part

    @pl.when(step > 0)
    def _():
        total[...] += part

    @pl.when(step == pl.num_programs(0) - 1)
    def _():
        summed = total[...]
        normal, _ = norm_parts(summed)
        out_o[...] = (normal * vecs[4:5] + vecs[5:6]).astype(BF16)
        grad, gain, shift = norm_back(summed, vecs[4:5], cot[...].astype(F32))
        gts_o[...] = grad
        go_o[...] = grad.astype(BF16)
        grads_o[...] = jnp.concatenate([gain, shift] + [jnp.zeros_like(gain)] * 6, axis=0)


def ffn_forward(low, second, stack, cot, vecs):
    count, width = low.shape
    spec = full(low.shape)
    wide = pl.BlockSpec((count, 1024), lambda i: (0, i))
    return call(
        ffn_body, "ffn_forward",
        [shape((count, 4096), BF16), shape((count, 4096), F32), shape(low.shape, BF16), shape(low.shape, F32), shape(low.shape, BF16), shape((8, width), F32)],
        (4,),
        [spec, spec, pl.BlockSpec((BLOCKS, 32, 1024), lambda i: (0, 4 + i, 0)), pl.BlockSpec((8, 128, 1024), lambda i: (i, 0, 0)), spec, full(vecs.shape)],
        [wide, wide, spec, spec, spec, full((8, width))],
        scratch=[pltpu.VMEM(low.shape, F32)],
        flops=16 * count * width * width, moved=24 * MIB,
    )(low, second, stack, stack, cot, vecs)


def ffn_back_body(go, gts, slope, inner, outer, summed, wo, vecs, gi_o, gss_o, gci_o, gcm_o, grads_o, total):
    step = pl.program_id(0)
    grad = nt(go[...], whole(outer))
    low = (grad * slope[...]).astype(BF16)
    gi_o[...] = low
    part = nt(low, whole(inner))

    @pl.when(step == 0)
    def _():
        total[...] = gts[...] + part

    @pl.when(step > 0)
    def _():
        total[...] += part

    @pl.when(step == pl.num_programs(0) - 1)
    def _():
        grad, gain, shift = norm_back(summed[...], vecs[2:3], total[...])
        gss_o[...] = grad
        low = grad.astype(BF16)
        gci_o[...] = low
        gcm_o[...] = nt(low, whole(wo)).astype(BF16)
        grads_o[...] = jnp.concatenate([gain, shift] + [jnp.zeros_like(gain)] * 6, axis=0)


def ffn_backward(go, gts, slope, stack, summed, squares, at, vecs):
    count, width = go.shape
    spec = full(go.shape)
    wide = pl.BlockSpec((count, 1024), lambda i: (0, i))
    low = shape(go.shape, BF16)
    return call(
        ffn_back_body, "ffn_backward",
        [shape((count, 4096), BF16), shape(go.shape, F32), low, low, shape((8, width), F32)],
        (4,),
        [spec, spec, wide, pl.BlockSpec((BLOCKS, 32, 1024), lambda i: (0, 4 + i, 0)), pl.BlockSpec((8, 128, 1024), lambda i: (i, 0, 0)), spec, weight(at), full(vecs.shape)],
        [wide, spec, spec, spec, full((8, width))],
        scratch=[pltpu.VMEM(go.shape, F32)],
        flops=18 * count * width * width, moved=26 * MIB,
    )(go, gts, slope, stack, stack, summed, squares, vecs)


def cross_back_body(length, q, k, v, g, mixture, lse, dq_o, dk_o, dv_o):
    live = length[0]
    slots = k.shape[0]
    count = q.shape[0]
    q2 = stack_pair(q[...])
    g2 = stack_pair(g[...])
    totals = jnp.concatenate([lse[0, 0:1], lse[0, 1:2]], axis=1) * LOG2E
    inner = pair_inner(mixture[...], g[...])
    tile = 256
    grad_q = jnp.zeros((128, 2 * count), F32)
    for at in range(0, slots, tile):
        mask = None
        if at + tile > slots // 2:
            row = lax.broadcasted_iota(jnp.int32, (tile, 2 * count), 0) + at

            def mask(probs, row=row):
                return jnp.where(row < live, probs, 0.0)

        cut = slice(at, at + tile)
        dq, dk, dv = pair_tile_back(q2, g2, k[cut], v[cut], totals, inner, mask)
        grad_q = grad_q + dq
        dk_o[cut] = dk.astype(BF16)
        dv_o[cut] = dv.astype(BF16)
    dq_o[...] = join_grad_queries(grad_q)


def cross_backward(length, q, k, v, g, mixture, lse):
    count, width = q.shape
    slots = k.shape[0]
    pairs = width // 128
    small = pl.BlockSpec((count, 128), lambda i, _: (0, i))
    large = pl.BlockSpec((slots, 128), lambda i, _: (0, i))
    return call(
        cross_back_body, "cross_backward",
        [shape(q.shape, BF16), shape(k.shape, BF16), shape(k.shape, BF16)], (pairs,),
        [small, large, large, small, small, pl.BlockSpec((1, 8, count), lambda i, _: (i, 0, 0))],
        [small, large, large], prefetch=1,
        flops=40 * count * slots * width, moved=18 * MIB,
    )(length, q, k, v, g, mixture, lse)


def memory_grad_body(dk, dv, wk, wv, out):
    out[...] = nt(dk[...], whole(wk)) + nt(dv[...], whole(wv))


def memory_gradient(dk, dv, stack, at_k, at_v):
    count, width = dk.shape
    tile = 512
    spec = pl.BlockSpec((tile, width), lambda i: (i, 0))
    return call(
        memory_grad_body, "memory_grad", shape(dk.shape, F32), (count // tile,),
        [spec, spec, weight(at_k), weight(at_v)], spec,
        flops=4 * count * width * width, moved=20 * MIB,
    )(dk, dv, stack, stack)


def self_back_body(length, gss, dcq, wcq, summed, wo, vecs, q, k, v, mixture, lse, gfs_o, gsi_o, gq_o, gk_o, gv_o, grads_o):
    live = length[0]
    count, width = gss.shape
    upstream = gss[...] + nt(dcq[...], whole(wcq))
    grad, gain, shift = norm_back(summed[...], vecs[0:1], upstream)
    gfs_o[...] = grad
    grads_o[...] = jnp.concatenate([gain, shift] + [jnp.zeros_like(gain)] * 6, axis=0)
    low = grad.astype(BF16)
    gsi_o[...] = low
    mix_grad = nt(low, whole(wo)).astype(BF16)
    at_k = lax.broadcasted_iota(jnp.int32, (count, 2 * count), 0)
    at_q = lax.rem(lax.broadcasted_iota(jnp.int32, (count, 2 * count), 1), count)
    allowed = (at_k <= at_q) & (at_k < live)
    for pair in range(width // 128):
        cut = slice(pair * 128, pair * 128 + 128)
        g = mix_grad[:, cut]
        totals = jnp.concatenate([lse[2 * pair : 2 * pair + 1], lse[2 * pair + 1 : 2 * pair + 2]], axis=1) * LOG2E
        scores_back = pair_tile_back(
            stack_pair(q[:, cut]), stack_pair(g), k[:, cut], v[:, cut], totals,
            pair_inner(mixture[:, cut], g),
            lambda probs: jnp.where(allowed, probs, 0.0),
        )
        dq, dk, dv = scores_back
        gq_o[:, cut] = join_grad_queries(dq)
        gk_o[:, cut] = dk.astype(BF16)
        gv_o[:, cut] = dv.astype(BF16)


def self_backward(length, gss, dcq, stack, at_cq, at_o, summed, vecs, q, k, v, mixture, lse):
    count, width = q.shape
    spec = full(q.shape)
    low = shape(q.shape, BF16)
    return call(
        self_back_body, "self_backward",
        [shape(q.shape, F32), low, low, low, low, shape((8, width), F32)], (1,),
        [spec, spec, weight(at_cq), spec, weight(at_o), full(vecs.shape), spec, spec, spec, spec, full(lse.shape)],
        [spec] * 5 + [full((8, width))], prefetch=1,
        flops=8 * count * width * width, moved=12 * MIB,
    )(length, gss, dcq, stack, summed, stack, vecs, q, k, v, mixture, lse)


def tokens_grad_body(gfs, gq, gk, gv, wq, wk, wv, out):
    out[...] = gfs[...] + nt(gq[...], whole(wq)) + nt(gk[...], whole(wk)) + nt(gv[...], whole(wv))


def tokens_gradient(gfs, gq, gk, gv, stack, at):
    spec = full(gfs.shape)
    return call(
        tokens_grad_body, "tokens_grad", shape(gfs.shape, F32), (1,),
        [spec] * 4 + [weight(k) for k in at], spec,
        flops=6 * MIB * 256, moved=10 * MIB,
    )(gfs, gq, gk, gv, stack, stack, stack)


def place(keep, send, at, size, pieces, me):
    low = lax.rem(me, 8)
    for j in range(8):
        rows = pieces(lax.bitwise_xor(low, j))
        target = send if j % 2 else keep
        target[j // 2, at : at + size, :] = rows.astype(BF16)


def outer_body(me, act, go, keep, send, held):
    held[...] = tn(act[...], go[...])
    place(keep, send, 0, 128, lambda d: held[pl.ds(pl.multiple_of(d * 128, 128), 128), :], me[0])


def inner_body(me, low, gi, keep, send, held):
    for part in range(4):
        held[...] = tn(low[...], gi[:, part * 1024 : part * 1024 + 1024])
        place(keep, send, part * 32, 32, lambda d: held[pl.ds(pl.multiple_of(d * 32, 32), 32), :], me[0])


def group_of(step, me):
    return lax.bitwise_xor(step, lax.div(me[0], 8))


def payload(rows, width):
    out = [shape((16, rows, width), BF16)] * 2
    spec = [pl.BlockSpec((4, rows, width), lambda i, _: (i, 0, 0))] * 2
    return out, spec


def outer_weights(me, act, go):
    count, width = go.shape
    out, spec = payload(128, width)
    return call(
        outer_body, "outer_weights", out, (4,),
        [pl.BlockSpec((count, 1024), lambda i, me: (0, group_of(i, me))), full(go.shape)],
        spec, [pltpu.VMEM((1024, width), F32)], 1,
        flops=8 * count * width * width, moved=11 * MIB,
    )(me, act, go)


def inner_weights(me, low, gi):
    count, width = low.shape
    out, spec = payload(128, width)
    return call(
        inner_body, "inner_weights", out, (4,),
        [pl.BlockSpec((count, 256), lambda i, me: (0, group_of(i, me))), full(gi.shape)],
        spec, [pltpu.VMEM((256, width), F32)], 1,
        flops=8 * count * width * width, moved=11 * MIB,
    )(me, low, gi)


def square_body(me, *refs):
    count = (len(refs) - 3) // 2
    keep, send, held = refs[-3:]
    for at in range(count):
        held[...] = tn(refs[2 * at][...], refs[2 * at + 1][...])
        place(keep, send, at * 32, 32, lambda d: held[pl.ds(pl.multiple_of(d * 32, 32), 32), :], me[0])


def square_vec_body(me, *refs):
    vecs = refs[-4]
    square_body(me, *refs[:-4], *refs[-3:])
    keep, send = refs[-3:-1]
    rows = vecs[...]
    step = group_of(pl.program_id(0), me)
    width = rows.shape[1]

    def pieces(d):
        return pltpu.roll(rows, lax.rem(width - (step * 8 + d) * 32, width), 1)

    place(keep, send, 128, 16, pieces, me[0])


def square_weights(me, pairs, name, vecs=None):
    width = pairs[0][0].shape[1]
    out, spec = payload(128 if vecs is None else 144, width)
    ins, operands, flops = [], [], 0
    for rows, grads in pairs:
        ins.append(pl.BlockSpec((rows.shape[0], 256), lambda i, me: (0, group_of(i, me))))
        ins.append(full(grads.shape))
        operands += [rows, grads]
        flops += 2 * rows.shape[0] * width * width
    if vecs is not None:
        ins.append(full(vecs.shape))
        operands.append(vecs)
    return call(
        square_body if vecs is None else square_vec_body, name, out, (4,), ins, spec,
        [pltpu.VMEM((256, width), F32)], 1, flops=flops, moved=20 * MIB,
    )(me, *operands)


def swap(rows, distance):
    return lax.ppermute(rows, "dp", [(i, i ^ distance) for i in range(BLOCKS)])


def scatter_sum(keep, send):
    rows, width = keep.shape[1:]
    cut = (rows // 32) * 16
    came = swap(send, 1)
    dims = (2, 2, 2, 2, rows, width)
    keep, came = keep.reshape(dims), came.reshape(dims)

    def start(index, part):
        return keep[index][..., part, :].astype(F32) + came[index][..., part, :].astype(F32)

    a, b = slice(0, cut), slice(cut, rows)
    every = slice(None)
    a_came = swap(start((every, every, every, 1), a).astype(BF16), 2)
    b_came = swap(start((every, every, 1), b).astype(BF16), 4)

    def a_second(at):
        return start((every, every, at, 0), a) + a_came[:, :, at].astype(F32)

    def b_second(at):
        return start((every, every, 0, at), b) + b_came[:, :, at].astype(F32)

    a_more = swap(a_second(1).astype(BF16), 4)
    b_more = swap(b_second(1).astype(BF16), 2)

    def third(at):
        return jnp.concatenate(
            [a_second(0)[at] + a_more[at].astype(F32), b_second(0)[at] + b_more[at].astype(F32)], axis=-2
        )

    far = swap(third(1).astype(BF16), 16)

    def fourth(at):
        return third(0)[at] + far[at].astype(F32)

    near = swap(fourth(1).astype(BF16), 8)
    return fourth(0) + near.astype(F32)


def absolute(keep, send):
    return jnp.stack([keep, send], axis=1).reshape((BLOCKS,) + keep.shape[1:])


def pack_vectors(vectors, devices):
    own = vectors[0].shape[0]
    rows = jnp.stack(vectors)
    return jnp.pad(rows, ((0, 16 - len(vectors)), (0, 1024 - own)))


def gather(rows):
    return lax.all_gather(rows, "dp", axis=0, tiled=True)


def on_device(
    devices, tokens, memory, target_lengths, memory_lengths, cotangent,
    self_query, self_key, self_value, self_output, first_gain, first_shift,
    cross_query, cross_key, cross_value, cross_output, second_gain, second_shift,
    inner_weight, outer_weight, third_gain, third_shift,
):
    width = tokens.shape[1]
    hidden = inner_weight.shape[1]
    direct = devices == BLOCKS
    squares = [cross_key, cross_value, self_query, self_key, self_value, self_output, cross_query, cross_output]
    vectors = [first_gain, first_shift, second_gain, second_shift, third_gain, third_shift]
    if direct:
        me = lax.axis_index("dp").astype(jnp.int32).reshape(1)
        pack = jnp.concatenate(squares + [pack_vectors(vectors, devices)], axis=0)
        stack = gather(pack).reshape(BLOCKS, -1, width)
        vecs = stack[:, 256:264, :32].transpose(1, 0, 2).reshape(8, width).astype(F32)
        parts = [outer_weight] + [inner_weight[:, i : i + width] for i in range(0, hidden, width)]
        pack = jnp.concatenate(parts, axis=0)
        pack, _ = lax.optimization_barrier((pack, stack[0, :1]))
        wide = gather(pack).reshape(BLOCKS, -1, width)
    else:
        me = jnp.zeros((1,), jnp.int32)
        stack = jnp.concatenate([gather(w).reshape(BLOCKS, 32, width) for w in squares], axis=1)
        vecs = jnp.pad(jnp.stack([gather(v) for v in vectors]), ((0, 2), (0, 0))).astype(F32)
        inner_full = gather(inner_weight)
        parts = [gather(outer_weight).reshape(BLOCKS, 128, width)]
        parts += [inner_full[:, i : i + width].reshape(BLOCKS, 32, width) for i in range(0, hidden, width)]
        wide = jnp.concatenate(parts, axis=1)

    keys, values = kv_project(memory, stack, 0, 1)
    q, k, v, mixture, first_sum, first_out, first_low, cross_q, lse = self_forward(
        target_lengths, tokens, stack, (2, 3, 4, 5, 6), vecs
    )
    cross_mixture, cross_lse = cross_forward(memory_lengths, cross_q, keys, values)
    second_sum, second, second_low = second_norm(cross_mixture, stack, 7, first_out, vecs)
    act, slope, output_rows, gts, go, third_grads = ffn_forward(second_low, second, wide, cotangent, vecs)
    outer_pay = outer_weights(me, act, go)
    gi, gss, gci, gcm, second_grads = ffn_backward(go, gts, slope, wide, second_sum, stack, 7, vecs)
    inner_pay = inner_weights(me, second_low, gi)
    dq, dk, dv = cross_backward(memory_lengths, cross_q, keys, values, gcm, cross_mixture, cross_lse)
    cross_pay = square_weights(
        me, [(first_low, dq), (memory, dk), (memory, dv), (cross_mixture, gci)], "cross_weights"
    )
    gfs, gsi, gq, gk, gv, first_grads = self_backward(
        target_lengths, gss, dq, stack, 6, 5, first_sum, vecs, q, k, v, mixture, lse
    )
    grads = jnp.concatenate([first_grads[:2], second_grads[:2], third_grads[:2], jnp.zeros((10, width), F32)])
    self_pay = square_weights(me, [(tokens, gq), (tokens, gk), (tokens, gv), (mixture, gsi)], "self_weights", grads)
    memory_grad = memory_gradient(dk, dv, stack, 0, 1)
    tokens_grad = tokens_gradient(gfs, gq, gk, gv, stack, (2, 3, 4))

    if direct:
        outer_own = scatter_sum(*outer_pay)
        inner_own = scatter_sum(*inner_pay)
        cross_own = scatter_sum(*cross_pay)
        self_own = scatter_sum(*self_pay)
        inner_own = jnp.concatenate([inner_own[i : i + 32] for i in range(0, 128, 32)], axis=1)
        cross_own = [cross_own[i : i + 32] for i in range(0, 128, 32)]
        vec_own = [self_own[128 + i, :32] for i in range(6)]
        self_own = [self_own[i : i + 32] for i in range(0, 128, 32)]
    else:
        def owned(rows):
            return lax.psum_scatter(rows.astype(F32), "dp", scatter_dimension=0, tiled=True)

        outer_own = owned(absolute(*outer_pay).reshape(-1, width))
        inner_rows = absolute(*inner_pay)
        inner_rows = jnp.concatenate([inner_rows[:, i : i + 32].reshape(-1, width) for i in range(0, 128, 32)], axis=1)
        inner_own = owned(inner_rows)
        cross_rows, self_rows = absolute(*cross_pay), absolute(*self_pay)
        cross_own = [owned(cross_rows[:, i : i + 32].reshape(-1, width)) for i in range(0, 128, 32)]
        self_own = [owned(self_rows[:, i : i + 32].reshape(-1, width)) for i in range(0, 128, 32)]
        vec_own = [owned(grads[i]) for i in range(6)]

    return (
        output_rows, tokens_grad, memory_grad,
        *self_own, vec_own[0], vec_own[1],
        *cross_own, vec_own[2], vec_own[3],
        inner_own, outer_own, vec_own[4], vec_own[5],
    )


def solution(mesh):
    rows, line = P("dp", None), P("dp")
    block = [rows] * 4 + [line] * 2
    placed = (rows, rows, line, line, rows, *block, *block, rows, rows, line, line)
    return jax.shard_map(
        functools.partial(on_device, mesh.shape["dp"]),
        mesh=mesh,
        in_specs=placed,
        out_specs=(rows, rows, rows, *block, *block, rows, rows, line, line),
        check_vma=False,
    )
```

```python
import functools
import math

import jax
import jax.numpy as jnp
from jax import lax
from jax.experimental import pallas as pl
from jax.experimental.pallas import tpu as pltpu
from jax.sharding import PartitionSpec as P

HEAD = 64
EPS = 1e-05
SCALE = 1.0 / math.sqrt(HEAD)
LOG2E = 1.4426950408889634
BLOCKS = 32
MIB = 1024 * 1024
F32 = jnp.float32
BF16 = jnp.bfloat16


def nn(a, b):
    return jnp.dot(a, b, preferred_element_type=F32)


def nt(a, b):
    return lax.dot_general(a, b, (((1,), (1,)), ((), ())), preferred_element_type=F32)


def tn(a, b):
    return lax.dot_general(a, b, (((0,), (0,)), ((), ())), preferred_element_type=F32)


def whole(ref):
    return ref[...].reshape(-1, ref.shape[-1])


def call(body, name, out, grid=(), ins=None, outs=None, scratch=(), prefetch=0, limit=56, flops=0, moved=0):
    return pl.pallas_call(
        body,
        out_shape=out,
        grid_spec=pltpu.PrefetchScalarGridSpec(
            num_scalar_prefetch=prefetch,
            grid=grid,
            in_specs=ins,
            out_specs=outs,
            scratch_shapes=scratch,
        ),
        compiler_params=pltpu.CompilerParams(vmem_limit_bytes=limit * MIB),
        cost_estimate=pl.CostEstimate(flops=flops, bytes_accessed=moved, transcendentals=0),
        name=name,
    )


def full(shape):
    return pl.BlockSpec(shape, lambda *_: (0,) * len(shape))


def weight(at):
    return pl.BlockSpec((BLOCKS, 32, 1024), lambda *_: (0, at, 0))


def shape(dims, dtype):
    return jax.ShapeDtypeStruct(dims, dtype)


def norm_parts(summed):
    average = jnp.mean(summed, axis=-1, keepdims=True)
    centred = summed - average
    spread = jnp.mean(centred * centred, axis=-1, keepdims=True)
    scale = lax.rsqrt(spread + EPS)
    return centred * scale, scale


def norm_back(summed, gain, upstream):
    normal, scale = norm_parts(summed)
    grad_gain = jnp.sum(upstream * normal, axis=0, keepdims=True)
    grad_shift = jnp.sum(upstream, axis=0, keepdims=True)
    scaled = upstream * gain
    first = jnp.mean(scaled, axis=-1, keepdims=True)
    second = jnp.mean(scaled * normal, axis=-1, keepdims=True)
    return scale * (scaled - first - normal * second), grad_gain, grad_shift


def lanes(rows):
    return lax.broadcasted_iota(jnp.int32, (rows, 128), 1)


def stack_pair(rows):
    low = lanes(rows.shape[0]) < HEAD
    zero = jnp.zeros_like(rows)
    return jnp.concatenate([jnp.where(low, rows, zero), jnp.where(low, zero, rows)], axis=0)


def unstack_pair(stacked):
    half = stacked.shape[0] // 2
    return jnp.where(lanes(half) < HEAD, stacked[:half], stacked[half:])


def pair_forward(stacked, keys, values, mask):
    scores = nt(stacked, keys)
    if mask is not None:
        scores = mask(scores)
    peak = jnp.max(scores, axis=-1, keepdims=True)
    raised = jnp.exp2((scores - peak) * (SCALE * LOG2E))
    total = jnp.sum(raised, axis=-1, keepdims=True)
    mixed = nn(raised.astype(BF16), values) / total
    return mixed, peak * SCALE + jnp.log(total)


def pair_tile_back(q2, g2, keys, values, totals, inner, mask):
    scores = nt(keys, q2)
    probs = jnp.exp2(scores * (SCALE * LOG2E) - totals)
    if mask is not None:
        probs = mask(probs)
    grad_probs = nt(values, g2)
    grad_scores = (probs * (grad_probs - inner)).astype(BF16)
    grad_values = nn(probs.astype(BF16), g2)
    grad_keys = nn(grad_scores, q2) * SCALE
    grad_queries = tn(keys, grad_scores)
    return grad_queries, grad_keys, grad_values


def pair_inner(mixture, grad):
    product = mixture.astype(F32) * grad.astype(F32)
    half = jnp.where(
        (lax.broadcasted_iota(jnp.int32, (8, 128), 1) // HEAD)
        == lax.broadcasted_iota(jnp.int32, (8, 128), 0),
        1.0,
        0.0,
    ).astype(F32)
    sums = lax.dot_general(
        half, product, (((1,), (1,)), ((), ())),
        preferred_element_type=F32, precision=lax.Precision.HIGHEST,
    )
    return jnp.concatenate([sums[0:1], sums[1:2]], axis=1)


def join_grad_queries(grad):
    count = grad.shape[1] // 2
    joined = jnp.concatenate([grad[:HEAD, :count], grad[HEAD:, count:]], axis=0) * SCALE
    return joined.T.astype(BF16)


def kv_body(memory, wk, wv, keys, values):
    rows = memory[...]
    keys[...] = nn(rows, whole(wk)).astype(BF16)
    values[...] = nn(rows, whole(wv)).astype(BF16)


def kv_project(memory, stack, at_k, at_v):
    count, width = memory.shape
    tile = 512
    spec = pl.BlockSpec((tile, width), lambda i: (i, 0))
    return call(
        kv_body, "cross_kv", [shape(memory.shape, BF16)] * 2, (count // tile,),
        [spec, weight(at_k), weight(at_v)], [spec, spec],
        flops=4 * count * width * width, moved=12 * MIB + 4 * MIB,
    )(memory, stack, stack)


def self_body(length, tokens, wq, wk, wv, wo, wcq, vecs, q_o, k_o, v_o, mix_o, sum_o, first_o, low_o, cq_o, lse_o):
    rows = tokens[...]
    count, width = rows.shape
    q_o[...] = nn(rows, whole(wq)).astype(BF16)
    k_o[...] = nn(rows, whole(wk)).astype(BF16)
    v_o[...] = nn(rows, whole(wv)).astype(BF16)
    live = length[0]
    at_q = lax.rem(lax.broadcasted_iota(jnp.int32, (2 * count, count), 0), count)
    at_k = lax.broadcasted_iota(jnp.int32, (2 * count, count), 1)
    allowed = (at_k <= at_q) & (at_k < live)
    column = lanes(count)
    totals = jnp.zeros((count, 128), F32)
    for pair in range(width // 128):
        cut = slice(pair * 128, pair * 128 + 128)
        mixed, log_total = pair_forward(
            stack_pair(q_o[:, cut]), k_o[:, cut], v_o[:, cut],
            lambda scores: jnp.where(allowed, scores, -1e30),
        )
        mix_o[:, cut] = unstack_pair(mixed).astype(BF16)
        totals = jnp.where(column == 2 * pair, log_total[:count], totals)
        totals = jnp.where(column == 2 * pair + 1, log_total[count:], totals)
    lse_o[...] = totals.T
    summed = rows.astype(F32) + nn(mix_o[...], whole(wo))
    sum_o[...] = summed
    normal, _ = norm_parts(summed)
    first = normal * vecs[0:1] + vecs[1:2]
    first_o[...] = first
    low = first.astype(BF16)
    low_o[...] = low
    cq_o[...] = nn(low, whole(wcq)).astype(BF16)


def self_forward(length, tokens, stack, at, vecs):
    count, width = tokens.shape
    low = shape(tokens.shape, BF16)
    wide = shape(tokens.shape, F32)
    spec = full(tokens.shape)
    return call(
        self_body, "self_forward",
        [low, low, low, low, wide, wide, low, low, shape((128, count), F32)], (1,),
        [spec] + [weight(k) for k in at] + [full(vecs.shape)],
        [spec] * 8 + [full((128, count))], prefetch=1,
        flops=10 * count * width * width, moved=16 * MIB,
    )(length, tokens, stack, stack, stack, stack, stack, vecs)


def cross_body(length, q, k, v, mix_o, lse_o):
    count = q.shape[0]
    slots = k.shape[0]
    live = length[0]
    q2 = stack_pair(q[...])
    keys = k[...]
    values = v[...]
    half = slots // 2
    tile = 128
    column = lax.broadcasted_iota(jnp.int32, (tile, slots - half), 1) + half

    def mask(scores):
        upper = jnp.where(column < live, scores[:, half:], -1e30)
        return jnp.concatenate([scores[:, :half], upper], axis=1)

    mixes, logs = [], []
    for at in range(0, 2 * count, tile):
        mixed, log_total = pair_forward(q2[at : at + tile], keys, values, mask)
        mixes.append(mixed)
        logs.append(log_total)
    mix_o[...] = unstack_pair(jnp.concatenate(mixes, axis=0)).astype(BF16)
    logs = jnp.concatenate(logs, axis=0)
    column = lanes(count)
    totals = jnp.where(column == 0, logs[:count], jnp.where(column == 1, logs[count:], 0.0))
    lse_o[0] = totals.T[:8]


def cross_forward(length, q, k, v):
    count, width = q.shape
    slots = k.shape[0]
    pairs = width // 128
    return call(
        cross_body, "cross_forward",
        [shape(q.shape, BF16), shape((pairs, 8, count), F32)], (pairs,),
        [pl.BlockSpec((count, 128), lambda i, _: (0, i))]
        + [pl.BlockSpec((slots, 128), lambda i, _: (0, i))] * 2,
        [pl.BlockSpec((count, 128), lambda i, _: (0, i)), pl.BlockSpec((1, 8, count), lambda i, _: (i, 0, 0))],
        prefetch=1, flops=16 * count * slots * width, moved=10 * MIB,
    )(length, q, k, v)


def second_body(mixture, wo, first, vecs, sum_o, second_o, low_o):
    summed = first[...] + nn(mixture[...], whole(wo))
    sum_o[...] = summed
    normal, _ = norm_parts(summed)
    second = normal * vecs[2:3] + vecs[3:4]
    second_o[...] = second
    low_o[...] = second.astype(BF16)


def second_norm(mixture, stack, at, first, vecs):
    spec = full(mixture.shape)
    return call(
        second_body, "second_norm",
        [shape(mixture.shape, F32), shape(mixture.shape, F32), shape(mixture.shape, BF16)], (1,),
        [spec, weight(at), spec, full(vecs.shape)], [spec] * 3,
        flops=MIB * 512, moved=6 * MIB,
    )(mixture, stack, first, vecs)


def erf(x):
    return lax.erf(x)


def ffn_body(low, second, inner, outer, cot, vecs, act_o, slope_o, out_o, gts_o, go_o, grads_o, total):
    step = pl.program_id(0)
    pre = nn(low[...], whole(inner))
    half = 0.5 * (1.0 + erf(pre * math.sqrt(0.5)))
    active = (pre * half).astype(BF16)
    act_o[...] = active
    slope_o[...] = half + pre * (jnp.exp(-0.5 * pre * pre) * (1.0 / math.sqrt(2.0 * math.pi)))
    part = nn(active, whole(outer))

    @pl.when(step == 0)
    def _():
        total[...] = second[...] + part

    @pl.when(step > 0)
    def _():
        total[...] += part

    @pl.when(step == pl.num_programs(0) - 1)
    def _():
        summed = total[...]
        normal, _ = norm_parts(summed)
        out_o[...] = (normal * vecs[4:5] + vecs[5:6]).astype(BF16)
        grad, gain, shift = norm_back(summed, vecs[4:5], cot[...].astype(F32))
        gts_o[...] = grad
        go_o[...] = grad.astype(BF16)
        grads_o[...] = jnp.concatenate([gain, shift] + [jnp.zeros_like(gain)] * 6, axis=0)


def ffn_forward(low, second, stack, cot, vecs):
    count, width = low.shape
    spec = full(low.shape)
    wide = pl.BlockSpec((count, 1024), lambda i: (0, i))
    return call(
        ffn_body, "ffn_forward",
        [shape((count, 4096), BF16), shape((count, 4096), F32), shape(low.shape, BF16), shape(low.shape, F32), shape(low.shape, BF16), shape((8, width), F32)],
        (4,),
        [spec, spec, pl.BlockSpec((BLOCKS, 32, 1024), lambda i: (0, 4 + i, 0)), pl.BlockSpec((8, 128, 1024), lambda i: (i, 0, 0)), spec, full(vecs.shape)],
        [wide, wide, spec, spec, spec, full((8, width))],
        scratch=[pltpu.VMEM(low.shape, F32)],
        flops=16 * count * width * width, moved=24 * MIB,
    )(low, second, stack, stack, cot, vecs)


def ffn_back_body(go, gts, slope, inner, outer, summed, wo, vecs, gi_o, gss_o, gci_o, gcm_o, grads_o, total):
    step = pl.program_id(0)
    grad = nt(go[...], whole(outer))
    low = (grad * slope[...]).astype(BF16)
    gi_o[...] = low
    part = nt(low, whole(inner))

    @pl.when(step == 0)
    def _():
        total[...] = gts[...] + part

    @pl.when(step > 0)
    def _():
        total[...] += part

    @pl.when(step == pl.num_programs(0) - 1)
    def _():
        grad, gain, shift = norm_back(summed[...], vecs[2:3], total[...])
        gss_o[...] = grad
        low = grad.astype(BF16)
        gci_o[...] = low
        gcm_o[...] = nt(low, whole(wo)).astype(BF16)
        grads_o[...] = jnp.concatenate([gain, shift] + [jnp.zeros_like(gain)] * 6, axis=0)


def ffn_backward(go, gts, slope, stack, summed, squares, at, vecs):
    count, width = go.shape
    spec = full(go.shape)
    wide = pl.BlockSpec((count, 1024), lambda i: (0, i))
    low = shape(go.shape, BF16)
    return call(
        ffn_back_body, "ffn_backward",
        [shape((count, 4096), BF16), shape(go.shape, F32), low, low, shape((8, width), F32)],
        (4,),
        [spec, spec, wide, pl.BlockSpec((BLOCKS, 32, 1024), lambda i: (0, 4 + i, 0)), pl.BlockSpec((8, 128, 1024), lambda i: (i, 0, 0)), spec, weight(at), full(vecs.shape)],
        [wide, spec, spec, spec, full((8, width))],
        scratch=[pltpu.VMEM(go.shape, F32)],
        flops=18 * count * width * width, moved=26 * MIB,
    )(go, gts, slope, stack, stack, summed, squares, vecs)


def cross_back_body(length, q, k, v, g, mixture, lse, dq_o, dk_o, dv_o):
    live = length[0]
    slots = k.shape[0]
    count = q.shape[0]
    q2 = stack_pair(q[...])
    g2 = stack_pair(g[...])
    totals = jnp.concatenate([lse[0, 0:1], lse[0, 1:2]], axis=1) * LOG2E
    inner = pair_inner(mixture[...], g[...])
    tile = 256
    grad_q = jnp.zeros((128, 2 * count), F32)
    for at in range(0, slots, tile):
        mask = None
        if at + tile > slots // 2:
            row = lax.broadcasted_iota(jnp.int32, (tile, 2 * count), 0) + at

            def mask(probs, row=row):
                return jnp.where(row < live, probs, 0.0)

        cut = slice(at, at + tile)
        dq, dk, dv = pair_tile_back(q2, g2, k[cut], v[cut], totals, inner, mask)
        grad_q = grad_q + dq
        dk_o[cut] = dk.astype(BF16)
        dv_o[cut] = dv.astype(BF16)
    dq_o[...] = join_grad_queries(grad_q)


def cross_backward(length, q, k, v, g, mixture, lse):
    count, width = q.shape
    slots = k.shape[0]
    pairs = width // 128
    small = pl.BlockSpec((count, 128), lambda i, _: (0, i))
    large = pl.BlockSpec((slots, 128), lambda i, _: (0, i))
    return call(
        cross_back_body, "cross_backward",
        [shape(q.shape, BF16), shape(k.shape, BF16), shape(k.shape, BF16)], (pairs,),
        [small, large, large, small, small, pl.BlockSpec((1, 8, count), lambda i, _: (i, 0, 0))],
        [small, large, large], prefetch=1,
        flops=40 * count * slots * width, moved=18 * MIB,
    )(length, q, k, v, g, mixture, lse)


def memory_grad_body(dk, dv, wk, wv, out):
    out[...] = nt(dk[...], whole(wk)) + nt(dv[...], whole(wv))


def memory_gradient(dk, dv, stack, at_k, at_v):
    count, width = dk.shape
    tile = 512
    spec = pl.BlockSpec((tile, width), lambda i: (i, 0))
    return call(
        memory_grad_body, "memory_grad", shape(dk.shape, F32), (count // tile,),
        [spec, spec, weight(at_k), weight(at_v)], spec,
        flops=4 * count * width * width, moved=20 * MIB,
    )(dk, dv, stack, stack)


def self_back_body(length, gss, dcq, wcq, summed, wo, vecs, q, k, v, mixture, lse, gfs_o, gsi_o, gq_o, gk_o, gv_o, grads_o):
    live = length[0]
    count, width = gss.shape
    upstream = gss[...] + nt(dcq[...], whole(wcq))
    grad, gain, shift = norm_back(summed[...], vecs[0:1], upstream)
    gfs_o[...] = grad
    grads_o[...] = jnp.concatenate([gain, shift] + [jnp.zeros_like(gain)] * 6, axis=0)
    low = grad.astype(BF16)
    gsi_o[...] = low
    mix_grad = nt(low, whole(wo)).astype(BF16)
    at_k = lax.broadcasted_iota(jnp.int32, (count, 2 * count), 0)
    at_q = lax.rem(lax.broadcasted_iota(jnp.int32, (count, 2 * count), 1), count)
    allowed = (at_k <= at_q) & (at_k < live)
    for pair in range(width // 128):
        cut = slice(pair * 128, pair * 128 + 128)
        g = mix_grad[:, cut]
        totals = jnp.concatenate([lse[2 * pair : 2 * pair + 1], lse[2 * pair + 1 : 2 * pair + 2]], axis=1) * LOG2E
        scores_back = pair_tile_back(
            stack_pair(q[:, cut]), stack_pair(g), k[:, cut], v[:, cut], totals,
            pair_inner(mixture[:, cut], g),
            lambda probs: jnp.where(allowed, probs, 0.0),
        )
        dq, dk, dv = scores_back
        gq_o[:, cut] = join_grad_queries(dq)
        gk_o[:, cut] = dk.astype(BF16)
        gv_o[:, cut] = dv.astype(BF16)


def self_backward(length, gss, dcq, stack, at_cq, at_o, summed, vecs, q, k, v, mixture, lse):
    count, width = q.shape
    spec = full(q.shape)
    low = shape(q.shape, BF16)
    return call(
        self_back_body, "self_backward",
        [shape(q.shape, F32), low, low, low, low, shape((8, width), F32)], (1,),
        [spec, spec, weight(at_cq), spec, weight(at_o), full(vecs.shape), spec, spec, spec, spec, full(lse.shape)],
        [spec] * 5 + [full((8, width))], prefetch=1,
        flops=8 * count * width * width, moved=12 * MIB,
    )(length, gss, dcq, stack, summed, stack, vecs, q, k, v, mixture, lse)


def tokens_grad_body(gfs, gq, gk, gv, wq, wk, wv, out):
    out[...] = gfs[...] + nt(gq[...], whole(wq)) + nt(gk[...], whole(wk)) + nt(gv[...], whole(wv))


def tokens_gradient(gfs, gq, gk, gv, stack, at):
    spec = full(gfs.shape)
    return call(
        tokens_grad_body, "tokens_grad", shape(gfs.shape, F32), (1,),
        [spec] * 4 + [weight(k) for k in at], spec,
        flops=6 * MIB * 256, moved=10 * MIB,
    )(gfs, gq, gk, gv, stack, stack, stack)


def place(keep, send, at, size, pieces, me):
    low = lax.rem(me, 8)
    for j in range(8):
        rows = pieces(lax.bitwise_xor(low, j))
        target = send if j % 2 else keep
        target[j // 2, at : at + size, :] = rows.astype(BF16)


def group_of(step, me):
    return lax.bitwise_xor(step, lax.div(me[0], 8))


def payload(rows, width):
    out = [shape((16, rows, width), BF16)] * 2
    spec = [pl.BlockSpec((4, rows, width), lambda i, _: (i, 0, 0))] * 2
    return out, spec


def ffn_weights_body(act, go, low, gi, out):
    step = pl.program_id(0)
    width = go.shape[1]

    @pl.when(step < 4)
    def _():
        out[...] = tn(act[...], go[...]).astype(BF16).reshape(8, 128, width)

    @pl.when(step >= 4)
    def _():
        for part in range(4):
            rows = tn(low[...], gi[:, part * 1024 : part * 1024 + 1024]).astype(BF16)
            out[:, part * 32 : part * 32 + 32, :] = rows.reshape(8, 32, width)


def ffn_weights(act, go, low, gi):
    count, width = go.shape
    return call(
        ffn_weights_body, "ffn_weights", shape((BLOCKS, 256, width), BF16), (8,),
        [
            pl.BlockSpec((count, 1024), lambda i: (0, jnp.minimum(i, 3))),
            full(go.shape),
            pl.BlockSpec((count, 256), lambda i: (0, jnp.maximum(i - 4, 0))),
            full(gi.shape),
        ],
        pl.BlockSpec((8, 128, width), lambda i: (lax.rem(i, 4), lax.div(i, 4), 0)),
        flops=16 * count * width * width, moved=22 * MIB,
    )(act, go, low, gi)


def square_body(me, *refs):
    count = (len(refs) - 3) // 2
    keep, send, held = refs[-3:]
    for at in range(count):
        held[...] = tn(refs[2 * at][...], refs[2 * at + 1][...])
        place(keep, send, at * 32, 32, lambda d: held[pl.ds(pl.multiple_of(d * 32, 32), 32), :], me[0])


def square_vec_body(me, *refs):
    vecs = refs[-4]
    square_body(me, *refs[:-4], *refs[-3:])
    keep, send = refs[-3:-1]
    rows = vecs[...]
    step = group_of(pl.program_id(0), me)
    width = rows.shape[1]

    def pieces(d):
        return pltpu.roll(rows, lax.rem(width - (step * 8 + d) * 32, width), 1)

    place(keep, send, 128, 32, pieces, me[0])


def square_weights(me, pairs, name, vecs=None):
    width = pairs[0][0].shape[1]
    out, spec = payload(128 if vecs is None else 160, width)
    ins, operands, flops = [], [], 0
    for rows, grads in pairs:
        ins.append(pl.BlockSpec((rows.shape[0], 256), lambda i, me: (0, group_of(i, me))))
        ins.append(full(grads.shape))
        operands += [rows, grads]
        flops += 2 * rows.shape[0] * width * width
    if vecs is not None:
        ins.append(full(vecs.shape))
        operands.append(vecs)
    return call(
        square_body if vecs is None else square_vec_body, name, out, (4,), ins, spec,
        [pltpu.VMEM((256, width), F32)], 1, flops=flops, moved=20 * MIB,
    )(me, *operands)


def flip(me, bit):
    return me + bit - 2 * bit * lax.rem(lax.div(me, bit), 2)

def send(src, dst, out_sem, in_sem, to):
    return pltpu.make_async_remote_copy(src_ref=src, dst_ref=dst, send_sem=out_sem, recv_sem=in_sem, device_id=(to,), device_id_type=pl.DeviceIdType.MESH)

def greet(me, bits):
    barrier = pltpu.get_barrier_semaphore()
    for bit in bits:
        pl.semaphore_signal(barrier, inc=1, device_id=(flip(me, bit),), device_id_type=pl.DeviceIdType.MESH)
    pl.semaphore_wait(barrier, len(bits))

PAIR=32; HALF=16
CORE,XB,YB,NEAR,FAR=1,2,4,8,16

def gather_body(own, g, local_sem, out_sem, in_sem):
    me = lax.axis_index("dp").astype(jnp.int32)
    c, x, y, zl, zh = [lax.rem(lax.div(me, b), 2) for b in (1, 2, 4, 8, 16)]
    ticks = own.shape[0] // PAIR
    every = slice(None)
    greet(me, (CORE, XB, YB, NEAR, FAR))

    def rows(p): return pl.ds(pl.multiple_of(p * PAIR, PAIR), PAIR)
    def half(p, k): return pl.ds(pl.multiple_of(p * PAIR + k * HALF, HALF), HALF)
    def local(p): return pltpu.make_async_copy(own.at[rows(p)], g.at[zh, zl, y, x, c, rows(p)], local_sem.at[p])
    def same(ref, k, p, bit):
        return send(ref, ref, out_sem.at[k, p], in_sem.at[k, p], flip(me, bit))
    def near(p):
        return send(own.at[rows(p)], g.at[zh, zl, y, x, c, rows(p)], out_sem.at[0, p], in_sem.at[0, p], flip(me, NEAR))
    def far(p): return same(g.at[zh, every, y, x, c, rows(p)], 1, p, FAR)
    def a1(p): return same(g.at[every, every, y, x, c, half(p, 0)], 2, p, XB)
    def b1(p): return same(g.at[every, every, y, x, c, half(p, 1)], 3, p, YB)
    def a2(p): return same(g.at[every, every, y, every, c, half(p, 0)], 4, p, YB)
    def b2(p): return same(g.at[every, every, every, x, c, half(p, 1)], 5, p, XB)
    def core(p): return same(g.at[every, every, every, every, c, rows(p)], 6, p, CORE)

    def tick(t, _):
        @pl.when(t < ticks)
        def _():
            local(t).start()
            near(t).start()
        @pl.when((t >= 1) & (t < ticks + 1))
        def _():
            p = t - 1
            local(p).wait()
            near(p).wait_recv()
            far(p).start()
        @pl.when((t >= 2) & (t < ticks + 2))
        def _():
            p = t - 2
            far(p).wait_recv()
            a1(p).start()
            b1(p).start()
        @pl.when((t >= 3) & (t < ticks + 3))
        def _():
            p = t - 3
            a1(p).wait_recv()
            a2(p).start()
            b1(p).wait_recv()
            b2(p).start()
        @pl.when((t >= 4) & (t < ticks + 4))
        def _():
            p = t - 4
            a2(p).wait_recv()
            b2(p).wait_recv()
            core(p).start()
        return 0
    lax.fori_loop(0, ticks + 4, tick, 0)
    def close(p, _):
        core(p).wait_recv()
        for copy in (near, far, a1, b1, a2, b2, core):
            copy(p).wait_send()
        return 0
    lax.fori_loop(0, ticks, close, 0)

def gather_rows(own):
    ticks = own.shape[0] // PAIR
    out = pl.pallas_call(
        gather_body,
        out_shape=jax.ShapeDtypeStruct((2,2,2,2,2)+own.shape, own.dtype),
        in_specs=[pl.BlockSpec(memory_space=pl.ANY)],
        out_specs=pl.BlockSpec(memory_space=pl.ANY),
        scratch_shapes=[pltpu.SemaphoreType.DMA((ticks,)), pltpu.SemaphoreType.DMA((7, ticks)), pltpu.SemaphoreType.DMA((7, ticks))],
        compiler_params=pltpu.CompilerParams(collective_id=0, has_side_effects=True, vmem_limit_bytes=40*MIB),
        name="gather_rows",
    )(own)
    return out.reshape((BLOCKS,)+own.shape)

def scatter_body(count, *refs):
    pays = [(refs[2*i], refs[2*i+1]) for i in range(count)]
    out, keep, came0, put1, came1, put2, came2, put3, came3, put4, came4, load_sem, out_sem, in_sem = refs[2*count:]
    me = lax.axis_index("dp").astype(jnp.int32)
    ticks = keep.shape[0]
    greet(me, (CORE, XB, YB, NEAR, FAR))
    first = []
    p = 0
    for kept, sent in pays:
        for at in range(0, kept.shape[1], PAIR):
            load = pltpu.make_async_copy(kept.at[:, pl.ds(at, PAIR)], keep.at[p], load_sem.at[p])
            load.start()
            put = send(sent.at[:, pl.ds(at, PAIR)], came0.at[p], out_sem.at[0, p], in_sem.at[0, p], flip(me, CORE))
            put.start()
            first.append(put)
            p += 1
    def loaded(p): return pltpu.make_async_copy(pays[0][0].at[:, pl.ds(0, PAIR)], keep.at[p], load_sem.at[p])
    def swap0(p): return send(pays[0][1].at[:, pl.ds(0, PAIR)], came0.at[p], out_sem.at[0, p], in_sem.at[0, p], flip(me, CORE))
    def a1(p): return send(put1.at[p, 0], came1.at[p, 0], out_sem.at[1, p], in_sem.at[1, p], flip(me, XB))
    def b1(p): return send(put1.at[p, 1], came1.at[p, 1], out_sem.at[2, p], in_sem.at[2, p], flip(me, YB))
    def a2(p): return send(put2.at[p, 0], came2.at[p, 0], out_sem.at[3, p], in_sem.at[3, p], flip(me, YB))
    def b2(p): return send(put2.at[p, 1], came2.at[p, 1], out_sem.at[4, p], in_sem.at[4, p], flip(me, XB))
    def far(p): return send(put3.at[p], came3.at[p], out_sem.at[5, p], in_sem.at[5, p], flip(me, FAR))
    def near(p): return send(put4.at[p], came4.at[p], out_sem.at[6, p], in_sem.at[6, p], flip(me, NEAR))
    def base(p, block, h):
        cut = slice(h * HALF, h * HALF + HALF)
        return keep[p, block, cut, :].astype(F32) + came0[p, block, cut, :].astype(F32)
    def second(p, z, other, h):
        block = z * 4 + (other * 2 if h == 0 else other)
        return base(p, block, h) + came1[p, h, z * 2 + other].astype(F32)
    def third(p, z, h):
        return second(p, z, 0, h) + came2[p, h, z].astype(F32)
    def fourth(p, zl, h):
        return third(p, zl, h) + came3[p, zl, h * HALF : h * HALF + HALF, :].astype(F32)
    def tick(t, _):
        @pl.when(t < ticks)
        def _():
            p = t
            loaded(p).wait()
            swap0(p).wait_recv()
            for z in range(4):
                for other in range(2):
                    put1[p, 0, z * 2 + other] = base(p, z * 4 + other * 2 + 1, 0).astype(BF16)
            a1(p).start()
            for z in range(4):
                for other in range(2):
                    put1[p, 1, z * 2 + other] = base(p, z * 4 + 2 + other, 1).astype(BF16)
            b1(p).start()
        @pl.when((t >= 1) & (t < ticks + 1))
        def _():
            p = t - 1
            a1(p).wait_recv()
            for z in range(4): put2[p, 0, z] = second(p, z, 1, 0).astype(BF16)
            a2(p).start()
            b1(p).wait_recv()
            for z in range(4): put2[p, 1, z] = second(p, z, 1, 1).astype(BF16)
            b2(p).start()
        @pl.when((t >= 2) & (t < ticks + 2))
        def _():
            p = t - 2
            a2(p).wait_recv()
            b2(p).wait_recv()
            for zl in range(2):
                for h in range(2):
                    put3[p, zl, h * HALF : h * HALF + HALF, :] = third(p, 2 + zl, h).astype(BF16)
            far(p).start()
        @pl.when((t >= 3) & (t < ticks + 3))
        def _():
            p = t - 3
            far(p).wait_recv()
            for h in range(2): put4[p, h * HALF : h * HALF + HALF, :] = fourth(p, 1, h).astype(BF16)
            near(p).start()
        @pl.when(t >= 4)
        def _():
            p = t - 4
            near(p).wait_recv()
            for h in range(2):
                at = pl.ds(pl.multiple_of(p * PAIR + h * HALF, HALF), HALF)
                out[at, :] = fourth(p, 0, h) + came4[p, h * HALF : h * HALF + HALF, :].astype(F32)
        return 0
    lax.fori_loop(0, ticks + 4, tick, 0)
    def close(p, _):
        for copy in (swap0, a1, b1, a2, b2, far, near):
            copy(p).wait_send()
        return 0
    lax.fori_loop(0, ticks, close, 0)

def scatter_rows(pays):
    ticks = sum(k.shape[1] for k, _ in pays) // PAIR
    width = pays[0][0].shape[2]
    v = lambda *s: pltpu.VMEM((ticks,)+s+(width,), BF16)
    flat = [a for p in pays for a in p]
    return pl.pallas_call(
        functools.partial(scatter_body, len(pays)),
        out_shape=jax.ShapeDtypeStruct((ticks * PAIR, width), F32),
        in_specs=[pl.BlockSpec(memory_space=pl.ANY)] * len(flat),
        out_specs=pl.BlockSpec(memory_space=pltpu.VMEM),
        scratch_shapes=[v(16, PAIR), v(16, PAIR), v(2, 8, HALF), v(2, 8, HALF), v(2, 4, HALF), v(2, 4, HALF), v(2, PAIR), v(2, PAIR), v(PAIR), v(PAIR),
            pltpu.SemaphoreType.DMA((ticks,)), pltpu.SemaphoreType.DMA((7, ticks)), pltpu.SemaphoreType.DMA((7, ticks))],
        compiler_params=pltpu.CompilerParams(collective_id=1, has_side_effects=True, vmem_limit_bytes=60*MIB),
        name="scatter_rows",
    )(*flat)


def absolute(keep, send):
    return jnp.stack([keep, send], axis=1).reshape((BLOCKS,) + keep.shape[1:])


def pack_vectors(vectors, devices):
    own = vectors[0].shape[0]
    rows = jnp.stack(vectors)
    return jnp.pad(rows, ((0, 32 - len(vectors)), (0, 1024 - own)))


def gather(rows):
    return lax.all_gather(rows, "dp", axis=0, tiled=True)


def on_device(
    devices, tokens, memory, target_lengths, memory_lengths, cotangent,
    self_query, self_key, self_value, self_output, first_gain, first_shift,
    cross_query, cross_key, cross_value, cross_output, second_gain, second_shift,
    inner_weight, outer_weight, third_gain, third_shift,
):
    width = tokens.shape[1]
    hidden = inner_weight.shape[1]
    direct = devices == BLOCKS
    squares = [cross_key, cross_value, self_query, self_key, self_value, self_output, cross_query, cross_output]
    vectors = [first_gain, first_shift, second_gain, second_shift, third_gain, third_shift]
    if direct:
        me = lax.axis_index("dp").astype(jnp.int32).reshape(1)
        pack = jnp.concatenate(squares + [pack_vectors(vectors, devices)], axis=0)
        stack = gather_rows(pack)
        vecs = stack[:, 256:264, :32].transpose(1, 0, 2).reshape(8, width).astype(F32)
        parts = [outer_weight] + [inner_weight[:, i : i + width] for i in range(0, hidden, width)]
        pack = jnp.concatenate(parts, axis=0)
        wide = gather(pack).reshape(BLOCKS, -1, width)
    else:
        me = jnp.zeros((1,), jnp.int32)
        stack = jnp.concatenate([gather(w).reshape(BLOCKS, 32, width) for w in squares], axis=1)
        vecs = jnp.pad(jnp.stack([gather(v) for v in vectors]), ((0, 2), (0, 0))).astype(F32)
        inner_full = gather(inner_weight)
        parts = [gather(outer_weight).reshape(BLOCKS, 128, width)]
        parts += [inner_full[:, i : i + width].reshape(BLOCKS, 32, width) for i in range(0, hidden, width)]
        wide = jnp.concatenate(parts, axis=1)

    keys, values = kv_project(memory, stack, 0, 1)
    q, k, v, mixture, first_sum, first_out, first_low, cross_q, lse = self_forward(
        target_lengths, tokens, stack, (2, 3, 4, 5, 6), vecs
    )
    cross_mixture, cross_lse = cross_forward(memory_lengths, cross_q, keys, values)
    second_sum, second, second_low = second_norm(cross_mixture, stack, 7, first_out, vecs)
    act, slope, output_rows, gts, go, third_grads = ffn_forward(second_low, second, wide, cotangent, vecs)
    gi, gss, gci, gcm, second_grads = ffn_backward(go, gts, slope, wide, second_sum, stack, 7, vecs)
    ffn_pay = ffn_weights(act, go, second_low, gi)
    dq, dk, dv = cross_backward(memory_lengths, cross_q, keys, values, gcm, cross_mixture, cross_lse)
    cross_pay = square_weights(
        me, [(first_low, dq), (memory, dk), (memory, dv), (cross_mixture, gci)], "cross_weights"
    )
    gfs, gsi, gq, gk, gv, first_grads = self_backward(
        target_lengths, gss, dq, stack, 6, 5, first_sum, vecs, q, k, v, mixture, lse
    )
    grads = jnp.concatenate([first_grads[:2], second_grads[:2], third_grads[:2], jnp.zeros((26, width), F32)])
    self_pay = square_weights(me, [(tokens, gq), (tokens, gk), (tokens, gv), (mixture, gsi)], "self_weights", grads)
    memory_grad = memory_gradient(dk, dv, stack, 0, 1)
    tokens_grad = tokens_gradient(gfs, gq, gk, gv, stack, (2, 3, 4))

    if direct:
        ffn_own = lax.psum_scatter(ffn_pay.reshape(-1, width), "dp", scatter_dimension=0, tiled=True).astype(F32)
        outer_own = ffn_own[:128]
        inner_own = jnp.concatenate([ffn_own[i : i + 32] for i in range(128, 256, 32)], axis=1)
        owned = scatter_rows([cross_pay, self_pay])
        cross_own = [owned[i : i + 32] for i in range(0, 128, 32)]
        self_own = [owned[i : i + 32] for i in range(128, 256, 32)]
        vec_own = [owned[256 + i, :32] for i in range(6)]
    else:
        def summed(rows):
            return lax.psum_scatter(rows.astype(F32), "dp", scatter_dimension=0, tiled=True)

        outer_own = summed(ffn_pay[:, :128].reshape(-1, width))
        inner_own = summed(
            jnp.concatenate([ffn_pay[:, i : i + 32].reshape(-1, width) for i in range(128, 256, 32)], axis=1)
        )
        cross_rows, self_rows = absolute(*cross_pay), absolute(*self_pay)
        cross_own = [summed(cross_rows[:, i : i + 32].reshape(-1, width)) for i in range(0, 128, 32)]
        self_own = [summed(self_rows[:, i : i + 32].reshape(-1, width)) for i in range(0, 128, 32)]
        vec_own = [summed(grads[i]) for i in range(6)]

    return (
        output_rows, tokens_grad, memory_grad,
        *self_own, vec_own[0], vec_own[1],
        *cross_own, vec_own[2], vec_own[3],
        inner_own, outer_own, vec_own[4], vec_own[5],
    )


def solution(mesh):
    rows, line = P("dp", None), P("dp")
    block = [rows] * 4 + [line] * 2
    placed = (rows, rows, line, line, rows, *block, *block, rows, rows, line, line)
    return jax.shard_map(
        functools.partial(on_device, mesh.shape["dp"]),
        mesh=mesh,
        in_specs=placed,
        out_specs=(rows, rows, rows, *block, *block, rows, rows, line, line),
        check_vma=False,
    )
```

```python
import functools
import math

import jax
import jax.numpy as jnp
from jax import lax
from jax.experimental import pallas as pl
from jax.experimental.pallas import tpu as pltpu
from jax.sharding import PartitionSpec as P

HEAD = 64
EPS = 1e-05
SCALE = 1.0 / math.sqrt(HEAD)
LOG2E = 1.4426950408889634
BLOCKS = 32
MIB = 1024 * 1024
F32 = jnp.float32
BF16 = jnp.bfloat16
PAIR, HALF = 32, 16
CORE, XBIT, YBIT, NEAR, FAR, BOTH = PARTNERS = (1, 2, 4, 8, 16, 24)
LAG = 2
GATHER_LAG = 1
FIRST_TILE = 7


def nn(a, b):
    return jnp.dot(a, b, preferred_element_type=F32)


def nt(a, b):
    return lax.dot_general(a, b, (((1,), (1,)), ((), ())), preferred_element_type=F32)


def tn(a, b):
    return lax.dot_general(a, b, (((0,), (0,)), ((), ())), preferred_element_type=F32)


def whole(ref):
    return ref[...].reshape(-1, ref.shape[-1])


def call(body, name, out, grid=(), ins=None, outs=None, scratch=(), prefetch=0, limit=56, flops=0, moved=0):
    return pl.pallas_call(
        body,
        out_shape=out,
        grid_spec=pltpu.PrefetchScalarGridSpec(
            num_scalar_prefetch=prefetch,
            grid=grid,
            in_specs=ins,
            out_specs=outs,
            scratch_shapes=scratch,
        ),
        compiler_params=pltpu.CompilerParams(vmem_limit_bytes=limit * MIB),
        cost_estimate=pl.CostEstimate(flops=flops, bytes_accessed=moved, transcendentals=0),
        name=name,
    )


def full(shape):
    return pl.BlockSpec(shape, lambda *_: (0,) * len(shape))


def weight(at):
    return pl.BlockSpec((BLOCKS, 32, 1024), lambda *_: (0, at, 0))


def shape(dims, dtype):
    return jax.ShapeDtypeStruct(dims, dtype)


def norm_parts(summed):
    average = jnp.mean(summed, axis=-1, keepdims=True)
    centred = summed - average
    spread = jnp.mean(centred * centred, axis=-1, keepdims=True)
    scale = lax.rsqrt(spread + EPS)
    return centred * scale, scale


def norm_back(summed, gain, upstream):
    normal, scale = norm_parts(summed)
    grad_gain = jnp.sum(upstream * normal, axis=0, keepdims=True)
    grad_shift = jnp.sum(upstream, axis=0, keepdims=True)
    scaled = upstream * gain
    first = jnp.mean(scaled, axis=-1, keepdims=True)
    second = jnp.mean(scaled * normal, axis=-1, keepdims=True)
    return scale * (scaled - first - normal * second), grad_gain, grad_shift


def lanes(rows):
    return lax.broadcasted_iota(jnp.int32, (rows, 128), 1)


def stack_pair(rows):
    low = lanes(rows.shape[0]) < HEAD
    zero = jnp.zeros_like(rows)
    return jnp.concatenate([jnp.where(low, rows, zero), jnp.where(low, zero, rows)], axis=0)


def unstack_pair(stacked):
    half = stacked.shape[0] // 2
    return jnp.where(lanes(half) < HEAD, stacked[:half], stacked[half:])


def pair_forward(stacked, keys, values, mask):
    scores = nt(stacked, keys)
    if mask is not None:
        scores = mask(scores)
    peak = jnp.max(scores, axis=-1, keepdims=True)
    raised = jnp.exp2((scores - peak) * (SCALE * LOG2E))
    total = jnp.sum(raised, axis=-1, keepdims=True)
    mixed = nn(raised.astype(BF16), values) / total
    return mixed, peak * SCALE + jnp.log(total)


def pair_tile_back(q2, g2, keys, values, totals, inner, mask):
    scores = nt(keys, q2)
    probs = jnp.exp2(scores * (SCALE * LOG2E) - totals)
    if mask is not None:
        probs = mask(probs)
    grad_probs = nt(values, g2)
    grad_scores = (probs * (grad_probs - inner)).astype(BF16)
    grad_values = nn(probs.astype(BF16), g2)
    grad_keys = nn(grad_scores, q2) * SCALE
    grad_queries = tn(keys, grad_scores)
    return grad_queries, grad_keys, grad_values


def pair_inner(mixture, grad):
    product = mixture.astype(F32) * grad.astype(F32)
    half = jnp.where(
        (lax.broadcasted_iota(jnp.int32, (8, 128), 1) // HEAD)
        == lax.broadcasted_iota(jnp.int32, (8, 128), 0),
        1.0,
        0.0,
    ).astype(F32)
    sums = lax.dot_general(
        half, product, (((1,), (1,)), ((), ())),
        preferred_element_type=F32, precision=lax.Precision.HIGHEST,
    )
    return jnp.concatenate([sums[0:1], sums[1:2]], axis=1)


def join_grad_queries(grad):
    count = grad.shape[1] // 2
    joined = jnp.concatenate([grad[:HEAD, :count], grad[HEAD:, count:]], axis=0) * SCALE
    return joined.T.astype(BF16)


def kv_body(memory, wk, wv, keys, values):
    rows = memory[...]
    keys[...] = nn(rows, whole(wk)).astype(BF16)
    values[...] = nn(rows, whole(wv)).astype(BF16)


def kv_project(memory, stack, at_k, at_v):
    count, width = memory.shape
    tile = 512
    spec = pl.BlockSpec((tile, width), lambda i: (i, 0))
    return call(
        kv_body, "cross_kv", [shape(memory.shape, BF16)] * 2, (count // tile,),
        [spec, weight(at_k), weight(at_v)], [spec, spec],
        flops=4 * count * width * width, moved=12 * MIB + 4 * MIB,
    )(memory, stack, stack)


def self_attention(live, q_o, k_o, v_o, mix_o, lse_o):
    count, width = q_o.shape
    at_q = lax.rem(lax.broadcasted_iota(jnp.int32, (2 * count, count), 0), count)
    at_k = lax.broadcasted_iota(jnp.int32, (2 * count, count), 1)
    allowed = (at_k <= at_q) & (at_k < live)
    column = lanes(count)
    totals = jnp.zeros((count, 128), F32)
    for pair in range(width // 128):
        cut = slice(pair * 128, pair * 128 + 128)
        mixed, log_total = pair_forward(
            stack_pair(q_o[:, cut]), k_o[:, cut], v_o[:, cut],
            lambda scores: jnp.where(allowed, scores, -1e30),
        )
        mix_o[:, cut] = unstack_pair(mixed).astype(BF16)
        totals = jnp.where(column == 2 * pair, log_total[:count], totals)
        totals = jnp.where(column == 2 * pair + 1, log_total[count:], totals)
    lse_o[...] = totals.T


def self_body(length, tokens, wq, wk, wv, wo, wcq, vecs, q_o, k_o, v_o, mix_o, sum_o, first_o, low_o, cq_o, lse_o):
    rows = tokens[...]
    count, width = rows.shape
    q_o[...] = nn(rows, whole(wq)).astype(BF16)
    k_o[...] = nn(rows, whole(wk)).astype(BF16)
    v_o[...] = nn(rows, whole(wv)).astype(BF16)
    self_attention(length[0], q_o, k_o, v_o, mix_o, lse_o)
    summed = rows.astype(F32) + nn(mix_o[...], whole(wo))
    sum_o[...] = summed
    normal, _ = norm_parts(summed)
    first = normal * vecs[0:1] + vecs[1:2]
    first_o[...] = first
    low = first.astype(BF16)
    low_o[...] = low
    cq_o[...] = nn(low, whole(wcq)).astype(BF16)


def self_forward(length, tokens, stack, at, vecs):
    count, width = tokens.shape
    low = shape(tokens.shape, BF16)
    wide = shape(tokens.shape, F32)
    spec = full(tokens.shape)
    return call(
        self_body, "self_forward",
        [low, low, low, low, wide, wide, low, low, shape((128, count), F32)], (1,),
        [spec] + [weight(k) for k in at] + [full(vecs.shape)],
        [spec] * 8 + [full((128, count))], prefetch=1,
        flops=10 * count * width * width, moved=16 * MIB,
    )(length, tokens, stack, stack, stack, stack, stack, vecs)


def cross_body(length, q, k, v, mix_o, lse_o):
    count = q.shape[0]
    slots = k.shape[0]
    live = length[0]
    q2 = stack_pair(q[...])
    keys = k[...]
    values = v[...]
    half = slots // 2
    tile = 128
    column = lax.broadcasted_iota(jnp.int32, (tile, slots - half), 1) + half

    def mask(scores):
        upper = jnp.where(column < live, scores[:, half:], -1e30)
        return jnp.concatenate([scores[:, :half], upper], axis=1)

    mixes, logs = [], []
    for at in range(0, 2 * count, tile):
        mixed, log_total = pair_forward(q2[at : at + tile], keys, values, mask)
        mixes.append(mixed)
        logs.append(log_total)
    mix_o[...] = unstack_pair(jnp.concatenate(mixes, axis=0)).astype(BF16)
    logs = jnp.concatenate(logs, axis=0)
    column = lanes(count)
    totals = jnp.where(column == 0, logs[:count], jnp.where(column == 1, logs[count:], 0.0))
    lse_o[0] = totals.T[:8]


def cross_forward(length, q, k, v):
    count, width = q.shape
    slots = k.shape[0]
    pairs = width // 128
    return call(
        cross_body, "cross_forward",
        [shape(q.shape, BF16), shape((pairs, 8, count), F32)], (pairs,),
        [pl.BlockSpec((count, 128), lambda i, _: (0, i))]
        + [pl.BlockSpec((slots, 128), lambda i, _: (0, i))] * 2,
        [pl.BlockSpec((count, 128), lambda i, _: (0, i)), pl.BlockSpec((1, 8, count), lambda i, _: (i, 0, 0))],
        prefetch=1, flops=16 * count * slots * width, moved=10 * MIB,
    )(length, q, k, v)


def second_rows(mixture, wo, first, vecs, sum_o, second_o, low_o):
    summed = first + nn(mixture, wo)
    sum_o[...] = summed
    normal, _ = norm_parts(summed)
    second = normal * vecs[2:3, :] + vecs[3:4, :]
    second_o[...] = second
    low_o[...] = second.astype(BF16)


def second_body(mixture, wo, first, vecs, sum_o, second_o, low_o):
    second_rows(mixture[...], whole(wo), first[...], vecs, sum_o, second_o, low_o)


def second_norm(mixture, stack, at, first, vecs):
    spec = full(mixture.shape)
    return call(
        second_body, "second_norm",
        [shape(mixture.shape, F32), shape(mixture.shape, F32), shape(mixture.shape, BF16)], (1,),
        [spec, weight(at), spec, full(vecs.shape)], [spec] * 3,
        flops=MIB * 512, moved=6 * MIB,
    )(mixture, stack, first, vecs)


def erf(x):
    return lax.erf(x)


def ffn_body(low, second, inner, outer, cot, vecs, act_o, slope_o, out_o, gts_o, go_o, grads_o, total):
    step = pl.program_id(0)
    pre = nn(low[...], whole(inner))
    half = 0.5 * (1.0 + erf(pre * math.sqrt(0.5)))
    active = (pre * half).astype(BF16)
    act_o[...] = active
    slope_o[...] = half + pre * (jnp.exp(-0.5 * pre * pre) * (1.0 / math.sqrt(2.0 * math.pi)))
    part = nn(active, whole(outer))

    @pl.when(step == 0)
    def _():
        total[...] = second[...] + part

    @pl.when(step > 0)
    def _():
        total[...] += part

    @pl.when(step == pl.num_programs(0) - 1)
    def _():
        summed = total[...]
        normal, _ = norm_parts(summed)
        out_o[...] = (normal * vecs[4:5] + vecs[5:6]).astype(BF16)
        grad, gain, shift = norm_back(summed, vecs[4:5], cot[...].astype(F32))
        gts_o[...] = grad
        go_o[...] = grad.astype(BF16)
        grads_o[...] = jnp.concatenate([gain, shift] + [jnp.zeros_like(gain)] * 6, axis=0)


def ffn_forward(low, second, stack, cot, vecs):
    count, width = low.shape
    spec = full(low.shape)
    wide = pl.BlockSpec((count, 1024), lambda i: (0, i))
    return call(
        ffn_body, "ffn_forward",
        [shape((count, 4096), BF16), shape((count, 4096), F32), shape(low.shape, BF16), shape(low.shape, F32), shape(low.shape, BF16), shape((8, width), F32)],
        (4,),
        [spec, spec, pl.BlockSpec((BLOCKS, 32, 1024), lambda i: (0, i, 0)), pl.BlockSpec((8, 128, 1024), lambda i: (i, 1, 0)), spec, full(vecs.shape)],
        [wide, wide, spec, spec, spec, full((8, width))],
        scratch=[pltpu.VMEM(low.shape, F32)],
        flops=16 * count * width * width, moved=24 * MIB,
    )(low, second, stack, stack, cot, vecs)


def ffn_back_body(go, gts, slope, inner, outer, summed, wo, vecs, gi_o, gss_o, gci_o, gcm_o, grads_o, total):
    step = pl.program_id(0)
    grad = nt(go[...], whole(outer))
    low = (grad * slope[...]).astype(BF16)
    gi_o[...] = low
    part = nt(low, whole(inner))

    @pl.when(step == 0)
    def _():
        total[...] = gts[...] + part

    @pl.when(step > 0)
    def _():
        total[...] += part

    @pl.when(step == pl.num_programs(0) - 1)
    def _():
        grad, gain, shift = norm_back(summed[...], vecs[2:3], total[...])
        gss_o[...] = grad
        low = grad.astype(BF16)
        gci_o[...] = low
        gcm_o[...] = nt(low, whole(wo)).astype(BF16)
        grads_o[...] = jnp.concatenate([gain, shift] + [jnp.zeros_like(gain)] * 6, axis=0)


def ffn_backward(go, gts, slope, stack, summed, squares, at, vecs):
    count, width = go.shape
    spec = full(go.shape)
    wide = pl.BlockSpec((count, 1024), lambda i: (0, i))
    low = shape(go.shape, BF16)
    return call(
        ffn_back_body, "ffn_backward",
        [shape((count, 4096), BF16), shape(go.shape, F32), low, low, shape((8, width), F32)],
        (4,),
        [spec, spec, wide, pl.BlockSpec((BLOCKS, 32, 1024), lambda i: (0, i, 0)), pl.BlockSpec((8, 128, 1024), lambda i: (i, 1, 0)), spec, weight(at), full(vecs.shape)],
        [wide, spec, spec, spec, full((8, width))],
        scratch=[pltpu.VMEM(go.shape, F32)],
        flops=18 * count * width * width, moved=26 * MIB,
    )(go, gts, slope, stack, stack, summed, squares, vecs)


def cross_back_body(length, q, k, v, g, mixture, lse, dq_o, dk_o, dv_o):
    live = length[0]
    slots = k.shape[0]
    count = q.shape[0]
    q2 = stack_pair(q[...])
    g2 = stack_pair(g[...])
    totals = jnp.concatenate([lse[0, 0:1], lse[0, 1:2]], axis=1) * LOG2E
    inner = pair_inner(mixture[...], g[...])
    tile = 256
    grad_q = jnp.zeros((128, 2 * count), F32)
    for at in range(0, slots, tile):
        mask = None
        if at + tile > slots // 2:
            row = lax.broadcasted_iota(jnp.int32, (tile, 2 * count), 0) + at

            def mask(probs, row=row):
                return jnp.where(row < live, probs, 0.0)

        cut = slice(at, at + tile)
        dq, dk, dv = pair_tile_back(q2, g2, k[cut], v[cut], totals, inner, mask)
        grad_q = grad_q + dq
        dk_o[cut] = dk.astype(BF16)
        dv_o[cut] = dv.astype(BF16)
    dq_o[...] = join_grad_queries(grad_q)


def cross_backward(length, q, k, v, g, mixture, lse):
    count, width = q.shape
    slots = k.shape[0]
    pairs = width // 128
    small = pl.BlockSpec((count, 128), lambda i, _: (0, i))
    large = pl.BlockSpec((slots, 128), lambda i, _: (0, i))
    return call(
        cross_back_body, "cross_backward",
        [shape(q.shape, BF16), shape(k.shape, BF16), shape(k.shape, BF16)], (pairs,),
        [small, large, large, small, small, pl.BlockSpec((1, 8, count), lambda i, _: (i, 0, 0))],
        [small, large, large], prefetch=1,
        flops=40 * count * slots * width, moved=18 * MIB,
    )(length, q, k, v, g, mixture, lse)


def memory_grad_body(dk, dv, wk, wv, out):
    out[...] = nt(dk[...], whole(wk)) + nt(dv[...], whole(wv))


def memory_gradient(dk, dv, stack, at_k, at_v):
    count, width = dk.shape
    tile = 512
    spec = pl.BlockSpec((tile, width), lambda i: (i, 0))
    return call(
        memory_grad_body, "memory_grad", shape(dk.shape, F32), (count // tile,),
        [spec, spec, weight(at_k), weight(at_v)], spec,
        flops=4 * count * width * width, moved=20 * MIB,
    )(dk, dv, stack, stack)


def self_back_body(length, gss, dcq, wcq, summed, wo, vecs, q, k, v, mixture, lse, gfs_o, gsi_o, gq_o, gk_o, gv_o, grads_o):
    live = length[0]
    count, width = gss.shape
    upstream = gss[...] + nt(dcq[...], whole(wcq))
    grad, gain, shift = norm_back(summed[...], vecs[0:1], upstream)
    gfs_o[...] = grad
    grads_o[...] = jnp.concatenate([gain, shift] + [jnp.zeros_like(gain)] * 6, axis=0)
    low = grad.astype(BF16)
    gsi_o[...] = low
    mix_grad = nt(low, whole(wo)).astype(BF16)
    at_k = lax.broadcasted_iota(jnp.int32, (count, 2 * count), 0)
    at_q = lax.rem(lax.broadcasted_iota(jnp.int32, (count, 2 * count), 1), count)
    allowed = (at_k <= at_q) & (at_k < live)
    for pair in range(width // 128):
        cut = slice(pair * 128, pair * 128 + 128)
        g = mix_grad[:, cut]
        totals = jnp.concatenate([lse[2 * pair : 2 * pair + 1], lse[2 * pair + 1 : 2 * pair + 2]], axis=1) * LOG2E
        scores_back = pair_tile_back(
            stack_pair(q[:, cut]), stack_pair(g), k[:, cut], v[:, cut], totals,
            pair_inner(mixture[:, cut], g),
            lambda probs: jnp.where(allowed, probs, 0.0),
        )
        dq, dk, dv = scores_back
        gq_o[:, cut] = join_grad_queries(dq)
        gk_o[:, cut] = dk.astype(BF16)
        gv_o[:, cut] = dv.astype(BF16)


def self_backward(length, gss, dcq, stack, at_cq, at_o, summed, vecs, q, k, v, mixture, lse):
    count, width = q.shape
    spec = full(q.shape)
    low = shape(q.shape, BF16)
    return call(
        self_back_body, "self_backward",
        [shape(q.shape, F32), low, low, low, low, shape((8, width), F32)], (1,),
        [spec, spec, weight(at_cq), spec, weight(at_o), full(vecs.shape), spec, spec, spec, spec, full(lse.shape)],
        [spec] * 5 + [full((8, width))], prefetch=1,
        flops=8 * count * width * width, moved=12 * MIB,
    )(length, gss, dcq, stack, summed, stack, vecs, q, k, v, mixture, lse)


def tokens_grad_body(gfs, gq, gk, gv, wq, wk, wv, out):
    out[...] = gfs[...] + nt(gq[...], whole(wq)) + nt(gk[...], whole(wk)) + nt(gv[...], whole(wv))


def tokens_gradient(gfs, gq, gk, gv, stack, at):
    spec = full(gfs.shape)
    return call(
        tokens_grad_body, "tokens_grad", shape(gfs.shape, F32), (1,),
        [spec] * 4 + [weight(k) for k in at], spec,
        flops=6 * MIB * 256, moved=10 * MIB,
    )(gfs, gq, gk, gv, stack, stack, stack)


def place(keep, send, at, size, pieces, me):
    low = lax.rem(me, 8)
    for j in range(8):
        rows = pieces(lax.bitwise_xor(low, j))
        target = send if j % 2 else keep
        target[j // 2, at : at + size, :] = rows.astype(BF16)


def group_of(step, me):
    return lax.bitwise_xor(step, lax.div(me[0], 8))


def payload(rows, width):
    out = [shape((16, rows, width), BF16)] * 2
    spec = [pl.BlockSpec((4, rows, width), lambda i, _: (i, 0, 0))] * 2
    return out, spec


def ffn_weights_body(me, act, go, low, gi, keep, send, held):
    step = pl.program_id(0)

    @pl.when(step < 4)
    def _():
        held[...] = tn(act[...], go[...])
        place(keep, send, 0, 128, lambda d: held[pl.ds(pl.multiple_of(d * 128, 128), 128), :], me[0])

    @pl.when(step >= 4)
    def _():
        for part in range(4):
            held[:256, :] = tn(low[...], gi[:, part * 1024 : part * 1024 + 1024])
            place(keep, send, part * 32, 32, lambda d: held[pl.ds(pl.multiple_of(d * 32, 32), 32), :], me[0])


def ffn_weights(me, act, go, low, gi):
    count, width = go.shape
    spec = pl.BlockSpec((4, 128, width), lambda i, me: (lax.rem(i, 4), lax.div(i, 4), 0))
    return call(
        ffn_weights_body, "ffn_weights", [shape((16, 256, width), BF16)] * 2, (8,),
        [
            pl.BlockSpec((count, 1024), lambda i, me: (0, group_of(jnp.minimum(i, 3), me))),
            full(go.shape),
            pl.BlockSpec((count, 256), lambda i, me: (0, group_of(jnp.maximum(i - 4, 0), me))),
            full(gi.shape),
        ],
        [spec, spec], [pltpu.VMEM((1024, width), F32)], 1,
        flops=16 * count * width * width, moved=22 * MIB,
    )(me, act, go, low, gi)


def square_body(me, *refs):
    count = (len(refs) - 3) // 2
    keep, send, held = refs[-3:]
    for at in range(count):
        held[...] = tn(refs[2 * at][...], refs[2 * at + 1][...])
        place(keep, send, at * 32, 32, lambda d: held[pl.ds(pl.multiple_of(d * 32, 32), 32), :], me[0])


def square_weights(me, pairs, name):
    width = pairs[0][0].shape[1]
    out, spec = payload(128, width)
    ins, operands, flops = [], [], 0
    for rows, grads in pairs:
        ins.append(pl.BlockSpec((rows.shape[0], 256), lambda i, me: (0, group_of(i, me))))
        ins.append(full(grads.shape))
        operands += [rows, grads]
        flops += 2 * rows.shape[0] * width * width
    return call(
        square_body, name, out, (4,), ins, spec,
        [pltpu.VMEM((256, width), F32)], 1, flops=flops, moved=20 * MIB,
    )(me, *operands)


def flip(me, bits):
    for bit in (1, 2, 4, 8, 16):
        if bits & bit:
            me = me + bit - 2 * bit * lax.rem(lax.div(me, bit), 2)
    return me


def remote(src, dst, out_sem, in_sem, to):
    return pltpu.make_async_remote_copy(
        src_ref=src, dst_ref=dst, send_sem=out_sem, recv_sem=in_sem,
        device_id=(to,), device_id_type=pl.DeviceIdType.MESH,
    )


def greet(me):
    barrier = pltpu.get_barrier_semaphore()
    for bit in PARTNERS:
        pl.semaphore_signal(barrier, inc=1, device_id=(flip(me, bit),), device_id_type=pl.DeviceIdType.MESH)
    pl.semaphore_wait(barrier, len(PARTNERS))


class Scatter:
    def __init__(self, me, pays, refs, out):
        self.me, self.pays, self.out = me, pays, out
        (self.keep, self.came0, self.came1, self.came2, self.came3,
         self.load_sem, self.out_sem, self.in_sem) = refs
        self.ticks = self.keep.shape[0]
        self.loads = sum(kept.shape[3] for kept, _ in pays) // PAIR

    @staticmethod
    def scratch(ticks, width):
        def held(*dims):
            return pltpu.VMEM((ticks,) + dims + (width,), BF16)

        return [
            held(4, 2, 2, PAIR), held(4, 2, 2, PAIR), held(2, 4, 2, HALF), held(2, 4, HALF), held(3, PAIR),
            pltpu.SemaphoreType.DMA((ticks,)), pltpu.SemaphoreType.DMA((8, ticks)), pltpu.SemaphoreType.DMA((8, ticks)),
        ]

    def link(self, stage, p, src, dst, bit):
        return remote(src, dst, self.out_sem.at[stage, p], self.in_sem.at[stage, p], flip(self.me, bit))

    def load(self, p, kept, at):
        return pltpu.make_async_copy(kept.at[:, :, :, pl.ds(at, PAIR)], self.keep.at[p], self.load_sem.at[p])

    def swap(self, p, sent):
        return self.link(0, p, sent, self.came0.at[p], CORE)

    def hop(self, stage, p):
        keep, up, down = self.keep, pl.ds(0, HALF), pl.ds(HALF, HALF)
        if stage == 1:
            return self.link(1, p, keep.at[p, :, :, 1, up], self.came1.at[p, 0], XBIT)
        if stage == 2:
            return self.link(2, p, keep.at[p, :, 1, :, down], self.came1.at[p, 1], YBIT)
        if stage == 3:
            return self.link(3, p, keep.at[p, :, 1, 0, up], self.came2.at[p, 0], YBIT)
        if stage == 4:
            return self.link(4, p, keep.at[p, :, 0, 1, down], self.came2.at[p, 1], XBIT)
        z = stage - 4
        return self.link(stage, p, keep.at[p, z, 0, 0], self.came3.at[p, z - 1], (NEAR, FAR, BOTH)[z - 1])

    def begin(self):
        greet(self.me)
        p = 0
        for kept, sent in self.pays:
            for at in range(0, kept.shape[3], PAIR):
                self.load(p, kept, at).start()
                self.swap(p, sent.at[:, :, :, pl.ds(at, PAIR)]).start()
                p += 1

    def total(self, p, z, y, x, h, depth):
        cut = slice(h * HALF, h * HALF + HALF)
        sum_ = self.keep[p, z, y, x, cut, :].astype(F32) + self.came0[p, z, y, x, cut, :].astype(F32)
        if depth > 1:
            sum_ = sum_ + self.came1[p, h, z, y if h == 0 else x].astype(F32)
        if depth > 2:
            sum_ = sum_ + self.came2[p, h, z].astype(F32)
        if depth > 3:
            for other in range(3):
                sum_ = sum_ + self.came3[p, other, cut, :].astype(F32)
        return sum_

    def sums(self, p, blocks, h, depth):
        for z, y, x in blocks:
            self.keep[p, z, y, x, h * HALF : h * HALF + HALF, :] = self.total(p, z, y, x, h, depth).astype(BF16)

    def tick(self, t):
        ticks = self.ticks

        def stage(at):
            return pl.when((t >= at * LAG) & (t < ticks + at * LAG))

        @pl.when((t >= 0) & (t < self.loads))
        def _():
            self.load(t, self.pays[0][0], 0).wait()

        @stage(0)
        def _():
            self.swap(t, self.came0.at[t]).wait_recv()
            self.sums(t, [(z, y, 1) for z in range(4) for y in range(2)], 0, 1)
            self.hop(1, t).start()
            self.sums(t, [(z, 1, x) for z in range(4) for x in range(2)], 1, 1)
            self.hop(2, t).start()

        @stage(1)
        def _():
            p = t - 1 * LAG
            self.hop(1, p).wait_recv()
            self.sums(p, [(z, 1, 0) for z in range(4)], 0, 2)
            self.hop(3, p).start()
            self.hop(2, p).wait_recv()
            self.sums(p, [(z, 0, 1) for z in range(4)], 1, 2)
            self.hop(4, p).start()

        @stage(2)
        def _():
            p = t - 2 * LAG
            self.hop(3, p).wait_recv()
            self.hop(4, p).wait_recv()
            for z in (2, 3, 1):
                for h in range(2):
                    self.sums(p, [(z, 0, 0)], h, 3)
                self.hop(4 + z, p).start()

        @stage(3)
        def _():
            p = t - 3 * LAG
            for z in (1, 2, 3):
                self.hop(4 + z, p).wait_recv()
            for h in range(2):
                at = pl.ds(pl.multiple_of(p * PAIR + h * HALF, HALF), HALF)
                self.out[at, :] = self.total(p, 0, 0, 0, h, 4)

    def close(self):
        def ended(p, _):
            self.swap(p, self.came0.at[p]).wait_send()
            for stage in range(1, 8):
                self.hop(stage, p).wait_send()
            return 0

        lax.fori_loop(0, self.ticks, ended, 0)


def weight_blocks(held, me, target):
    low = lax.rem(me, 8)
    for j in range(8):
        rows = held[pl.ds(pl.multiple_of(flip(low, j) * 32, 32), 32), :].astype(BF16)
        target(j // 4, (j // 2) % 2, j % 2)[...] = rows


def group_at(me, z):
    high = flip(lax.div(me, 8), z)
    return pl.ds(pl.multiple_of(high * 256, 256), 256)


def once(dims):
    return pl.BlockSpec(dims, lambda *_: (0,) * len(dims), pipeline_mode=pl.Buffered(1))


def weight_once(at):
    return pl.BlockSpec((BLOCKS, 32, 1024), lambda *_: (0, at, 0), pipeline_mode=pl.Buffered(1))


class Gather:
    def __init__(self, me, g, shift, local_sem, out_sem, in_sem):
        self.me, self.g, self.shift = me, g, shift
        self.local_sem, self.out_sem, self.in_sem = local_sem, out_sem, in_sem
        self.c, self.x, self.y = [lax.rem(lax.div(me, bit), 2) for bit in (CORE, XBIT, YBIT)]
        self.z = lax.div(me, NEAR)
        self.ticks = g.shape[4] // PAIR

    @staticmethod
    def scratch(ticks):
        return [pltpu.SemaphoreType.DMA((ticks,)), pltpu.SemaphoreType.DMA((8, ticks)), pltpu.SemaphoreType.DMA((8, ticks))]

    def rows(self, p):
        return pl.ds(pl.multiple_of(lax.rem(p + self.shift, self.ticks) * PAIR, PAIR), PAIR)

    def half(self, p, h):
        return pl.ds(pl.multiple_of(lax.rem(p + self.shift, self.ticks) * PAIR + h * HALF, HALF), HALF)

    def mine(self, p):
        return self.g.at[self.z, self.y, self.x, self.c, self.rows(p)]

    def local(self, p, src):
        return pltpu.make_async_copy(src, self.mine(p), self.local_sem.at[p])

    def hop(self, stage, p):
        g, every = self.g, slice(None)
        if stage < 3:
            ref, bits = self.mine(p), (NEAR, FAR, BOTH)[stage]
        elif stage == 3:
            ref, bits = g.at[every, self.y, self.x, self.c, self.half(p, 0)], XBIT
        elif stage == 4:
            ref, bits = g.at[every, self.y, self.x, self.c, self.half(p, 1)], YBIT
        elif stage == 5:
            ref, bits = g.at[every, self.y, every, self.c, self.half(p, 0)], YBIT
        elif stage == 6:
            ref, bits = g.at[every, every, self.x, self.c, self.half(p, 1)], XBIT
        else:
            ref, bits = g.at[every, every, every, self.c, self.rows(p)], CORE
        return remote(ref, ref, self.out_sem.at[stage, p], self.in_sem.at[stage, p], flip(self.me, bits))

    def begin(self, sources):
        for p, src in enumerate(sources):
            self.local(p, src).start()
        greet(self.me)

    def tick(self, t):
        def stage(at):
            return pl.when((t >= at * GATHER_LAG) & (t < self.ticks + at * GATHER_LAG))

        @stage(0)
        def _():
            self.local(t, self.mine(t)).wait()
            for k in (1, 2, 0):
                self.hop(k, t).start()

        @stage(1)
        def _():
            p = t - GATHER_LAG
            for k in range(3):
                self.hop(k, p).wait_recv()
            self.hop(3, p).start()
            self.hop(4, p).start()

        @stage(2)
        def _():
            p = t - 2 * GATHER_LAG
            self.hop(3, p).wait_recv()
            self.hop(5, p).start()
            self.hop(4, p).wait_recv()
            self.hop(6, p).start()

        @stage(3)
        def _():
            p = t - 3 * GATHER_LAG
            self.hop(5, p).wait_recv()
            self.hop(6, p).wait_recv()
            self.hop(7, p).start()

        @stage(4)
        def _():
            self.hop(7, t - 4 * GATHER_LAG).wait_recv()

    def close(self):
        def ended(p, _):
            for stage in range(8):
                self.hop(stage, p).wait_send()
            return 0

        lax.fori_loop(0, self.ticks, ended, 0)


def forward_body(cross_live, self_live, tokens, *refs):
    sources, (inner, outer, memory_in), g = refs[:9], refs[9:12], refs[12]
    outs, held = refs[13:30], refs[30:47]
    weights, vec_rows, memory, load_sem, store_sem = refs[47:52]
    keys, values, q, k, v, mix, summed, first, low, cq, lse, cmix, clse, second_sum, second, second_low, vecs = held
    step = pl.program_id(0)
    me = lax.axis_index("dp").astype(jnp.int32)
    engine = Gather(me, g, 8, *refs[52:])
    count, width = tokens.shape
    pairs = width // 128
    ready = 4 * GATHER_LAG + 1

    def load(at):
        every = slice(None)
        target = vec_rows if at == VEC else weights.at[at if at < VEC else at - 1]
        return pltpu.make_async_copy(g.at[every, every, every, every, engine.rows(at)], target, load_sem.at[at])

    def weight_of(at):
        load(at).wait()
        return weights[at if at < VEC else at - 1].reshape(width, width)

    def load_memory():
        return pltpu.make_async_copy(memory_in, memory, load_sem.at[9])

    def store(*which):
        for at in which:
            pltpu.make_async_copy(held[at], outs[at], store_sem.at[at]).start()

    def on(at):
        return pl.when(step == at)

    @on(0)
    def _():
        load_memory().start()
        parts = [inner.at[:, pl.ds(i, width)] for i in range(0, inner.shape[1], width)]
        parts += [outer.at[pl.ds(i, PAIR)] for i in range(0, outer.shape[0], PAIR)]
        engine.begin(list(sources) + parts)

    tile = 512

    @on(ready)
    def _():
        load_memory().wait()
        factor = weight_of(0)
        for at in range(0, memory.shape[0], tile):
            keys[at : at + tile, :] = nn(memory[at : at + tile, :], factor).astype(BF16)
        store(0)

    @on(ready + 1)
    def _():
        factor = weight_of(1)
        for at in range(0, memory.shape[0], tile):
            values[at : at + tile, :] = nn(memory[at : at + tile, :], factor).astype(BF16)
        store(1)

    for at, rows in ((2, q), (3, k), (4, v)):
        @on(ready + at)
        def _(at=at, rows=rows):
            rows[...] = nn(tokens[...], weight_of(at)).astype(BF16)
            store(at)

    @on(ready + VEC)
    def _():
        load(VEC).wait()
        total = jnp.zeros((16, width), F32)
        for z in range(4):
            for y in range(2):
                for x in range(2):
                    for c in range(2):
                        total = total + vec_rows[z, y, x, c, :16, :].astype(F32)
        vecs[...] = total
        self_attention(self_live[0], q, k, v, mix, lse)
        store(16, 5, 10)

    @on(ready + 6)
    def _():
        total = tokens[...].astype(F32) + nn(mix[...], weight_of(6))
        summed[...] = total
        normal, _ = norm_parts(total)
        rows = normal * vecs[0:1, :] + vecs[1:2, :]
        first[...] = rows
        low[...] = rows.astype(BF16)
        store(6, 7, 8)

    @on(ready + 7)
    def _():
        cq[...] = nn(low[...], weight_of(7)).astype(BF16)
        store(9)

    each = 2
    start = ready + 8

    @pl.when((step >= start) & (step < start + pairs // each))
    def _():
        for part in range(each):
            pair = (step - start) * each + part
            cut = pl.ds(pl.multiple_of(pair * 128, 128), 128)
            cross_body(
                cross_live, cq.at[:, cut], keys.at[:, cut], values.at[:, cut], cmix.at[:, cut], clse.at[pl.ds(pair, 1)]
            )

    @on(start + pairs // each)
    def _():
        second_rows(cmix[...], weight_of(8), first[...], vecs, second_sum, second, second_low)
        store(11, 12, 13, 14, 15)

    engine.tick(step)

    for at in range(9):
        @on(at + 4 * GATHER_LAG)
        def _(at=at):
            load(at).start()

    @on(pl.num_programs(0) - 1)
    def _():
        engine.close()
        for at in range(17):
            pltpu.make_async_copy(held[at], outs[at], store_sem.at[at]).wait()


VEC = 5


def forward_beside(cross_live, self_live, tokens, sources, inner, outer, memory):
    count, width = tokens.shape
    slots = memory.shape[0]
    pairs = width // 128
    rows = PAIR * len(sources) + inner.shape[0] * inner.shape[1] // width + outer.shape[0]
    ticks = rows // PAIR
    low, wide = shape(tokens.shape, BF16), shape(tokens.shape, F32)
    large = shape(memory.shape, BF16)
    parts = [
        large, large, low, low, low, low, wide, wide, low, low, shape((128, count), F32),
        low, shape((pairs, 8, count), F32), wide, wide, low, shape((16, width), F32),
    ]
    scalar = pl.BlockSpec(memory_space=pltpu.SMEM)
    hbm = pl.BlockSpec(memory_space=pl.ANY)
    block = (4, 2, 2, 2)
    out = pl.pallas_call(
        forward_body,
        grid=(ticks + 4 * GATHER_LAG + 1,),
        out_shape=[shape(block + (rows, width), BF16)] + parts,
        in_specs=[scalar, scalar, once(tokens.shape)] + [hbm] * (len(sources) + 3),
        out_specs=[hbm] * (1 + len(parts)),
        scratch_shapes=[pltpu.VMEM(part.shape, part.dtype) for part in parts]
        + [pltpu.VMEM((8,) + block + (PAIR, width), BF16), pltpu.VMEM(block + (PAIR, width), BF16), pltpu.VMEM(memory.shape, BF16)]
        + [pltpu.SemaphoreType.DMA((10,)), pltpu.SemaphoreType.DMA((len(parts),))]
        + Gather.scratch(ticks),
        compiler_params=pltpu.CompilerParams(collective_id=0, has_side_effects=True, vmem_limit_bytes=60 * MIB),
        cost_estimate=pl.CostEstimate(flops=6 * slots * width * width, bytes_accessed=90 * MIB, transcendentals=0),
        name="forward_beside_gather",
    )(cross_live, self_live, tokens, *sources, inner, outer, memory)
    return out[0].reshape(BLOCKS, rows, width), out[1:]


def back_body(
    cross_live, self_live, q, k, v, g, mixture, lse, gss, wcq, first_sum, wo, vecs, sq, sk, sv, smix, slse,
    tokens, wq, wk, wv, second_grads, third_grads, ffn_keep, ffn_send,
    dq_o, dk_o, dv_o, tokens_grad, self_keep, self_send, own, *scratch,
):
    refs, (gfs, gsi, gq, gk, gv, grads, held) = scratch[:8], scratch[8:]
    step = pl.program_id(0)
    me = lax.axis_index("dp").astype(jnp.int32)
    engine = Scatter(me, [(ffn_keep, ffn_send)], refs, own)
    pairs = dq_o.shape[1] // 128
    width = dq_o.shape[1]

    @pl.when(step == 0)
    def _():
        engine.begin()

    @pl.when(step < pairs)
    def _():
        part = dq_o.at[:, pl.ds(pl.multiple_of(step * 128, 128), 128)]
        cross_back_body(cross_live, q, k, v, g, mixture, lse, part, dk_o, dv_o)

    @pl.when(step == pairs)
    def _():
        self_back_body(
            self_live, gss, dq_o, wcq, first_sum, wo, vecs, sq, sk, sv, smix, slse, gfs, gsi, gq, gk, gv, grads.at[pl.ds(0, 8)]
        )
        grads[2:4, :] = second_grads[0:2, :]
        grads[4:6, :] = third_grads[0:2, :]
        grads[8:32, :] = jnp.zeros((24, width), F32)

    for z in range(4):
        @pl.when(step == pairs + 1 + z)
        def _(z=z):
            columns = group_at(me, z)
            for at, (rows, grad) in enumerate([(tokens, gq), (tokens, gk), (tokens, gv), (smix, gsi)]):
                held[...] = tn(rows[:, columns], grad[...])

                def target(y, x, c, at=at):
                    return (self_send if c else self_keep).at[0, y, x, pl.ds(at * 32, 32)]

                weight_blocks(held, me, target)
            low = grads[...].astype(BF16)
            for y in range(2):
                for x in range(2):
                    self_keep[0, y, x, 128:160, :] = low
                    self_send[0, y, x, 128:160, :] = low

    @pl.when(step == pairs + 5)
    def _():
        tokens_grad_body(gfs, gq, gk, gv, wq, wk, wv, tokens_grad)

    engine.tick(step)

    @pl.when(step == pl.num_programs(0) - 1)
    def _():
        engine.close()


def blocks_of(pay):
    return pay.reshape((4, 2, 2) + pay.shape[1:])


def backward_beside(
    cross_live, self_live, q, k, v, g, mixture, lse, gss, stack, first_sum, vecs, sq, sk, sv, smix, slse, tokens,
    second_grads, third_grads, ffn_pay,
):
    count, width = q.shape
    slots = k.shape[0]
    pairs = width // 128
    last = pairs - 1
    ffn_keep, ffn_send = [blocks_of(pay) for pay in ffn_pay]
    ticks = ffn_keep.shape[3] // PAIR
    small = pl.BlockSpec((count, 128), lambda i: (0, jnp.minimum(i, last)))
    large = pl.BlockSpec((slots, 128), lambda i: (0, jnp.minimum(i, last)))
    scalar = pl.BlockSpec(memory_space=pltpu.SMEM)
    hbm = pl.BlockSpec(memory_space=pl.ANY)
    square = once((count, width))
    pay_shape = (4, 2, 2, 160, width)
    pay = pl.BlockSpec((1, 2, 2, 160, width), lambda i: (jnp.clip(i - pairs - 1, 0, 3), 0, 0, 0, 0))
    low = shape(q.shape, BF16)
    dq, dk, dv, tokens_grad, self_keep, self_send, own = pl.pallas_call(
        back_body,
        grid=(max(pairs + 6, ticks + 3 * LAG),),
        out_shape=[low, shape(k.shape, BF16), shape(k.shape, BF16), shape(q.shape, F32), shape(pay_shape, BF16), shape(pay_shape, BF16), shape((ticks * PAIR, width), F32)],
        in_specs=[
            scalar, scalar, small, large, large, small, small,
            pl.BlockSpec((1, 8, count), lambda i: (jnp.minimum(i, last), 0, 0)),
            square, weight_once(15), square, weight_once(14), once(vecs.shape), square, square, square, square, once(slse.shape),
            square, weight_once(10), weight_once(11), weight_once(12), once(second_grads.shape), once(third_grads.shape), hbm, hbm,
        ],
        out_specs=[full(q.shape), large, large, full(q.shape), pay, pay, full((ticks * PAIR, width))],
        scratch_shapes=Scatter.scratch(ticks, width)
        + [pltpu.VMEM(q.shape, F32)] + [pltpu.VMEM(q.shape, BF16)] * 4
        + [pltpu.VMEM((32, width), F32), pltpu.VMEM((256, width), F32)],
        compiler_params=pltpu.CompilerParams(collective_id=1, has_side_effects=True, vmem_limit_bytes=62 * MIB),
        cost_estimate=pl.CostEstimate(flops=60 * count * slots * width, bytes_accessed=80 * MIB, transcendentals=0),
        name="backward_beside_sum",
    )(
        cross_live, self_live, q, k, v, g, mixture, lse, gss, stack, first_sum, stack, vecs, sq, sk, sv, smix, slse,
        tokens, stack, stack, stack, second_grads, third_grads, ffn_keep, ffn_send,
    )
    return dq, dk, dv, tokens_grad, (self_keep, self_send), own


def finish_body(
    memory, dk, dv, first_low, dq, mixture, gci, wk, wv, self_keep, self_send, memory_grad, own, *scratch
):
    refs, (sent, held) = scratch[:8], scratch[8:]
    step = pl.program_id(0)
    me = lax.axis_index("dp").astype(jnp.int32)
    engine = Scatter(me, [(self_keep, self_send)], refs, own)
    loads = engine.loads
    tile = memory_grad.shape[0]

    @pl.when(step == 0)
    def _():
        engine.begin()

    def weights(w, rows, grad, groups):
        for z in groups:
            held[...] = tn(rows[:, group_at(me, z)], grad[...])

            def target(y, x, c, z=z):
                return sent.at[w, z, y, x] if c else engine.keep.at[loads + w, z, y, x]

            weight_blocks(held, me, target)

    for w, rows, grad in ((2, memory, dk), (3, memory, dv)):
        for z in range(4):
            @pl.when(step == (w - 2) * 4 + z + 1)
            def _(w=w, rows=rows, grad=grad, z=z):
                weights(w, rows, grad, (z,))
                if z == 3:
                    engine.swap(loads + w, sent.at[w]).start()

    for w, rows, grad in ((0, first_low, dq), (1, mixture, gci)):
        @pl.when(step == w)
        def _(w=w, rows=rows, grad=grad):
            weights(w, rows, grad, range(4))
            engine.swap(loads + w, sent.at[w]).start()

    @pl.when((step >= FIRST_TILE) & (step < FIRST_TILE + dk.shape[0] // tile))
    def _():
        at = pl.ds(pl.multiple_of((step - FIRST_TILE) * tile, tile), tile)
        memory_grad[...] = nt(dk[at, :], whole(wk)) + nt(dv[at, :], whole(wv))

    engine.tick(step)

    @pl.when(step == pl.num_programs(0) - 1)
    def _():
        engine.close()


def finish(memory, dk, dv, first_low, dq, mixture, gci, stack, self_pay):
    slots, width = memory.shape
    count = dq.shape[0]
    tile = 256
    tiles = slots // tile
    ticks = self_pay[0].shape[3] // PAIR + 4
    hbm = pl.BlockSpec(memory_space=pl.ANY)
    large, square = once(memory.shape), once(dq.shape)
    return pl.pallas_call(
        finish_body,
        grid=(ticks + 3 * LAG,),
        out_shape=[shape(memory.shape, F32), shape((ticks * PAIR, width), F32)],
        in_specs=[large, large, large, square, square, square, square, weight_once(8), weight_once(9), hbm, hbm],
        out_specs=[pl.BlockSpec((tile, width), lambda i: (jnp.clip(i - FIRST_TILE, 0, tiles - 1), 0)), full((ticks * PAIR, width))],
        scratch_shapes=Scatter.scratch(ticks, width)
        + [pltpu.VMEM((4, 4, 2, 2, PAIR, width), BF16), pltpu.VMEM((256, width), F32)],
        compiler_params=pltpu.CompilerParams(collective_id=2, has_side_effects=True, vmem_limit_bytes=62 * MIB),
        cost_estimate=pl.CostEstimate(flops=8 * slots * width * width, bytes_accessed=60 * MIB, transcendentals=0),
        name="finish_beside_sum",
    )(memory, dk, dv, first_low, dq, mixture, gci, stack, stack, *self_pay)


def absolute(keep, send):
    return jnp.stack([keep, send], axis=1).reshape((BLOCKS,) + keep.shape[1:])


def gather(rows):
    return lax.all_gather(rows, "dp", axis=0, tiled=True)


def on_device(
    devices, tokens, memory, target_lengths, memory_lengths, cotangent,
    self_query, self_key, self_value, self_output, first_gain, first_shift,
    cross_query, cross_key, cross_value, cross_output, second_gain, second_shift,
    inner_weight, outer_weight, third_gain, third_shift,
):
    width = tokens.shape[1]
    hidden = inner_weight.shape[1]
    direct = devices == BLOCKS
    squares = [cross_key, cross_value, self_query, self_key, self_value, self_output, cross_query, cross_output]
    vectors = [first_gain, first_shift, second_gain, second_shift, third_gain, third_shift]
    if direct:
        place_of = lax.axis_index("dp").astype(jnp.int32)
        me = place_of.reshape(1)
        own = lax.dynamic_update_slice(jnp.zeros((32, width), BF16), jnp.stack(vectors), (0, place_of * 32))
        stack, parts = forward_beside(
            memory_lengths, target_lengths, tokens, squares[:VEC] + [own] + squares[VEC:], inner_weight, outer_weight, memory
        )
        (keys, values, q, k, v, mixture, first_sum, first_out, first_low, cross_q, lse,
         cross_mixture, cross_lse, second_sum, second, second_low, vecs) = parts
    else:
        me = jnp.zeros((1,), jnp.int32)
        inner_full = gather(inner_weight)
        parts = [inner_full[:, i : i + width].reshape(BLOCKS, 32, width) for i in range(0, hidden, width)]
        parts.append(gather(outer_weight).reshape(BLOCKS, 128, width))
        parts += [gather(w).reshape(BLOCKS, 32, width) for w in squares[:VEC]] + [jnp.zeros((BLOCKS, 32, width), BF16)]
        parts += [gather(w).reshape(BLOCKS, 32, width) for w in squares[VEC:]]
        stack = jnp.concatenate(parts, axis=1)
        vecs = jnp.pad(jnp.stack([gather(v) for v in vectors]), ((0, 10), (0, 0))).astype(F32)
        keys, values = kv_project(memory, stack, 8, 9)
        q, k, v, mixture, first_sum, first_out, first_low, cross_q, lse = self_forward(
            target_lengths, tokens, stack, (10, 11, 12, 14, 15), vecs
        )
        cross_mixture, cross_lse = cross_forward(memory_lengths, cross_q, keys, values)
        second_sum, second, second_low = second_norm(cross_mixture, stack, 16, first_out, vecs)

    act, slope, output_rows, gts, go, third_grads = ffn_forward(second_low, second, stack, cotangent, vecs)
    gi, gss, gci, gcm, second_grads = ffn_backward(go, gts, slope, stack, second_sum, stack, 16, vecs)
    ffn_pay = ffn_weights(me, act, go, second_low, gi)
    if direct:
        dq, dk, dv, tokens_grad, self_pay, ffn_own = backward_beside(
            memory_lengths, target_lengths, cross_q, keys, values, gcm, cross_mixture, cross_lse, gss, stack,
            first_sum, vecs, q, k, v, mixture, lse, tokens, second_grads, third_grads, ffn_pay,
        )
        outer_own = ffn_own[:128]
        inner_own = jnp.concatenate([ffn_own[i : i + 32] for i in range(128, 256, 32)], axis=1)
        memory_grad, owned = finish(memory, dk, dv, first_low, dq, cross_mixture, gci, stack, self_pay)
        self_own = [owned[i : i + 32] for i in range(0, 128, 32)]
        vec_rows = lax.dynamic_slice(owned, (128, me[0] * 32), (6, 32))
        vec_own = [vec_rows[i] for i in range(6)]
        cross_own = [owned[i : i + 32] for i in (160, 224, 256, 192)]
    else:
        dq, dk, dv = cross_backward(memory_lengths, cross_q, keys, values, gcm, cross_mixture, cross_lse)
        cross_pay = square_weights(
            me, [(first_low, dq), (memory, dk), (memory, dv), (cross_mixture, gci)], "cross_weights"
        )
        gfs, gsi, gq, gk, gv, first_grads = self_backward(
            target_lengths, gss, dq, stack, 15, 14, first_sum, vecs, q, k, v, mixture, lse
        )
        self_pay = square_weights(me, [(tokens, gq), (tokens, gk), (tokens, gv), (mixture, gsi)], "self_weights")
        memory_grad = memory_gradient(dk, dv, stack, 8, 9)
        tokens_grad = tokens_gradient(gfs, gq, gk, gv, stack, (10, 11, 12))

        def summed(rows):
            return lax.psum_scatter(rows.astype(F32), "dp", scatter_dimension=0, tiled=True)

        ffn_rows, cross_rows, self_rows = absolute(*ffn_pay), absolute(*cross_pay), absolute(*self_pay)
        outer_own = summed(ffn_rows[:, :128].reshape(-1, width))
        inner_own = summed(
            jnp.concatenate([ffn_rows[:, i : i + 32].reshape(-1, width) for i in range(128, 256, 32)], axis=1)
        )
        cross_own = [summed(cross_rows[:, i : i + 32].reshape(-1, width)) for i in range(0, 128, 32)]
        self_own = [summed(self_rows[:, i : i + 32].reshape(-1, width)) for i in range(0, 128, 32)]
        vec_own = [summed(rows[i]) for rows in (first_grads, second_grads, third_grads) for i in range(2)]

    return (
        output_rows, tokens_grad, memory_grad,
        *self_own, vec_own[0], vec_own[1],
        *cross_own, vec_own[2], vec_own[3],
        inner_own, outer_own, vec_own[4], vec_own[5],
    )


def solution(mesh):
    rows, line = P("dp", None), P("dp")
    block = [rows] * 4 + [line] * 2
    placed = (rows, rows, line, line, rows, *block, *block, rows, rows, line, line)
    return jax.shard_map(
        functools.partial(on_device, mesh.shape["dp"]),
        mesh=mesh,
        in_specs=placed,
        out_specs=(rows, rows, rows, *block, *block, rows, rows, line, line),
        check_vma=False,
    )
```

```python
import functools
import math

import jax
import jax.numpy as jnp
from jax import lax
from jax.experimental import pallas as pl
from jax.experimental.pallas import tpu as pltpu
from jax.sharding import PartitionSpec as P

HEAD = 64
EPS = 1e-05
SCALE = 1.0 / math.sqrt(HEAD)
LOG2E = 1.4426950408889634
BLOCKS = 32
MIB = 1024 * 1024
F32 = jnp.float32
BF16 = jnp.bfloat16
PAIR, HALF = 32, 16
CORE, XBIT, YBIT, NEAR, FAR, BOTH = PARTNERS = (1, 2, 4, 8, 16, 24)
LAG = 1
GATHER_LAG = 1
FIRST_TILE = 7


def nn(a, b):
    return jnp.dot(a, b, preferred_element_type=F32)


def nt(a, b):
    return lax.dot_general(a, b, (((1,), (1,)), ((), ())), preferred_element_type=F32)


def tn(a, b):
    return lax.dot_general(a, b, (((0,), (0,)), ((), ())), preferred_element_type=F32)


def whole(ref):
    return ref[...].reshape(-1, ref.shape[-1])


def call(body, name, out, grid=(), ins=None, outs=None, scratch=(), prefetch=0, limit=56, flops=0, moved=0):
    return pl.pallas_call(
        body,
        out_shape=out,
        grid_spec=pltpu.PrefetchScalarGridSpec(
            num_scalar_prefetch=prefetch,
            grid=grid,
            in_specs=ins,
            out_specs=outs,
            scratch_shapes=scratch,
        ),
        compiler_params=pltpu.CompilerParams(vmem_limit_bytes=limit * MIB),
        cost_estimate=pl.CostEstimate(flops=flops, bytes_accessed=moved, transcendentals=0),
        name=name,
    )


def full(shape):
    return pl.BlockSpec(shape, lambda *_: (0,) * len(shape))


def weight(at):
    return pl.BlockSpec((BLOCKS, 32, 1024), lambda *_: (0, at, 0))


def shape(dims, dtype):
    return jax.ShapeDtypeStruct(dims, dtype)


def norm_parts(summed):
    average = jnp.mean(summed, axis=-1, keepdims=True)
    centred = summed - average
    spread = jnp.mean(centred * centred, axis=-1, keepdims=True)
    scale = lax.rsqrt(spread + EPS)
    return centred * scale, scale


def norm_back(summed, gain, upstream):
    normal, scale = norm_parts(summed)
    grad_gain = jnp.sum(upstream * normal, axis=0, keepdims=True)
    grad_shift = jnp.sum(upstream, axis=0, keepdims=True)
    scaled = upstream * gain
    first = jnp.mean(scaled, axis=-1, keepdims=True)
    second = jnp.mean(scaled * normal, axis=-1, keepdims=True)
    return scale * (scaled - first - normal * second), grad_gain, grad_shift


def lanes(rows):
    return lax.broadcasted_iota(jnp.int32, (rows, 128), 1)


def stack_pair(rows):
    low = lanes(rows.shape[0]) < HEAD
    zero = jnp.zeros_like(rows)
    return jnp.concatenate([jnp.where(low, rows, zero), jnp.where(low, zero, rows)], axis=0)


def unstack_pair(stacked):
    half = stacked.shape[0] // 2
    return jnp.where(lanes(half) < HEAD, stacked[:half], stacked[half:])


def pair_forward(stacked, keys, values, mask):
    scores = nt(stacked, keys)
    if mask is not None:
        scores = mask(scores)
    peak = jnp.max(scores, axis=-1, keepdims=True)
    raised = jnp.exp2((scores - peak) * (SCALE * LOG2E))
    total = jnp.sum(raised, axis=-1, keepdims=True)
    mixed = nn(raised.astype(BF16), values) / total
    return mixed, peak * SCALE + jnp.log(total)


def pair_tile_back(q2, g2, keys, values, totals, inner, mask):
    scores = nt(keys, q2)
    probs = jnp.exp2(scores * (SCALE * LOG2E) - totals)
    if mask is not None:
        probs = mask(probs)
    grad_probs = nt(values, g2)
    grad_scores = (probs * (grad_probs - inner)).astype(BF16)
    grad_values = nn(probs.astype(BF16), g2)
    grad_keys = nn(grad_scores, q2) * SCALE
    grad_queries = tn(keys, grad_scores)
    return grad_queries, grad_keys, grad_values


def pair_inner(mixture, grad):
    product = mixture.astype(F32) * grad.astype(F32)
    half = jnp.where(
        (lax.broadcasted_iota(jnp.int32, (8, 128), 1) // HEAD)
        == lax.broadcasted_iota(jnp.int32, (8, 128), 0),
        1.0,
        0.0,
    ).astype(F32)
    sums = lax.dot_general(
        half, product, (((1,), (1,)), ((), ())),
        preferred_element_type=F32, precision=lax.Precision.HIGHEST,
    )
    return jnp.concatenate([sums[0:1], sums[1:2]], axis=1)


def join_grad_queries(grad):
    count = grad.shape[1] // 2
    joined = jnp.concatenate([grad[:HEAD, :count], grad[HEAD:, count:]], axis=0) * SCALE
    return joined.T.astype(BF16)


def kv_body(memory, wk, wv, keys, values):
    rows = memory[...]
    keys[...] = nn(rows, whole(wk)).astype(BF16)
    values[...] = nn(rows, whole(wv)).astype(BF16)


def kv_project(memory, stack, at_k, at_v):
    count, width = memory.shape
    tile = 512
    spec = pl.BlockSpec((tile, width), lambda i: (i, 0))
    return call(
        kv_body, "cross_kv", [shape(memory.shape, BF16)] * 2, (count // tile,),
        [spec, weight(at_k), weight(at_v)], [spec, spec],
        flops=4 * count * width * width, moved=12 * MIB + 4 * MIB,
    )(memory, stack, stack)


def self_attention(live, q_o, k_o, v_o, mix_o, lse_o):
    count, width = q_o.shape
    at_q = lax.rem(lax.broadcasted_iota(jnp.int32, (2 * count, count), 0), count)
    at_k = lax.broadcasted_iota(jnp.int32, (2 * count, count), 1)
    allowed = (at_k <= at_q) & (at_k < live)
    column = lanes(count)
    totals = jnp.zeros((count, 128), F32)
    for pair in range(width // 128):
        cut = slice(pair * 128, pair * 128 + 128)
        mixed, log_total = pair_forward(
            stack_pair(q_o[:, cut]), k_o[:, cut], v_o[:, cut],
            lambda scores: jnp.where(allowed, scores, -1e30),
        )
        mix_o[:, cut] = unstack_pair(mixed).astype(BF16)
        totals = jnp.where(column == 2 * pair, log_total[:count], totals)
        totals = jnp.where(column == 2 * pair + 1, log_total[count:], totals)
    lse_o[...] = totals.T


def self_body(length, tokens, wq, wk, wv, wo, wcq, vecs, q_o, k_o, v_o, mix_o, sum_o, first_o, low_o, cq_o, lse_o):
    rows = tokens[...]
    count, width = rows.shape
    q_o[...] = nn(rows, whole(wq)).astype(BF16)
    k_o[...] = nn(rows, whole(wk)).astype(BF16)
    v_o[...] = nn(rows, whole(wv)).astype(BF16)
    self_attention(length[0], q_o, k_o, v_o, mix_o, lse_o)
    summed = rows.astype(F32) + nn(mix_o[...], whole(wo))
    sum_o[...] = summed
    normal, _ = norm_parts(summed)
    first = normal * vecs[0:1] + vecs[1:2]
    first_o[...] = first
    low = first.astype(BF16)
    low_o[...] = low
    cq_o[...] = nn(low, whole(wcq)).astype(BF16)


def self_forward(length, tokens, stack, at, vecs):
    count, width = tokens.shape
    low = shape(tokens.shape, BF16)
    wide = shape(tokens.shape, F32)
    spec = full(tokens.shape)
    return call(
        self_body, "self_forward",
        [low, low, low, low, wide, wide, low, low, shape((128, count), F32)], (1,),
        [spec] + [weight(k) for k in at] + [full(vecs.shape)],
        [spec] * 8 + [full((128, count))], prefetch=1,
        flops=10 * count * width * width, moved=16 * MIB,
    )(length, tokens, stack, stack, stack, stack, stack, vecs)


def cross_body(length, q, k, v, mix_o, lse_o):
    count = q.shape[0]
    slots = k.shape[0]
    live = length[0]
    q2 = stack_pair(q[...])
    keys = k[...]
    values = v[...]
    half = slots // 2
    tile = 128
    column = lax.broadcasted_iota(jnp.int32, (tile, slots - half), 1) + half

    def mask(scores):
        upper = jnp.where(column < live, scores[:, half:], -1e30)
        return jnp.concatenate([scores[:, :half], upper], axis=1)

    mixes, logs = [], []
    for at in range(0, 2 * count, tile):
        mixed, log_total = pair_forward(q2[at : at + tile], keys, values, mask)
        mixes.append(mixed)
        logs.append(log_total)
    mix_o[...] = unstack_pair(jnp.concatenate(mixes, axis=0)).astype(BF16)
    logs = jnp.concatenate(logs, axis=0)
    column = lanes(count)
    totals = jnp.where(column == 0, logs[:count], jnp.where(column == 1, logs[count:], 0.0))
    lse_o[0] = totals.T[:8]


def cross_forward(length, q, k, v):
    count, width = q.shape
    slots = k.shape[0]
    pairs = width // 128
    return call(
        cross_body, "cross_forward",
        [shape(q.shape, BF16), shape((pairs, 8, count), F32)], (pairs,),
        [pl.BlockSpec((count, 128), lambda i, _: (0, i))]
        + [pl.BlockSpec((slots, 128), lambda i, _: (0, i))] * 2,
        [pl.BlockSpec((count, 128), lambda i, _: (0, i)), pl.BlockSpec((1, 8, count), lambda i, _: (i, 0, 0))],
        prefetch=1, flops=16 * count * slots * width, moved=10 * MIB,
    )(length, q, k, v)


def second_rows(mixture, wo, first, vecs, sum_o, second_o, low_o):
    summed = first + nn(mixture, wo)
    sum_o[...] = summed
    normal, _ = norm_parts(summed)
    second = normal * vecs[2:3, :] + vecs[3:4, :]
    second_o[...] = second
    low_o[...] = second.astype(BF16)


def second_body(mixture, wo, first, vecs, sum_o, second_o, low_o):
    second_rows(mixture[...], whole(wo), first[...], vecs, sum_o, second_o, low_o)


def second_norm(mixture, stack, at, first, vecs):
    spec = full(mixture.shape)
    return call(
        second_body, "second_norm",
        [shape(mixture.shape, F32), shape(mixture.shape, F32), shape(mixture.shape, BF16)], (1,),
        [spec, weight(at), spec, full(vecs.shape)], [spec] * 3,
        flops=MIB * 512, moved=6 * MIB,
    )(mixture, stack, first, vecs)


def erf(x):
    return lax.erf(x)


def ffn_body(low, second, inner, outer, cot, vecs, act_o, slope_o, out_o, gts_o, go_o, grads_o, total):
    step = pl.program_id(0)
    pre = nn(low[...], whole(inner))
    half = 0.5 * (1.0 + erf(pre * math.sqrt(0.5)))
    active = (pre * half).astype(BF16)
    act_o[...] = active
    slope_o[...] = half + pre * (jnp.exp(-0.5 * pre * pre) * (1.0 / math.sqrt(2.0 * math.pi)))
    part = nn(active, whole(outer))

    @pl.when(step == 0)
    def _():
        total[...] = second[...] + part

    @pl.when(step > 0)
    def _():
        total[...] += part

    @pl.when(step == pl.num_programs(0) - 1)
    def _():
        summed = total[...]
        normal, _ = norm_parts(summed)
        out_o[...] = (normal * vecs[4:5] + vecs[5:6]).astype(BF16)
        grad, gain, shift = norm_back(summed, vecs[4:5], cot[...].astype(F32))
        gts_o[...] = grad
        go_o[...] = grad.astype(BF16)
        grads_o[...] = jnp.concatenate([gain, shift] + [jnp.zeros_like(gain)] * 6, axis=0)


def ffn_forward(low, second, stack, cot, vecs):
    count, width = low.shape
    spec = full(low.shape)
    wide = pl.BlockSpec((count, 1024), lambda i: (0, i))
    return call(
        ffn_body, "ffn_forward",
        [shape((count, 4096), BF16), shape((count, 4096), F32), shape(low.shape, BF16), shape(low.shape, F32), shape(low.shape, BF16), shape((8, width), F32)],
        (4,),
        [spec, spec, pl.BlockSpec((BLOCKS, 32, 1024), lambda i: (0, i, 0)), pl.BlockSpec((8, 128, 1024), lambda i: (i, 1, 0)), spec, full(vecs.shape)],
        [wide, wide, spec, spec, spec, full((8, width))],
        scratch=[pltpu.VMEM(low.shape, F32)],
        flops=16 * count * width * width, moved=24 * MIB,
    )(low, second, stack, stack, cot, vecs)


def ffn_back_body(go, gts, slope, inner, outer, summed, wo, vecs, gi_o, gss_o, gci_o, gcm_o, grads_o, total):
    step = pl.program_id(0)
    grad = nt(go[...], whole(outer))
    low = (grad * slope[...]).astype(BF16)
    gi_o[...] = low
    part = nt(low, whole(inner))

    @pl.when(step == 0)
    def _():
        total[...] = gts[...] + part

    @pl.when(step > 0)
    def _():
        total[...] += part

    @pl.when(step == pl.num_programs(0) - 1)
    def _():
        grad, gain, shift = norm_back(summed[...], vecs[2:3], total[...])
        gss_o[...] = grad
        low = grad.astype(BF16)
        gci_o[...] = low
        gcm_o[...] = nt(low, whole(wo)).astype(BF16)
        grads_o[...] = jnp.concatenate([gain, shift] + [jnp.zeros_like(gain)] * 6, axis=0)


def ffn_backward(go, gts, slope, stack, summed, squares, at, vecs):
    count, width = go.shape
    spec = full(go.shape)
    wide = pl.BlockSpec((count, 1024), lambda i: (0, i))
    low = shape(go.shape, BF16)
    return call(
        ffn_back_body, "ffn_backward",
        [shape((count, 4096), BF16), shape(go.shape, F32), low, low, shape((8, width), F32)],
        (4,),
        [spec, spec, wide, pl.BlockSpec((BLOCKS, 32, 1024), lambda i: (0, i, 0)), pl.BlockSpec((8, 128, 1024), lambda i: (i, 1, 0)), spec, weight(at), full(vecs.shape)],
        [wide, spec, spec, spec, full((8, width))],
        scratch=[pltpu.VMEM(go.shape, F32)],
        flops=18 * count * width * width, moved=26 * MIB,
    )(go, gts, slope, stack, stack, summed, squares, vecs)


def cross_back_body(length, q, k, v, g, mixture, lse, dq_o, dk_o, dv_o):
    live = length[0]
    slots = k.shape[0]
    count = q.shape[0]
    q2 = stack_pair(q[...])
    g2 = stack_pair(g[...])
    totals = jnp.concatenate([lse[0, 0:1], lse[0, 1:2]], axis=1) * LOG2E
    inner = pair_inner(mixture[...], g[...])
    tile = 256
    grad_q = jnp.zeros((128, 2 * count), F32)
    for at in range(0, slots, tile):
        mask = None
        if at + tile > slots // 2:
            row = lax.broadcasted_iota(jnp.int32, (tile, 2 * count), 0) + at

            def mask(probs, row=row):
                return jnp.where(row < live, probs, 0.0)

        cut = slice(at, at + tile)
        dq, dk, dv = pair_tile_back(q2, g2, k[cut], v[cut], totals, inner, mask)
        grad_q = grad_q + dq
        dk_o[cut] = dk.astype(BF16)
        dv_o[cut] = dv.astype(BF16)
    dq_o[...] = join_grad_queries(grad_q)


def cross_backward(length, q, k, v, g, mixture, lse):
    count, width = q.shape
    slots = k.shape[0]
    pairs = width // 128
    small = pl.BlockSpec((count, 128), lambda i, _: (0, i))
    large = pl.BlockSpec((slots, 128), lambda i, _: (0, i))
    return call(
        cross_back_body, "cross_backward",
        [shape(q.shape, BF16), shape(k.shape, BF16), shape(k.shape, BF16)], (pairs,),
        [small, large, large, small, small, pl.BlockSpec((1, 8, count), lambda i, _: (i, 0, 0))],
        [small, large, large], prefetch=1,
        flops=40 * count * slots * width, moved=18 * MIB,
    )(length, q, k, v, g, mixture, lse)


def memory_grad_body(dk, dv, wk, wv, out):
    out[...] = nt(dk[...], whole(wk)) + nt(dv[...], whole(wv))


def memory_gradient(dk, dv, stack, at_k, at_v):
    count, width = dk.shape
    tile = 512
    spec = pl.BlockSpec((tile, width), lambda i: (i, 0))
    return call(
        memory_grad_body, "memory_grad", shape(dk.shape, F32), (count // tile,),
        [spec, spec, weight(at_k), weight(at_v)], spec,
        flops=4 * count * width * width, moved=20 * MIB,
    )(dk, dv, stack, stack)


def self_back_body(length, gss, dcq, wcq, summed, wo, vecs, q, k, v, mixture, lse, gfs_o, gsi_o, gq_o, gk_o, gv_o, grads_o):
    live = length[0]
    count, width = gss.shape
    upstream = gss[...] + nt(dcq[...], whole(wcq))
    grad, gain, shift = norm_back(summed[...], vecs[0:1], upstream)
    gfs_o[...] = grad
    grads_o[...] = jnp.concatenate([gain, shift] + [jnp.zeros_like(gain)] * 6, axis=0)
    low = grad.astype(BF16)
    gsi_o[...] = low
    mix_grad = nt(low, whole(wo)).astype(BF16)
    at_k = lax.broadcasted_iota(jnp.int32, (count, 2 * count), 0)
    at_q = lax.rem(lax.broadcasted_iota(jnp.int32, (count, 2 * count), 1), count)
    allowed = (at_k <= at_q) & (at_k < live)
    for pair in range(width // 128):
        cut = slice(pair * 128, pair * 128 + 128)
        g = mix_grad[:, cut]
        totals = jnp.concatenate([lse[2 * pair : 2 * pair + 1], lse[2 * pair + 1 : 2 * pair + 2]], axis=1) * LOG2E
        scores_back = pair_tile_back(
            stack_pair(q[:, cut]), stack_pair(g), k[:, cut], v[:, cut], totals,
            pair_inner(mixture[:, cut], g),
            lambda probs: jnp.where(allowed, probs, 0.0),
        )
        dq, dk, dv = scores_back
        gq_o[:, cut] = join_grad_queries(dq)
        gk_o[:, cut] = dk.astype(BF16)
        gv_o[:, cut] = dv.astype(BF16)


def self_backward(length, gss, dcq, stack, at_cq, at_o, summed, vecs, q, k, v, mixture, lse):
    count, width = q.shape
    spec = full(q.shape)
    low = shape(q.shape, BF16)
    return call(
        self_back_body, "self_backward",
        [shape(q.shape, F32), low, low, low, low, shape((8, width), F32)], (1,),
        [spec, spec, weight(at_cq), spec, weight(at_o), full(vecs.shape), spec, spec, spec, spec, full(lse.shape)],
        [spec] * 5 + [full((8, width))], prefetch=1,
        flops=8 * count * width * width, moved=12 * MIB,
    )(length, gss, dcq, stack, summed, stack, vecs, q, k, v, mixture, lse)


def tokens_grad_body(gfs, gq, gk, gv, wq, wk, wv, out):
    out[...] = gfs[...] + nt(gq[...], whole(wq)) + nt(gk[...], whole(wk)) + nt(gv[...], whole(wv))


def tokens_gradient(gfs, gq, gk, gv, stack, at):
    spec = full(gfs.shape)
    return call(
        tokens_grad_body, "tokens_grad", shape(gfs.shape, F32), (1,),
        [spec] * 4 + [weight(k) for k in at], spec,
        flops=6 * MIB * 256, moved=10 * MIB,
    )(gfs, gq, gk, gv, stack, stack, stack)


def place(keep, send, at, size, pieces, me):
    low = lax.rem(me, 8)
    for j in range(8):
        rows = pieces(lax.bitwise_xor(low, j))
        target = send if j % 2 else keep
        target[j // 2, at : at + size, :] = rows.astype(BF16)


def group_of(step, me):
    return lax.bitwise_xor(step, lax.div(me[0], 8))


def payload(rows, width):
    out = [shape((16, rows, width), BF16)] * 2
    spec = [pl.BlockSpec((4, rows, width), lambda i, _: (i, 0, 0))] * 2
    return out, spec


def ffn_weights_body(me, act, go, low, gi, keep, send, held):
    step = pl.program_id(0)

    @pl.when(step < 4)
    def _():
        held[...] = tn(act[...], go[...])
        place(keep, send, 0, 128, lambda d: held[pl.ds(pl.multiple_of(d * 128, 128), 128), :], me[0])

    @pl.when(step >= 4)
    def _():
        for part in range(4):
            held[:256, :] = tn(low[...], gi[:, part * 1024 : part * 1024 + 1024])
            place(keep, send, part * 32, 32, lambda d: held[pl.ds(pl.multiple_of(d * 32, 32), 32), :], me[0])


def ffn_weights(me, act, go, low, gi):
    count, width = go.shape
    spec = pl.BlockSpec((4, 128, width), lambda i, me: (lax.rem(i, 4), lax.div(i, 4), 0))
    return call(
        ffn_weights_body, "ffn_weights", [shape((16, 256, width), BF16)] * 2, (8,),
        [
            pl.BlockSpec((count, 1024), lambda i, me: (0, group_of(jnp.minimum(i, 3), me))),
            full(go.shape),
            pl.BlockSpec((count, 256), lambda i, me: (0, group_of(jnp.maximum(i - 4, 0), me))),
            full(gi.shape),
        ],
        [spec, spec], [pltpu.VMEM((1024, width), F32)], 1,
        flops=16 * count * width * width, moved=22 * MIB,
    )(me, act, go, low, gi)


def square_body(me, *refs):
    count = (len(refs) - 3) // 2
    keep, send, held = refs[-3:]
    for at in range(count):
        held[...] = tn(refs[2 * at][...], refs[2 * at + 1][...])
        place(keep, send, at * 32, 32, lambda d: held[pl.ds(pl.multiple_of(d * 32, 32), 32), :], me[0])


def square_weights(me, pairs, name):
    width = pairs[0][0].shape[1]
    out, spec = payload(128, width)
    ins, operands, flops = [], [], 0
    for rows, grads in pairs:
        ins.append(pl.BlockSpec((rows.shape[0], 256), lambda i, me: (0, group_of(i, me))))
        ins.append(full(grads.shape))
        operands += [rows, grads]
        flops += 2 * rows.shape[0] * width * width
    return call(
        square_body, name, out, (4,), ins, spec,
        [pltpu.VMEM((256, width), F32)], 1, flops=flops, moved=20 * MIB,
    )(me, *operands)


def flip(me, bits):
    for bit in (1, 2, 4, 8, 16):
        if bits & bit:
            me = me + bit - 2 * bit * lax.rem(lax.div(me, bit), 2)
    return me


def remote(src, dst, out_sem, in_sem, to):
    return pltpu.make_async_remote_copy(
        src_ref=src, dst_ref=dst, send_sem=out_sem, recv_sem=in_sem,
        device_id=(to,), device_id_type=pl.DeviceIdType.MESH,
    )


def greet(me):
    barrier = pltpu.get_barrier_semaphore()
    for bit in PARTNERS:
        pl.semaphore_signal(barrier, inc=1, device_id=(flip(me, bit),), device_id_type=pl.DeviceIdType.MESH)
    pl.semaphore_wait(barrier, len(PARTNERS))


class Scatter:
    def __init__(self, me, pays, refs, out):
        self.me, self.pays, self.out = me, pays, out
        (self.keep, self.came0, self.came1, self.came2, self.came3,
         self.load_sem, self.out_sem, self.in_sem) = refs
        self.ticks = self.keep.shape[0]
        self.loads = sum(kept.shape[3] for kept, _ in pays) // PAIR

    @staticmethod
    def scratch(ticks, width):
        def held(*dims):
            return pltpu.VMEM((ticks,) + dims + (width,), BF16)

        return [
            held(4, 2, 2, PAIR), held(4, 2, 2, PAIR), held(2, 4, 2, HALF), held(2, 4, HALF), held(3, PAIR),
            pltpu.SemaphoreType.DMA((ticks,)), pltpu.SemaphoreType.DMA((8, ticks)), pltpu.SemaphoreType.DMA((8, ticks)),
        ]

    def link(self, stage, p, src, dst, bit):
        return remote(src, dst, self.out_sem.at[stage, p], self.in_sem.at[stage, p], flip(self.me, bit))

    def load(self, p, kept, at):
        return pltpu.make_async_copy(kept.at[:, :, :, pl.ds(at, PAIR)], self.keep.at[p], self.load_sem.at[p])

    def swap(self, p, sent):
        return self.link(0, p, sent, self.came0.at[p], CORE)

    def hop(self, stage, p):
        keep, up, down = self.keep, pl.ds(0, HALF), pl.ds(HALF, HALF)
        if stage == 1:
            return self.link(1, p, keep.at[p, :, :, 1, up], self.came1.at[p, 0], XBIT)
        if stage == 2:
            return self.link(2, p, keep.at[p, :, 1, :, down], self.came1.at[p, 1], YBIT)
        if stage == 3:
            return self.link(3, p, keep.at[p, :, 1, 0, up], self.came2.at[p, 0], YBIT)
        if stage == 4:
            return self.link(4, p, keep.at[p, :, 0, 1, down], self.came2.at[p, 1], XBIT)
        z = stage - 4
        return self.link(stage, p, keep.at[p, z, 0, 0], self.came3.at[p, z - 1], (NEAR, FAR, BOTH)[z - 1])

    def begin(self):
        greet(self.me)
        p = 0
        for kept, sent in self.pays:
            for at in range(0, kept.shape[3], PAIR):
                self.load(p, kept, at).start()
                self.swap(p, sent.at[:, :, :, pl.ds(at, PAIR)]).start()
                p += 1

    def total(self, p, z, y, x, h, depth):
        cut = slice(h * HALF, h * HALF + HALF)
        sum_ = self.keep[p, z, y, x, cut, :].astype(F32) + self.came0[p, z, y, x, cut, :].astype(F32)
        if depth > 1:
            sum_ = sum_ + self.came1[p, h, z, y if h == 0 else x].astype(F32)
        if depth > 2:
            sum_ = sum_ + self.came2[p, h, z].astype(F32)
        if depth > 3:
            for other in range(3):
                sum_ = sum_ + self.came3[p, other, cut, :].astype(F32)
        return sum_

    def sums(self, p, blocks, h, depth):
        for z, y, x in blocks:
            self.keep[p, z, y, x, h * HALF : h * HALF + HALF, :] = self.total(p, z, y, x, h, depth).astype(BF16)

    def tick(self, t):
        ticks = self.ticks

        def stage(at):
            return pl.when((t >= at * LAG) & (t < ticks + at * LAG))

        if self.pays:
            @pl.when((t >= 0) & (t < self.loads))
            def _():
                self.load(t, self.pays[0][0], 0).wait()

        @stage(0)
        def _():
            self.swap(t, self.came0.at[t]).wait_recv()
            self.sums(t, [(z, y, 1) for z in range(4) for y in range(2)], 0, 1)
            self.hop(1, t).start()
            self.sums(t, [(z, 1, x) for z in range(4) for x in range(2)], 1, 1)
            self.hop(2, t).start()

        @stage(1)
        def _():
            p = t - 1 * LAG
            self.hop(1, p).wait_recv()
            self.sums(p, [(z, 1, 0) for z in range(4)], 0, 2)
            self.hop(3, p).start()
            self.hop(2, p).wait_recv()
            self.sums(p, [(z, 0, 1) for z in range(4)], 1, 2)
            self.hop(4, p).start()

        @stage(2)
        def _():
            p = t - 2 * LAG
            self.hop(3, p).wait_recv()
            self.hop(4, p).wait_recv()
            for z in (2, 3, 1):
                for h in range(2):
                    self.sums(p, [(z, 0, 0)], h, 3)
                self.hop(4 + z, p).start()

        @stage(3)
        def _():
            p = t - 3 * LAG
            for z in (1, 2, 3):
                self.hop(4 + z, p).wait_recv()
            for h in range(2):
                at = pl.ds(pl.multiple_of(p * PAIR + h * HALF, HALF), HALF)
                self.out[at, :] = self.total(p, 0, 0, 0, h, 4)

    def close(self, swapped=0):
        def swap_ended(p, _):
            self.swap(p, self.came0.at[p]).wait_send()
            return 0

        def ended(p, _):
            for stage in range(1, 8):
                self.hop(stage, p).wait_send()
            return 0

        lax.fori_loop(swapped, self.ticks, swap_ended, 0)
        lax.fori_loop(0, self.ticks, ended, 0)


def weight_blocks(held, me, target):
    low = lax.rem(me, 8)
    for j in range(8):
        rows = held[pl.ds(pl.multiple_of(flip(low, j) * 32, 32), 32), :].astype(BF16)
        target(j // 4, (j // 2) % 2, j % 2)[...] = rows


def group_at(me, z):
    high = flip(lax.div(me, 8), z)
    return pl.ds(pl.multiple_of(high * 256, 256), 256)


def once(dims):
    return pl.BlockSpec(dims, lambda *_: (0,) * len(dims), pipeline_mode=pl.Buffered(1))


def weight_once(at):
    return pl.BlockSpec((BLOCKS, 32, 1024), lambda *_: (0, at, 0), pipeline_mode=pl.Buffered(1))


class Gather:
    def __init__(self, me, g, shift, local_sem, out_sem, in_sem):
        self.me, self.g, self.shift = me, g, shift
        self.local_sem, self.out_sem, self.in_sem = local_sem, out_sem, in_sem
        self.c, self.x, self.y = [lax.rem(lax.div(me, bit), 2) for bit in (CORE, XBIT, YBIT)]
        self.z = lax.div(me, NEAR)
        self.ticks = g.shape[4] // PAIR

    @staticmethod
    def scratch(ticks):
        return [pltpu.SemaphoreType.DMA((ticks,)), pltpu.SemaphoreType.DMA((8, ticks)), pltpu.SemaphoreType.DMA((8, ticks))]

    def rows(self, p):
        return pl.ds(pl.multiple_of(lax.rem(p + self.shift, self.ticks) * PAIR, PAIR), PAIR)

    def half(self, p, h):
        return pl.ds(pl.multiple_of(lax.rem(p + self.shift, self.ticks) * PAIR + h * HALF, HALF), HALF)

    def mine(self, p):
        return self.g.at[self.z, self.y, self.x, self.c, self.rows(p)]

    def local(self, p, src):
        return pltpu.make_async_copy(src, self.mine(p), self.local_sem.at[p])

    def hop(self, stage, p):
        g, every = self.g, slice(None)
        if stage < 3:
            ref, bits = self.mine(p), (NEAR, FAR, BOTH)[stage]
        elif stage == 3:
            ref, bits = g.at[every, self.y, self.x, self.c, self.half(p, 0)], XBIT
        elif stage == 4:
            ref, bits = g.at[every, self.y, self.x, self.c, self.half(p, 1)], YBIT
        elif stage == 5:
            ref, bits = g.at[every, self.y, every, self.c, self.half(p, 0)], YBIT
        elif stage == 6:
            ref, bits = g.at[every, every, self.x, self.c, self.half(p, 1)], XBIT
        else:
            ref, bits = g.at[every, every, every, self.c, self.rows(p)], CORE
        return remote(ref, ref, self.out_sem.at[stage, p], self.in_sem.at[stage, p], flip(self.me, bits))

    def begin(self, sources):
        for p, src in enumerate(sources):
            self.local(p, src).start()
        greet(self.me)

    def tick(self, t):
        def stage(at):
            return pl.when((t >= at * GATHER_LAG) & (t < self.ticks + at * GATHER_LAG))

        @stage(0)
        def _():
            self.local(t, self.mine(t)).wait()
            for k in (1, 2, 0):
                self.hop(k, t).start()

        @stage(1)
        def _():
            p = t - GATHER_LAG
            for k in range(3):
                self.hop(k, p).wait_recv()
            self.hop(3, p).start()
            self.hop(4, p).start()

        @stage(2)
        def _():
            p = t - 2 * GATHER_LAG
            self.hop(3, p).wait_recv()
            self.hop(5, p).start()
            self.hop(4, p).wait_recv()
            self.hop(6, p).start()

        @stage(3)
        def _():
            p = t - 3 * GATHER_LAG
            self.hop(5, p).wait_recv()
            self.hop(6, p).wait_recv()
            self.hop(7, p).start()

        @stage(4)
        def _():
            self.hop(7, t - 4 * GATHER_LAG).wait_recv()

    def close(self):
        def ended(p, _):
            for stage in range(8):
                self.hop(stage, p).wait_send()
            return 0

        lax.fori_loop(0, self.ticks, ended, 0)


def forward_body(cross_live, self_live, tokens, *refs):
    sources, (inner, outer, memory_in), g = refs[:9], refs[9:12], refs[12]
    outs, held = refs[13:30], refs[30:47]
    weights, vec_rows, memory, load_sem, store_sem = refs[47:52]
    keys, values, q, k, v, mix, summed, first, low, cq, lse, cmix, clse, second_sum, second, second_low, vecs = held
    step = pl.program_id(0)
    me = lax.axis_index("dp").astype(jnp.int32)
    engine = Gather(me, g, 8, *refs[52:])
    count, width = tokens.shape
    pairs = width // 128
    ready = 4 * GATHER_LAG + 1

    def load(at):
        every = slice(None)
        target = vec_rows if at == VEC else weights.at[at if at < VEC else at - 1]
        return pltpu.make_async_copy(g.at[every, every, every, every, engine.rows(at)], target, load_sem.at[at])

    def weight_of(at):
        load(at).wait()
        return weights[at if at < VEC else at - 1].reshape(width, width)

    def load_memory():
        return pltpu.make_async_copy(memory_in, memory, load_sem.at[9])

    def store(*which):
        for at in which:
            pltpu.make_async_copy(held[at], outs[at], store_sem.at[at]).start()

    def on(at):
        return pl.when(step == at)

    @on(0)
    def _():
        load_memory().start()
        parts = [inner.at[:, pl.ds(i, width)] for i in range(0, inner.shape[1], width)]
        parts += [outer.at[pl.ds(i, PAIR)] for i in range(0, outer.shape[0], PAIR)]
        engine.begin(list(sources) + parts)

    tile = 512

    @on(ready)
    def _():
        load_memory().wait()
        factor = weight_of(0)
        for at in range(0, memory.shape[0], tile):
            keys[at : at + tile, :] = nn(memory[at : at + tile, :], factor).astype(BF16)
        store(0)

    @on(ready + 1)
    def _():
        factor = weight_of(1)
        for at in range(0, memory.shape[0], tile):
            values[at : at + tile, :] = nn(memory[at : at + tile, :], factor).astype(BF16)
        store(1)

    for at, rows in ((2, q), (3, k), (4, v)):
        @on(ready + at)
        def _(at=at, rows=rows):
            rows[...] = nn(tokens[...], weight_of(at)).astype(BF16)
            store(at)

    @on(ready + VEC)
    def _():
        load(VEC).wait()
        total = jnp.zeros((16, width), F32)
        for z in range(4):
            for y in range(2):
                for x in range(2):
                    for c in range(2):
                        total = total + vec_rows[z, y, x, c, :16, :].astype(F32)
        vecs[...] = total
        self_attention(self_live[0], q, k, v, mix, lse)
        store(16, 5, 10)

    @on(ready + 6)
    def _():
        total = tokens[...].astype(F32) + nn(mix[...], weight_of(6))
        summed[...] = total
        normal, _ = norm_parts(total)
        rows = normal * vecs[0:1, :] + vecs[1:2, :]
        first[...] = rows
        low[...] = rows.astype(BF16)
        store(6, 7, 8)

    @on(ready + 7)
    def _():
        cq[...] = nn(low[...], weight_of(7)).astype(BF16)
        store(9)

    each = 2
    start = ready + 8

    @pl.when((step >= start) & (step < start + pairs // each))
    def _():
        for part in range(each):
            pair = (step - start) * each + part
            cut = pl.ds(pl.multiple_of(pair * 128, 128), 128)
            cross_body(
                cross_live, cq.at[:, cut], keys.at[:, cut], values.at[:, cut], cmix.at[:, cut], clse.at[pl.ds(pair, 1)]
            )

    @on(start + pairs // each)
    def _():
        second_rows(cmix[...], weight_of(8), first[...], vecs, second_sum, second, second_low)
        store(11, 12, 13, 14, 15)

    engine.tick(step)

    for at in range(9):
        @on(at + 4 * GATHER_LAG)
        def _(at=at):
            load(at).start()

    @on(pl.num_programs(0) - 1)
    def _():
        engine.close()
        for at in range(17):
            pltpu.make_async_copy(held[at], outs[at], store_sem.at[at]).wait()


VEC = 5


def forward_beside(cross_live, self_live, tokens, sources, inner, outer, memory):
    count, width = tokens.shape
    slots = memory.shape[0]
    pairs = width // 128
    rows = PAIR * len(sources) + inner.shape[0] * inner.shape[1] // width + outer.shape[0]
    ticks = rows // PAIR
    low, wide = shape(tokens.shape, BF16), shape(tokens.shape, F32)
    large = shape(memory.shape, BF16)
    parts = [
        large, large, low, low, low, low, wide, wide, low, low, shape((128, count), F32),
        low, shape((pairs, 8, count), F32), wide, wide, low, shape((16, width), F32),
    ]
    scalar = pl.BlockSpec(memory_space=pltpu.SMEM)
    hbm = pl.BlockSpec(memory_space=pl.ANY)
    block = (4, 2, 2, 2)
    out = pl.pallas_call(
        forward_body,
        grid=(ticks + 4 * GATHER_LAG + 1,),
        out_shape=[shape(block + (rows, width), BF16)] + parts,
        in_specs=[scalar, scalar, once(tokens.shape)] + [hbm] * (len(sources) + 3),
        out_specs=[hbm] * (1 + len(parts)),
        scratch_shapes=[pltpu.VMEM(part.shape, part.dtype) for part in parts]
        + [pltpu.VMEM((8,) + block + (PAIR, width), BF16), pltpu.VMEM(block + (PAIR, width), BF16), pltpu.VMEM(memory.shape, BF16)]
        + [pltpu.SemaphoreType.DMA((10,)), pltpu.SemaphoreType.DMA((len(parts),))]
        + Gather.scratch(ticks),
        compiler_params=pltpu.CompilerParams(collective_id=0, has_side_effects=True, vmem_limit_bytes=60 * MIB),
        cost_estimate=pl.CostEstimate(flops=6 * slots * width * width, bytes_accessed=90 * MIB, transcendentals=0),
        name="forward_beside_gather",
    )(cross_live, self_live, tokens, *sources, inner, outer, memory)
    return out[0].reshape(BLOCKS, rows, width), out[1:]


def blocks_of(pay):
    return pay.reshape((4, 2, 2) + pay.shape[1:])


def back_body(
    cross_live, self_live, q, k, v, mixture, lse, vecs, slse, third_grads,
    act_in, go_in, low_in, slope_in, gts_in, second_in, sum_in, sq_in, sk_in, sv_in, smix_in, tokens_in, stack,
    dk_o, dv_o, own, dq_o, gci_o, tokens_grad, self_keep, self_send, *scratch,
):
    refs, scratch = scratch[:8], scratch[8:]
    sent, weights, slopes, hidden, gss, second_sum, first_sum, gfs = scratch[:8]
    go, low, gci, gcm, dq, sq, sk, sv, smix, tokens, gsi, gq, gk, gv = scratch[8:22]
    grads, held, staged, load_sem, store_sem = scratch[22:]
    step = pl.program_id(0)
    me = lax.axis_index("dp").astype(jnp.int32)
    engine = Scatter(me, [], refs, own)
    width = dq.shape[1]
    pairs = width // 128
    first_pair = 4
    after = first_pair + pairs

    def load(at, src, dst):
        return pltpu.make_async_copy(src, dst, load_sem.at[at])

    def store(at, src, dst):
        return pltpu.make_async_copy(src, dst, store_sem.at[at])

    act_load, go_load = load(0, act_in, hidden), load(1, go_in, go)
    ffn_loads = [load(2, low_in, low), load(3, gts_in, gss), load(4, second_in, second_sum)]
    self_loads = [
        load(5 + at, src, dst)
        for at, (src, dst) in enumerate(
            [(sum_in, first_sum), (sq_in, sq), (sk_in, sk), (sv_in, sv), (smix_in, smix), (tokens_in, tokens)]
        )
    ]

    def load_slope(part):
        return load(11 + part % 2, slope_in.at[:, pl.ds(part * width, width)], slopes.at[part % 2])

    def load_outer(part):
        return load(13, stack.at[pl.ds(8 * part, 8), pl.ds(128, 128)], weights.at[0].reshape(8, 128, width))

    def load_square(at, slot):
        return load(13 + slot, stack.at[:, pl.ds(at * 32, 32)], weights.at[slot])

    def on(at):
        return pl.when(step == at)

    def swaps(chunks):
        return [engine.swap(p, sent.at[p % 4]) for p in chunks]

    @on(0)
    def _():
        act_load.start()
        go_load.start()
        load_outer(0).start()
        load_square(0, 1).start()
        for part in range(2):
            load_slope(part).start()
        for copy in ffn_loads + self_loads:
            copy.start()
        greet(me)
        act_load.wait()
        go_load.wait()
        for z in range(4):
            group = flip(lax.div(me, 8), z)
            for part in range(4):
                columns = pl.ds(pl.multiple_of(group * 1024 + part * 256, 256), 256)
                held[pl.ds(part * 256, 256), :] = tn(hidden[:, columns], go[...]).astype(BF16)
            for j in range(8):
                row = pl.multiple_of(flip(lax.rem(me, 8), j) * 128, 128)
                for p in range(4):
                    rows = held[pl.ds(row + p * 32, 32), :]
                    target = sent.at[p, z, j // 4, (j // 2) % 2] if j % 2 else engine.keep.at[p, z, j // 4, (j // 2) % 2]
                    target[...] = rows
        for copy in swaps(range(4)):
            copy.start()

    for at in (1, 2):
        @on(at)
        def _(at=at):
            if at == 1:
                for copy in ffn_loads:
                    copy.wait()
            for part in (2 * at - 2, 2 * at - 1):
                load_outer(part).wait()
                grad = nt(go[...], whole(weights.at[0]))
                if part < 3:
                    load_outer(part + 1).start()
                else:
                    load_square(16, 0).start()
                load_slope(part).wait()
                rows = (grad * slopes[part % 2]).astype(BF16)
                if part < 2:
                    load_slope(part + 2).start()
                hidden[:, part * width : part * width + width] = rows
                load_square(part, 1).wait()
                gss[...] += nt(rows, whole(weights.at[1]))
                load_square(part + 1 if part < 3 else 15, 1).start()
            if at == 2:
                grad, gain, shift = norm_back(second_sum[...], vecs[2:3, :], gss[...])
                gss[...] = grad
                rows = grad.astype(BF16)
                gci[...] = rows
                load_square(16, 0).wait()
                gcm[...] = nt(rows, whole(weights.at[0])).astype(BF16)
                load_square(14, 0).start()
                grads[2:3, :] = gain
                grads[3:4, :] = shift
                grads[4:6, :] = third_grads[0:2, :]
                grads[8:32, :] = jnp.zeros((24, width), F32)
                store(0, gci, gci_o).start()

    @on(3)
    def _():
        for copy in swaps(range(4)):
            copy.wait_send()
        for part in range(4):
            for z in range(4):
                held[:256, :] = tn(low[:, group_at(me, z)], hidden[:, part * width : part * width + width]).astype(BF16)

                def target(y, x, c, z=z, part=part):
                    return sent.at[part, z, y, x] if c else engine.keep.at[4 + part, z, y, x]

                weight_blocks(held, me, target)
        for copy in swaps(range(4, 8)):
            copy.start()

    @pl.when((step >= first_pair) & (step < after))
    def _():
        cut = pl.ds(pl.multiple_of((step - first_pair) * 128, 128), 128)
        cross_back_body(cross_live, q, k, v, gcm.at[:, cut], mixture, lse, dq.at[:, cut], dk_o, dv_o)

    @on(after)
    def _():
        store(1, dq, dq_o).start()
        for copy in self_loads:
            copy.wait()
        load_square(15, 1).wait()
        load_square(14, 0).wait()
        self_back_body(
            self_live, gss, dq, weights.at[1], first_sum, weights.at[0], vecs, sq, sk, sv, smix, slse,
            gfs, gsi, gq, gk, gv, second_sum.at[pl.ds(0, 8)],
        )
        grads[0:2, :] = second_sum[0:2, :]
        load_square(10, 0).start()
        load_square(11, 1).start()

    def stores(z):
        return [store(2 + 2 * (z % 2) + c, staged.at[z % 2, c], (self_send if c else self_keep).at[z]) for c in range(2)]

    for z in range(4):
        @on(after + 1 + z // 2)
        def _(z=z):
            if z >= 2:
                for copy in stores(z - 2):
                    copy.wait()
            columns = group_at(me, z)
            for at, (rows, grad) in enumerate([(tokens, gq), (tokens, gk), (tokens, gv), (smix, gsi)]):
                held[:256, :] = tn(rows[:, columns], grad[...]).astype(BF16)

                def target(y, x, c, at=at):
                    return staged.at[z % 2, c, y, x, pl.ds(at * 32, 32)]

                weight_blocks(held, me, target)
            rows = grads[...].astype(BF16)
            for y in range(2):
                for x in range(2):
                    for c in range(2):
                        staged[z % 2, c, y, x, 128:160, :] = rows
            for copy in stores(z):
                copy.start()
            if z == 0:
                load_square(10, 0).wait()
                gfs[...] += nt(gq[...], whole(weights.at[0]))
                load_square(12, 0).start()
            if z == 1:
                load_square(11, 1).wait()
                gfs[...] += nt(gk[...], whole(weights.at[1]))
            if z == 2:
                load_square(12, 0).wait()
                gfs[...] += nt(gv[...], whole(weights.at[0]))
                store(6, gfs, tokens_grad).start()

    @pl.when((step < first_pair) | (step >= after) | (lax.rem(step, 2) == 1))
    def _():
        engine.tick(step - jnp.clip(lax.div(step - first_pair + 1, 2), 0, pairs // 2))

    @on(pl.num_programs(0) - 1)
    def _():
        engine.close(4)
        for copy in [store(0, gci, gci_o), store(1, dq, dq_o), store(6, gfs, tokens_grad)] + stores(2) + stores(3):
            copy.wait()


def backward_beside(
    cross_live, self_live, q, k, v, mixture, lse, vecs, slse, third_grads,
    act, go, low, slope, gts, second_sum, first_sum, sq, sk, sv, smix, tokens, stack,
):
    count, width = q.shape
    slots = k.shape[0]
    last = width // 128 - 1

    def pair(i):
        return jnp.clip(i - 4, 0, last)

    ticks = 8
    small = pl.BlockSpec((count, 128), lambda i: (0, pair(i)))
    large = pl.BlockSpec((slots, 128), lambda i: (0, pair(i)))
    scalar = pl.BlockSpec(memory_space=pltpu.SMEM)
    hbm = pl.BlockSpec(memory_space=pl.ANY)
    pay_shape = shape((4, 2, 2, 160, width), BF16)
    wide = pltpu.VMEM(q.shape, F32)
    thin = pltpu.VMEM(q.shape, BF16)
    dk, dv, own, dq, gci, tokens_grad, self_keep, self_send = pl.pallas_call(
        back_body,
        grid=(last + 1 + 7,),
        out_shape=[
            shape(k.shape, BF16), shape(k.shape, BF16), shape((ticks * PAIR, width), F32),
            shape(q.shape, BF16), shape(q.shape, BF16), shape(q.shape, F32), pay_shape, pay_shape,
        ],
        in_specs=[
            scalar, scalar, small, large, large, small, pl.BlockSpec((1, 8, count), lambda i: (pair(i), 0, 0)),
            once(vecs.shape), once(slse.shape), once(third_grads.shape),
        ] + [hbm] * 13,
        out_specs=[large, large, full((ticks * PAIR, width))] + [hbm] * 5,
        scratch_shapes=Scatter.scratch(ticks, width)
        + [
            pltpu.VMEM((4, 4, 2, 2, PAIR, width), BF16), pltpu.VMEM((2, BLOCKS, 32, width), BF16),
            pltpu.VMEM((2, count, width), F32), pltpu.VMEM(act.shape, BF16),
        ]
        + [wide] * 4 + [thin] * 14
        + [
            pltpu.VMEM((32, width), F32), pltpu.VMEM((1024, width), BF16), pltpu.VMEM((2, 2, 2, 2, 160, width), BF16),
            pltpu.SemaphoreType.DMA((15,)), pltpu.SemaphoreType.DMA((7,)),
        ],
        compiler_params=pltpu.CompilerParams(collective_id=1, has_side_effects=True, vmem_limit_bytes=63 * MIB),
        cost_estimate=pl.CostEstimate(flops=70 * count * slots * width, bytes_accessed=80 * MIB, transcendentals=0),
        name="backward_beside_sum",
    )(
        cross_live, self_live, q, k, v, mixture, lse, vecs, slse, third_grads,
        act, go, low, slope, gts, second_sum, first_sum, sq, sk, sv, smix, tokens, stack,
    )
    return dq, dk, dv, gci, tokens_grad, (self_keep, self_send), own


def finish_body(
    first_low, dq, mixture, gci, memory_in, dk_in, dv_in, stack, self_keep, self_send, memory_grad, own, *scratch
):
    refs, (sent, held, memory, dk, dv, weights, load_sem) = scratch[:8], scratch[8:]
    step = pl.program_id(0)
    me = lax.axis_index("dp").astype(jnp.int32)
    engine = Scatter(me, [(self_keep, self_send)], refs, own)
    early = engine.loads
    tile = memory_grad.shape[0]
    loads = [
        pltpu.make_async_copy(src, dst, load_sem.at[at])
        for at, (src, dst) in enumerate(
            [(memory_in, memory), (dk_in, dk), (dv_in, dv)]
            + [(stack.at[:, pl.ds((8 + slot) * 32, 32)], weights.at[slot]) for slot in range(2)]
        )
    ]

    def on(at):
        return pl.when(step == at)

    @on(0)
    def _():
        engine.begin()
        for load in loads:
            load.start()

    def weight(w, rows, grad, groups):
        for z in groups:
            held[...] = tn(rows[:, group_at(me, z)], grad[...])

            def target(y, x, c, z=z):
                return sent.at[w, z, y, x] if c else engine.keep.at[early + w, z, y, x]

            weight_blocks(held, me, target)

    for w, rows, grad in ((0, first_low, dq), (1, mixture, gci)):
        @on(w)
        def _(w=w, rows=rows, grad=grad):
            weight(w, rows, grad, range(4))
            engine.swap(early + w, sent.at[w]).start()

    for w, rows, grad in ((2, memory, dk), (3, memory, dv)):
        for z in range(4):
            @on((w - 2) * 4 + z + 1)
            def _(w=w, rows=rows, grad=grad, z=z):
                if z == 0:
                    for load in loads[:2] if w == 2 else loads[2:]:
                        load.wait()
                weight(w, rows, grad, (z,))
                if z == 3:
                    engine.swap(early + w, sent.at[w]).start()

    @pl.when((step >= FIRST_TILE) & (step < FIRST_TILE + dk.shape[0] // tile))
    def _():
        at = pl.ds(pl.multiple_of((step - FIRST_TILE) * tile, tile), tile)
        memory_grad[...] = nt(dk[at, :], whole(weights.at[0])) + nt(dv[at, :], whole(weights.at[1]))

    engine.tick(step)

    @on(pl.num_programs(0) - 1)
    def _():
        engine.close()


def finish(memory, dk, dv, first_low, dq, mixture, gci, stack, self_pay):
    slots, width = memory.shape
    tile = 512
    tiles = slots // tile
    ticks = self_pay[0].shape[3] // PAIR + 4
    hbm = pl.BlockSpec(memory_space=pl.ANY)
    square = once(dq.shape)
    large = pltpu.VMEM(memory.shape, BF16)
    return pl.pallas_call(
        finish_body,
        grid=(max(FIRST_TILE + tiles, ticks + 3 * LAG),),
        out_shape=[shape(memory.shape, F32), shape((ticks * PAIR, width), F32)],
        in_specs=[square, square, square, square] + [hbm] * 6,
        out_specs=[pl.BlockSpec((tile, width), lambda i: (jnp.clip(i - FIRST_TILE, 0, tiles - 1), 0)), full((ticks * PAIR, width))],
        scratch_shapes=Scatter.scratch(ticks, width)
        + [pltpu.VMEM((4, 4, 2, 2, PAIR, width), BF16), pltpu.VMEM((256, width), F32), large, large, large]
        + [pltpu.VMEM((2, BLOCKS, 32, width), BF16), pltpu.SemaphoreType.DMA((5,))],
        compiler_params=pltpu.CompilerParams(collective_id=2, has_side_effects=True, vmem_limit_bytes=62 * MIB),
        cost_estimate=pl.CostEstimate(flops=8 * slots * width * width, bytes_accessed=60 * MIB, transcendentals=0),
        name="finish_beside_sum",
    )(first_low, dq, mixture, gci, memory, dk, dv, stack, *self_pay)


def absolute(keep, send):
    return jnp.stack([keep, send], axis=1).reshape((BLOCKS,) + keep.shape[1:])


def gather(rows):
    return lax.all_gather(rows, "dp", axis=0, tiled=True)


def on_device(
    devices, tokens, memory, target_lengths, memory_lengths, cotangent,
    self_query, self_key, self_value, self_output, first_gain, first_shift,
    cross_query, cross_key, cross_value, cross_output, second_gain, second_shift,
    inner_weight, outer_weight, third_gain, third_shift,
):
    width = tokens.shape[1]
    hidden = inner_weight.shape[1]
    direct = devices == BLOCKS
    squares = [cross_key, cross_value, self_query, self_key, self_value, self_output, cross_query, cross_output]
    vectors = [first_gain, first_shift, second_gain, second_shift, third_gain, third_shift]
    if direct:
        place_of = lax.axis_index("dp").astype(jnp.int32)
        me = place_of.reshape(1)
        own = lax.dynamic_update_slice(jnp.zeros((32, width), BF16), jnp.stack(vectors), (0, place_of * 32))
        stack, parts = forward_beside(
            memory_lengths, target_lengths, tokens, squares[:VEC] + [own] + squares[VEC:], inner_weight, outer_weight, memory
        )
        (keys, values, q, k, v, mixture, first_sum, first_out, first_low, cross_q, lse,
         cross_mixture, cross_lse, second_sum, second, second_low, vecs) = parts
    else:
        me = jnp.zeros((1,), jnp.int32)
        inner_full = gather(inner_weight)
        parts = [inner_full[:, i : i + width].reshape(BLOCKS, 32, width) for i in range(0, hidden, width)]
        parts.append(gather(outer_weight).reshape(BLOCKS, 128, width))
        parts += [gather(w).reshape(BLOCKS, 32, width) for w in squares[:VEC]] + [jnp.zeros((BLOCKS, 32, width), BF16)]
        parts += [gather(w).reshape(BLOCKS, 32, width) for w in squares[VEC:]]
        stack = jnp.concatenate(parts, axis=1)
        vecs = jnp.pad(jnp.stack([gather(v) for v in vectors]), ((0, 10), (0, 0))).astype(F32)
        keys, values = kv_project(memory, stack, 8, 9)
        q, k, v, mixture, first_sum, first_out, first_low, cross_q, lse = self_forward(
            target_lengths, tokens, stack, (10, 11, 12, 14, 15), vecs
        )
        cross_mixture, cross_lse = cross_forward(memory_lengths, cross_q, keys, values)
        second_sum, second, second_low = second_norm(cross_mixture, stack, 16, first_out, vecs)

    act, slope, output_rows, gts, go, third_grads = ffn_forward(second_low, second, stack, cotangent, vecs)
    if direct:
        dq, dk, dv, gci, tokens_grad, self_pay, ffn_own = backward_beside(
            memory_lengths, target_lengths, cross_q, keys, values, cross_mixture, cross_lse, vecs, lse, third_grads,
            act, go, second_low, slope, gts, second_sum, first_sum, q, k, v, mixture, tokens, stack,
        )
        outer_own = ffn_own[:128]
        inner_own = jnp.concatenate([ffn_own[i : i + 32] for i in range(128, 256, 32)], axis=1)
        memory_grad, owned = finish(memory, dk, dv, first_low, dq, cross_mixture, gci, stack, self_pay)
        self_own = [owned[i : i + 32] for i in range(0, 128, 32)]
        vec_rows = lax.dynamic_slice(owned, (128, me[0] * 32), (6, 32))
        vec_own = [vec_rows[i] for i in range(6)]
        cross_own = [owned[i : i + 32] for i in (160, 224, 256, 192)]
    else:
        gi, gss, gci, gcm, second_grads = ffn_backward(go, gts, slope, stack, second_sum, stack, 16, vecs)
        ffn_pay = ffn_weights(me, act, go, second_low, gi)
        dq, dk, dv = cross_backward(memory_lengths, cross_q, keys, values, gcm, cross_mixture, cross_lse)
        cross_pay = square_weights(
            me, [(first_low, dq), (memory, dk), (memory, dv), (cross_mixture, gci)], "cross_weights"
        )
        gfs, gsi, gq, gk, gv, first_grads = self_backward(
            target_lengths, gss, dq, stack, 15, 14, first_sum, vecs, q, k, v, mixture, lse
        )
        self_pay = square_weights(me, [(tokens, gq), (tokens, gk), (tokens, gv), (mixture, gsi)], "self_weights")
        memory_grad = memory_gradient(dk, dv, stack, 8, 9)
        tokens_grad = tokens_gradient(gfs, gq, gk, gv, stack, (10, 11, 12))

        def summed(rows):
            return lax.psum_scatter(rows.astype(F32), "dp", scatter_dimension=0, tiled=True)

        ffn_rows, cross_rows, self_rows = absolute(*ffn_pay), absolute(*cross_pay), absolute(*self_pay)
        outer_own = summed(ffn_rows[:, :128].reshape(-1, width))
        inner_own = summed(
            jnp.concatenate([ffn_rows[:, i : i + 32].reshape(-1, width) for i in range(128, 256, 32)], axis=1)
        )
        cross_own = [summed(cross_rows[:, i : i + 32].reshape(-1, width)) for i in range(0, 128, 32)]
        self_own = [summed(self_rows[:, i : i + 32].reshape(-1, width)) for i in range(0, 128, 32)]
        vec_own = [summed(rows[i]) for rows in (first_grads, second_grads, third_grads) for i in range(2)]

    return (
        output_rows, tokens_grad, memory_grad,
        *self_own, vec_own[0], vec_own[1],
        *cross_own, vec_own[2], vec_own[3],
        inner_own, outer_own, vec_own[4], vec_own[5],
    )


def solution(mesh):
    rows, line = P("dp", None), P("dp")
    block = [rows] * 4 + [line] * 2
    placed = (rows, rows, line, line, rows, *block, *block, rows, rows, line, line)
    return jax.shard_map(
        functools.partial(on_device, mesh.shape["dp"]),
        mesh=mesh,
        in_specs=placed,
        out_specs=(rows, rows, rows, *block, *block, rows, rows, line, line),
        check_vma=False,
    )
```

```python
import functools
import math

import jax
import jax.numpy as jnp
from jax import lax
from jax.experimental import pallas as pl
from jax.experimental.pallas import tpu as pltpu
from jax.sharding import PartitionSpec as P

HEAD = 64
EPS = 1e-05
SCALE = 1.0 / math.sqrt(HEAD)
LOG2E = 1.4426950408889634
BLOCKS = 32
MIB = 1024 * 1024
F32 = jnp.float32
BF16 = jnp.bfloat16
PAIR, HALF = 32, 16
CORE, XBIT, YBIT, NEAR, FAR, BOTH = PARTNERS = (1, 2, 4, 8, 16, 24)
LAG = 2
PARTS = 2
GATHER_LAG = 1
FIRST_TILE = 7


def nn(a, b):
    return jnp.dot(a, b, preferred_element_type=F32)


def nt(a, b):
    return lax.dot_general(a, b, (((1,), (1,)), ((), ())), preferred_element_type=F32)


def tn(a, b):
    return lax.dot_general(a, b, (((0,), (0,)), ((), ())), preferred_element_type=F32)


def whole(ref):
    return ref[...].reshape(-1, ref.shape[-1])


def call(body, name, out, grid=(), ins=None, outs=None, scratch=(), prefetch=0, limit=56, flops=0, moved=0):
    return pl.pallas_call(
        body,
        out_shape=out,
        grid_spec=pltpu.PrefetchScalarGridSpec(
            num_scalar_prefetch=prefetch,
            grid=grid,
            in_specs=ins,
            out_specs=outs,
            scratch_shapes=scratch,
        ),
        compiler_params=pltpu.CompilerParams(vmem_limit_bytes=limit * MIB),
        cost_estimate=pl.CostEstimate(flops=flops, bytes_accessed=moved, transcendentals=0),
        name=name,
    )


def full(shape):
    return pl.BlockSpec(shape, lambda *_: (0,) * len(shape))


def weight(at):
    return pl.BlockSpec((BLOCKS, 32, 1024), lambda *_: (0, at, 0))


def shape(dims, dtype):
    return jax.ShapeDtypeStruct(dims, dtype)


def norm_parts(summed):
    average = jnp.mean(summed, axis=-1, keepdims=True)
    centred = summed - average
    spread = jnp.mean(centred * centred, axis=-1, keepdims=True)
    scale = lax.rsqrt(spread + EPS)
    return centred * scale, scale


def norm_back(summed, gain, upstream):
    normal, scale = norm_parts(summed)
    grad_gain = jnp.sum(upstream * normal, axis=0, keepdims=True)
    grad_shift = jnp.sum(upstream, axis=0, keepdims=True)
    scaled = upstream * gain
    first = jnp.mean(scaled, axis=-1, keepdims=True)
    second = jnp.mean(scaled * normal, axis=-1, keepdims=True)
    return scale * (scaled - first - normal * second), grad_gain, grad_shift


def lanes(rows):
    return lax.broadcasted_iota(jnp.int32, (rows, 128), 1)


def stack_pair(rows):
    low = lanes(rows.shape[0]) < HEAD
    zero = jnp.zeros_like(rows)
    return jnp.concatenate([jnp.where(low, rows, zero), jnp.where(low, zero, rows)], axis=0)


def unstack_pair(stacked):
    half = stacked.shape[0] // 2
    return jnp.where(lanes(half) < HEAD, stacked[:half], stacked[half:])


def pair_forward(stacked, keys, values, mask):
    scores = nt(stacked, keys)
    if mask is not None:
        scores = mask(scores)
    peak = jnp.max(scores, axis=-1, keepdims=True)
    raised = jnp.exp2((scores - peak) * (SCALE * LOG2E))
    total = jnp.sum(raised, axis=-1, keepdims=True)
    mixed = nn(raised.astype(BF16), values) / total
    return mixed, peak * SCALE + jnp.log(total)


def pair_tile_back(q2, g2, keys, values, totals, inner, mask):
    scores = nt(keys, q2)
    probs = jnp.exp2(scores * (SCALE * LOG2E) - totals)
    if mask is not None:
        probs = mask(probs)
    grad_probs = nt(values, g2)
    grad_scores = (probs * (grad_probs - inner)).astype(BF16)
    grad_values = nn(probs.astype(BF16), g2)
    grad_keys = nn(grad_scores, q2) * SCALE
    grad_queries = tn(keys, grad_scores)
    return grad_queries, grad_keys, grad_values


def pair_inner(mixture, grad):
    product = mixture.astype(F32) * grad.astype(F32)
    half = jnp.where(
        (lax.broadcasted_iota(jnp.int32, (8, 128), 1) // HEAD)
        == lax.broadcasted_iota(jnp.int32, (8, 128), 0),
        1.0,
        0.0,
    ).astype(F32)
    sums = lax.dot_general(
        half, product, (((1,), (1,)), ((), ())),
        preferred_element_type=F32, precision=lax.Precision.HIGHEST,
    )
    return jnp.concatenate([sums[0:1], sums[1:2]], axis=1)


def join_grad_queries(grad):
    count = grad.shape[1] // 2
    joined = jnp.concatenate([grad[:HEAD, :count], grad[HEAD:, count:]], axis=0) * SCALE
    return joined.T.astype(BF16)


def kv_body(memory, wk, wv, keys, values):
    rows = memory[...]
    keys[...] = nn(rows, whole(wk)).astype(BF16)
    values[...] = nn(rows, whole(wv)).astype(BF16)


def kv_project(memory, stack, at_k, at_v):
    count, width = memory.shape
    tile = 512
    spec = pl.BlockSpec((tile, width), lambda i: (i, 0))
    return call(
        kv_body, "cross_kv", [shape(memory.shape, BF16)] * 2, (count // tile,),
        [spec, weight(at_k), weight(at_v)], [spec, spec],
        flops=4 * count * width * width, moved=12 * MIB + 4 * MIB,
    )(memory, stack, stack)


def self_attention(live, q_o, k_o, v_o, mix_o, lse_o):
    count, width = q_o.shape
    at_q = lax.rem(lax.broadcasted_iota(jnp.int32, (2 * count, count), 0), count)
    at_k = lax.broadcasted_iota(jnp.int32, (2 * count, count), 1)
    allowed = (at_k <= at_q) & (at_k < live)
    column = lanes(count)
    totals = jnp.zeros((count, 128), F32)
    for pair in range(width // 128):
        cut = slice(pair * 128, pair * 128 + 128)
        mixed, log_total = pair_forward(
            stack_pair(q_o[:, cut]), k_o[:, cut], v_o[:, cut],
            lambda scores: jnp.where(allowed, scores, -1e30),
        )
        mix_o[:, cut] = unstack_pair(mixed).astype(BF16)
        totals = jnp.where(column == 2 * pair, log_total[:count], totals)
        totals = jnp.where(column == 2 * pair + 1, log_total[count:], totals)
    lse_o[...] = totals.T


def self_body(length, tokens, wq, wk, wv, wo, wcq, vecs, q_o, k_o, v_o, mix_o, sum_o, first_o, low_o, cq_o, lse_o):
    rows = tokens[...]
    count, width = rows.shape
    q_o[...] = nn(rows, whole(wq)).astype(BF16)
    k_o[...] = nn(rows, whole(wk)).astype(BF16)
    v_o[...] = nn(rows, whole(wv)).astype(BF16)
    self_attention(length[0], q_o, k_o, v_o, mix_o, lse_o)
    summed = rows.astype(F32) + nn(mix_o[...], whole(wo))
    sum_o[...] = summed
    normal, _ = norm_parts(summed)
    first = normal * vecs[0:1] + vecs[1:2]
    first_o[...] = first
    low = first.astype(BF16)
    low_o[...] = low
    cq_o[...] = nn(low, whole(wcq)).astype(BF16)


def self_forward(length, tokens, stack, at, vecs):
    count, width = tokens.shape
    low = shape(tokens.shape, BF16)
    wide = shape(tokens.shape, F32)
    spec = full(tokens.shape)
    return call(
        self_body, "self_forward",
        [low, low, low, low, wide, wide, low, low, shape((128, count), F32)], (1,),
        [spec] + [weight(k) for k in at] + [full(vecs.shape)],
        [spec] * 8 + [full((128, count))], prefetch=1,
        flops=10 * count * width * width, moved=16 * MIB,
    )(length, tokens, stack, stack, stack, stack, stack, vecs)


def cross_body(length, q, k, v, mix_o, lse_o):
    count = q.shape[0]
    slots = k.shape[0]
    live = length[0]
    q2 = stack_pair(q[...])
    keys = k[...]
    values = v[...]
    half = slots // 2
    tile = 128
    column = lax.broadcasted_iota(jnp.int32, (tile, slots - half), 1) + half

    def mask(scores):
        upper = jnp.where(column < live, scores[:, half:], -1e30)
        return jnp.concatenate([scores[:, :half], upper], axis=1)

    mixes, logs = [], []
    for at in range(0, 2 * count, tile):
        mixed, log_total = pair_forward(q2[at : at + tile], keys, values, mask)
        mixes.append(mixed)
        logs.append(log_total)
    mix_o[...] = unstack_pair(jnp.concatenate(mixes, axis=0)).astype(BF16)
    logs = jnp.concatenate(logs, axis=0)
    column = lanes(count)
    totals = jnp.where(column == 0, logs[:count], jnp.where(column == 1, logs[count:], 0.0))
    lse_o[0] = totals.T[:8]


def cross_forward(length, q, k, v):
    count, width = q.shape
    slots = k.shape[0]
    pairs = width // 128
    return call(
        cross_body, "cross_forward",
        [shape(q.shape, BF16), shape((pairs, 8, count), F32)], (pairs,),
        [pl.BlockSpec((count, 128), lambda i, _: (0, i))]
        + [pl.BlockSpec((slots, 128), lambda i, _: (0, i))] * 2,
        [pl.BlockSpec((count, 128), lambda i, _: (0, i)), pl.BlockSpec((1, 8, count), lambda i, _: (i, 0, 0))],
        prefetch=1, flops=16 * count * slots * width, moved=10 * MIB,
    )(length, q, k, v)


def second_rows(mixture, wo, first, vecs, sum_o, second_o, low_o):
    summed = first + nn(mixture, wo)
    sum_o[...] = summed
    normal, _ = norm_parts(summed)
    second = normal * vecs[2:3, :] + vecs[3:4, :]
    second_o[...] = second
    low_o[...] = second.astype(BF16)


def second_body(mixture, wo, first, vecs, sum_o, second_o, low_o):
    second_rows(mixture[...], whole(wo), first[...], vecs, sum_o, second_o, low_o)


def second_norm(mixture, stack, at, first, vecs):
    spec = full(mixture.shape)
    return call(
        second_body, "second_norm",
        [shape(mixture.shape, F32), shape(mixture.shape, F32), shape(mixture.shape, BF16)], (1,),
        [spec, weight(at), spec, full(vecs.shape)], [spec] * 3,
        flops=MIB * 512, moved=6 * MIB,
    )(mixture, stack, first, vecs)


def erf(x):
    return lax.erf(x)


def ffn_body(low, second, inner, outer, cot, vecs, act_o, slope_o, out_o, gts_o, go_o, grads_o, total):
    step = pl.program_id(0)
    pre = nn(low[...], whole(inner))
    half = 0.5 * (1.0 + erf(pre * math.sqrt(0.5)))
    active = (pre * half).astype(BF16)
    act_o[...] = active
    slope_o[...] = half + pre * (jnp.exp(-0.5 * pre * pre) * (1.0 / math.sqrt(2.0 * math.pi)))
    part = nn(active, whole(outer))

    @pl.when(step == 0)
    def _():
        total[...] = second[...] + part

    @pl.when(step > 0)
    def _():
        total[...] += part

    @pl.when(step == pl.num_programs(0) - 1)
    def _():
        summed = total[...]
        normal, _ = norm_parts(summed)
        out_o[...] = (normal * vecs[4:5] + vecs[5:6]).astype(BF16)
        grad, gain, shift = norm_back(summed, vecs[4:5], cot[...].astype(F32))
        gts_o[...] = grad
        go_o[...] = grad.astype(BF16)
        grads_o[...] = jnp.concatenate([gain, shift] + [jnp.zeros_like(gain)] * 6, axis=0)


def ffn_forward(low, second, stack, cot, vecs):
    count, width = low.shape
    spec = full(low.shape)
    wide = pl.BlockSpec((count, 1024), lambda i: (0, i))
    return call(
        ffn_body, "ffn_forward",
        [shape((count, 4096), BF16), shape((count, 4096), F32), shape(low.shape, BF16), shape(low.shape, F32), shape(low.shape, BF16), shape((8, width), F32)],
        (4,),
        [spec, spec, pl.BlockSpec((BLOCKS, 32, 1024), lambda i: (0, i, 0)), pl.BlockSpec((8, 128, 1024), lambda i: (i, 1, 0)), spec, full(vecs.shape)],
        [wide, wide, spec, spec, spec, full((8, width))],
        scratch=[pltpu.VMEM(low.shape, F32)],
        flops=16 * count * width * width, moved=24 * MIB,
    )(low, second, stack, stack, cot, vecs)


def ffn_back_body(go, gts, slope, inner, outer, summed, wo, vecs, gi_o, gss_o, gci_o, gcm_o, grads_o, total):
    step = pl.program_id(0)
    grad = nt(go[...], whole(outer))
    low = (grad * slope[...]).astype(BF16)
    gi_o[...] = low
    part = nt(low, whole(inner))

    @pl.when(step == 0)
    def _():
        total[...] = gts[...] + part

    @pl.when(step > 0)
    def _():
        total[...] += part

    @pl.when(step == pl.num_programs(0) - 1)
    def _():
        grad, gain, shift = norm_back(summed[...], vecs[2:3], total[...])
        gss_o[...] = grad
        low = grad.astype(BF16)
        gci_o[...] = low
        gcm_o[...] = nt(low, whole(wo)).astype(BF16)
        grads_o[...] = jnp.concatenate([gain, shift] + [jnp.zeros_like(gain)] * 6, axis=0)


def ffn_backward(go, gts, slope, stack, summed, squares, at, vecs):
    count, width = go.shape
    spec = full(go.shape)
    wide = pl.BlockSpec((count, 1024), lambda i: (0, i))
    low = shape(go.shape, BF16)
    return call(
        ffn_back_body, "ffn_backward",
        [shape((count, 4096), BF16), shape(go.shape, F32), low, low, shape((8, width), F32)],
        (4,),
        [spec, spec, wide, pl.BlockSpec((BLOCKS, 32, 1024), lambda i: (0, i, 0)), pl.BlockSpec((8, 128, 1024), lambda i: (i, 1, 0)), spec, weight(at), full(vecs.shape)],
        [wide, spec, spec, spec, full((8, width))],
        scratch=[pltpu.VMEM(go.shape, F32)],
        flops=18 * count * width * width, moved=26 * MIB,
    )(go, gts, slope, stack, stack, summed, squares, vecs)


def cross_back_body(length, q, k, v, g, mixture, lse, dq_o, dk_o, dv_o):
    live = length[0]
    slots = k.shape[0]
    count = q.shape[0]
    q2 = stack_pair(q[...])
    g2 = stack_pair(g[...])
    totals = jnp.concatenate([lse[0, 0:1], lse[0, 1:2]], axis=1) * LOG2E
    inner = pair_inner(mixture[...], g[...])
    tile = 256
    grad_q = jnp.zeros((128, 2 * count), F32)
    for at in range(0, slots, tile):
        mask = None
        if at + tile > slots // 2:
            row = lax.broadcasted_iota(jnp.int32, (tile, 2 * count), 0) + at

            def mask(probs, row=row):
                return jnp.where(row < live, probs, 0.0)

        cut = slice(at, at + tile)
        dq, dk, dv = pair_tile_back(q2, g2, k[cut], v[cut], totals, inner, mask)
        grad_q = grad_q + dq
        dk_o[cut] = dk.astype(BF16)
        dv_o[cut] = dv.astype(BF16)
    dq_o[...] = join_grad_queries(grad_q)


def cross_backward(length, q, k, v, g, mixture, lse):
    count, width = q.shape
    slots = k.shape[0]
    pairs = width // 128
    small = pl.BlockSpec((count, 128), lambda i, _: (0, i))
    large = pl.BlockSpec((slots, 128), lambda i, _: (0, i))
    return call(
        cross_back_body, "cross_backward",
        [shape(q.shape, BF16), shape(k.shape, BF16), shape(k.shape, BF16)], (pairs,),
        [small, large, large, small, small, pl.BlockSpec((1, 8, count), lambda i, _: (i, 0, 0))],
        [small, large, large], prefetch=1,
        flops=40 * count * slots * width, moved=18 * MIB,
    )(length, q, k, v, g, mixture, lse)


def memory_grad_body(dk, dv, wk, wv, out):
    out[...] = nt(dk[...], whole(wk)) + nt(dv[...], whole(wv))


def memory_gradient(dk, dv, stack, at_k, at_v):
    count, width = dk.shape
    tile = 512
    spec = pl.BlockSpec((tile, width), lambda i: (i, 0))
    return call(
        memory_grad_body, "memory_grad", shape(dk.shape, F32), (count // tile,),
        [spec, spec, weight(at_k), weight(at_v)], spec,
        flops=4 * count * width * width, moved=20 * MIB,
    )(dk, dv, stack, stack)


def self_back_body(length, gss, dcq, wcq, summed, wo, vecs, q, k, v, mixture, lse, gfs_o, gsi_o, gq_o, gk_o, gv_o, grads_o):
    live = length[0]
    count, width = gss.shape
    upstream = gss[...] + nt(dcq[...], whole(wcq))
    grad, gain, shift = norm_back(summed[...], vecs[0:1], upstream)
    gfs_o[...] = grad
    grads_o[...] = jnp.concatenate([gain, shift] + [jnp.zeros_like(gain)] * 6, axis=0)
    low = grad.astype(BF16)
    gsi_o[...] = low
    mix_grad = nt(low, whole(wo)).astype(BF16)
    at_k = lax.broadcasted_iota(jnp.int32, (count, 2 * count), 0)
    at_q = lax.rem(lax.broadcasted_iota(jnp.int32, (count, 2 * count), 1), count)
    allowed = (at_k <= at_q) & (at_k < live)
    for pair in range(width // 128):
        cut = slice(pair * 128, pair * 128 + 128)
        g = mix_grad[:, cut]
        totals = jnp.concatenate([lse[2 * pair : 2 * pair + 1], lse[2 * pair + 1 : 2 * pair + 2]], axis=1) * LOG2E
        scores_back = pair_tile_back(
            stack_pair(q[:, cut]), stack_pair(g), k[:, cut], v[:, cut], totals,
            pair_inner(mixture[:, cut], g),
            lambda probs: jnp.where(allowed, probs, 0.0),
        )
        dq, dk, dv = scores_back
        gq_o[:, cut] = join_grad_queries(dq)
        gk_o[:, cut] = dk.astype(BF16)
        gv_o[:, cut] = dv.astype(BF16)


def self_backward(length, gss, dcq, stack, at_cq, at_o, summed, vecs, q, k, v, mixture, lse):
    count, width = q.shape
    spec = full(q.shape)
    low = shape(q.shape, BF16)
    return call(
        self_back_body, "self_backward",
        [shape(q.shape, F32), low, low, low, low, shape((8, width), F32)], (1,),
        [spec, spec, weight(at_cq), spec, weight(at_o), full(vecs.shape), spec, spec, spec, spec, full(lse.shape)],
        [spec] * 5 + [full((8, width))], prefetch=1,
        flops=8 * count * width * width, moved=12 * MIB,
    )(length, gss, dcq, stack, summed, stack, vecs, q, k, v, mixture, lse)


def tokens_grad_body(gfs, gq, gk, gv, wq, wk, wv, out):
    out[...] = gfs[...] + nt(gq[...], whole(wq)) + nt(gk[...], whole(wk)) + nt(gv[...], whole(wv))


def tokens_gradient(gfs, gq, gk, gv, stack, at):
    spec = full(gfs.shape)
    return call(
        tokens_grad_body, "tokens_grad", shape(gfs.shape, F32), (1,),
        [spec] * 4 + [weight(k) for k in at], spec,
        flops=6 * MIB * 256, moved=10 * MIB,
    )(gfs, gq, gk, gv, stack, stack, stack)


def place(keep, send, at, size, pieces, me):
    low = lax.rem(me, 8)
    for j in range(8):
        rows = pieces(lax.bitwise_xor(low, j))
        target = send if j % 2 else keep
        target[j // 2, at : at + size, :] = rows.astype(BF16)


def group_of(step, me):
    return lax.bitwise_xor(step, lax.div(me[0], 8))


def payload(rows, width):
    out = [shape((16, rows, width), BF16)] * 2
    spec = [pl.BlockSpec((4, rows, width), lambda i, _: (i, 0, 0))] * 2
    return out, spec


def ffn_weights_body(me, act, go, low, gi, keep, send, held):
    step = pl.program_id(0)

    @pl.when(step < 4)
    def _():
        held[...] = tn(act[...], go[...])
        place(keep, send, 0, 128, lambda d: held[pl.ds(pl.multiple_of(d * 128, 128), 128), :], me[0])

    @pl.when(step >= 4)
    def _():
        for part in range(4):
            held[:256, :] = tn(low[...], gi[:, part * 1024 : part * 1024 + 1024])
            place(keep, send, part * 32, 32, lambda d: held[pl.ds(pl.multiple_of(d * 32, 32), 32), :], me[0])


def ffn_weights(me, act, go, low, gi):
    count, width = go.shape
    spec = pl.BlockSpec((4, 128, width), lambda i, me: (lax.rem(i, 4), lax.div(i, 4), 0))
    return call(
        ffn_weights_body, "ffn_weights", [shape((16, 256, width), BF16)] * 2, (8,),
        [
            pl.BlockSpec((count, 1024), lambda i, me: (0, group_of(jnp.minimum(i, 3), me))),
            full(go.shape),
            pl.BlockSpec((count, 256), lambda i, me: (0, group_of(jnp.maximum(i - 4, 0), me))),
            full(gi.shape),
        ],
        [spec, spec], [pltpu.VMEM((1024, width), F32)], 1,
        flops=16 * count * width * width, moved=22 * MIB,
    )(me, act, go, low, gi)


def square_body(me, *refs):
    count = (len(refs) - 3) // 2
    keep, send, held = refs[-3:]
    for at in range(count):
        held[...] = tn(refs[2 * at][...], refs[2 * at + 1][...])
        place(keep, send, at * 32, 32, lambda d: held[pl.ds(pl.multiple_of(d * 32, 32), 32), :], me[0])


def square_weights(me, pairs, name):
    width = pairs[0][0].shape[1]
    out, spec = payload(128, width)
    ins, operands, flops = [], [], 0
    for rows, grads in pairs:
        ins.append(pl.BlockSpec((rows.shape[0], 256), lambda i, me: (0, group_of(i, me))))
        ins.append(full(grads.shape))
        operands += [rows, grads]
        flops += 2 * rows.shape[0] * width * width
    return call(
        square_body, name, out, (4,), ins, spec,
        [pltpu.VMEM((256, width), F32)], 1, flops=flops, moved=20 * MIB,
    )(me, *operands)


def flip(me, bits):
    for bit in (1, 2, 4, 8, 16):
        if bits & bit:
            me = me + bit - 2 * bit * lax.rem(lax.div(me, bit), 2)
    return me


def remote(src, dst, out_sem, in_sem, to):
    return pltpu.make_async_remote_copy(
        src_ref=src, dst_ref=dst, send_sem=out_sem, recv_sem=in_sem,
        device_id=(to,), device_id_type=pl.DeviceIdType.MESH,
    )


def greet(me):
    barrier = pltpu.get_barrier_semaphore()
    for bit in PARTNERS:
        pl.semaphore_signal(barrier, inc=1, device_id=(flip(me, bit),), device_id_type=pl.DeviceIdType.MESH)
    pl.semaphore_wait(barrier, len(PARTNERS))


class Scatter:
    def __init__(self, me, pays, refs, out):
        self.me, self.pays, self.out = me, pays, out
        (self.keep, self.came0, self.came1, self.came2, self.came3,
         self.load_sem, self.out_sem, self.in_sem) = refs
        self.ticks = self.keep.shape[0]
        self.loads = sum(kept.shape[3] for kept, _ in pays) // PAIR * PARTS
        self.part_width = self.keep.shape[5]

    @staticmethod
    def scratch(ticks, width):
        def held(*dims):
            return pltpu.VMEM((ticks,) + dims + (width,), BF16)

        return [
            held(4, 2, 2, PAIR), held(4, 2, 2, PAIR), held(2, 4, 2, HALF), held(2, 4, HALF), held(3, PAIR),
            pltpu.SemaphoreType.DMA((ticks,)), pltpu.SemaphoreType.DMA((8, ticks)), pltpu.SemaphoreType.DMA((8, ticks)),
        ]

    def link(self, stage, p, src, dst, bit):
        return remote(src, dst, self.out_sem.at[stage, p], self.in_sem.at[stage, p], flip(self.me, bit))

    def load(self, p, kept, at):
        return pltpu.make_async_copy(
            kept.at[:, :, :, pl.ds(at, PAIR), pl.ds((p % PARTS) * self.part_width, self.part_width)], self.keep.at[p], self.load_sem.at[p]
        )

    def loaded(self, p):
        return pltpu.make_async_copy(self.came0.at[p], self.keep.at[p], self.load_sem.at[p])

    def put(self, target, p, block, rows):
        for part in range(PARTS):
            target.at[(p * PARTS + part, *block)][...] = rows[:, part * self.part_width : (part + 1) * self.part_width]

    def swap(self, p, sent):
        return self.link(0, p, sent, self.came0.at[p], CORE)

    def hop(self, stage, p):
        keep, up, down = self.keep, pl.ds(0, HALF), pl.ds(HALF, HALF)
        if stage == 1:
            return self.link(1, p, keep.at[p, :, :, 1, up], self.came1.at[p, 0], XBIT)
        if stage == 2:
            return self.link(2, p, keep.at[p, :, 1, :, down], self.came1.at[p, 1], YBIT)
        if stage == 3:
            return self.link(3, p, keep.at[p, :, 1, 0, up], self.came2.at[p, 0], YBIT)
        if stage == 4:
            return self.link(4, p, keep.at[p, :, 0, 1, down], self.came2.at[p, 1], XBIT)
        z = stage - 4
        return self.link(stage, p, keep.at[p, z, 0, 0], self.came3.at[p, z - 1], (NEAR, FAR, BOTH)[z - 1])

    def begin(self):
        greet(self.me)
        p = 0
        for kept, sent in self.pays:
            for at in range(0, kept.shape[3] * PARTS, PAIR):
                row = at // (PAIR * PARTS) * PAIR
                self.load(p, kept, row).start()
                cut = pl.ds((p % PARTS) * self.part_width, self.part_width)
                self.swap(p, sent.at[:, :, :, pl.ds(row, PAIR), cut]).start()
                p += 1

    def total(self, p, z, y, x, h, depth):
        cut = slice(h * HALF, h * HALF + HALF)
        sum_ = self.keep[p, z, y, x, cut, :].astype(F32) + self.came0[p, z, y, x, cut, :].astype(F32)
        if depth > 1:
            sum_ = sum_ + self.came1[p, h, z, y if h == 0 else x].astype(F32)
        if depth > 2:
            sum_ = sum_ + self.came2[p, h, z].astype(F32)
        if depth > 3:
            for other in range(3):
                sum_ = sum_ + self.came3[p, other, cut, :].astype(F32)
        return sum_

    def sums(self, p, blocks, h, depth):
        for z, y, x in blocks:
            self.keep[p, z, y, x, h * HALF : h * HALF + HALF, :] = self.total(p, z, y, x, h, depth).astype(BF16)

    def ticks_of(self, t):
        def one(i, _):
            self.tick(t * PARTS + i)
            return 0

        lax.fori_loop(0, PARTS, one, 0)

    def tick(self, t):
        ticks = self.ticks

        def stage(at):
            return pl.when((t >= at * LAG) & (t < ticks + at * LAG))

        if self.pays:
            @pl.when((t >= 0) & (t < self.loads))
            def _():
                self.loaded(t).wait()

        @stage(0)
        def _():
            self.swap(t, self.came0.at[t]).wait_recv()
            self.sums(t, [(z, y, 1) for z in range(4) for y in range(2)], 0, 1)
            self.hop(1, t).start()
            self.sums(t, [(z, 1, x) for z in range(4) for x in range(2)], 1, 1)
            self.hop(2, t).start()

        @stage(1)
        def _():
            p = t - 1 * LAG
            self.hop(1, p).wait_recv()
            self.sums(p, [(z, 1, 0) for z in range(4)], 0, 2)
            self.hop(3, p).start()
            self.hop(2, p).wait_recv()
            self.sums(p, [(z, 0, 1) for z in range(4)], 1, 2)
            self.hop(4, p).start()

        @stage(2)
        def _():
            p = t - 2 * LAG
            self.hop(3, p).wait_recv()
            self.hop(4, p).wait_recv()
            for z in (2, 3, 1):
                for h in range(2):
                    self.sums(p, [(z, 0, 0)], h, 3)
                self.hop(4 + z, p).start()

        @stage(3)
        def _():
            p = t - 3 * LAG
            for z in (1, 2, 3):
                self.hop(4 + z, p).wait_recv()
            for h in range(2):
                at = pl.ds(pl.multiple_of(lax.div(p, PARTS) * PAIR + h * HALF, HALF), HALF)
                cut = pl.ds(pl.multiple_of(lax.rem(p, PARTS) * self.part_width, 128), self.part_width)
                self.out[at, cut] = self.total(p, 0, 0, 0, h, 4)

    def close(self, swapped=0):
        def swap_ended(p, _):
            self.swap(p, self.came0.at[p]).wait_send()
            return 0

        def ended(p, _):
            for stage in range(1, 8):
                self.hop(stage, p).wait_send()
            return 0

        lax.fori_loop(swapped, self.ticks, swap_ended, 0)
        lax.fori_loop(0, self.ticks, ended, 0)


def weight_blocks(held, me, store):
    low = lax.rem(me, 8)
    for j in range(8):
        rows = held[pl.ds(pl.multiple_of(flip(low, j) * 32, 32), 32), :].astype(BF16)
        store(j // 4, (j // 2) % 2, j % 2, rows)


def group_at(me, z):
    high = flip(lax.div(me, 8), z)
    return pl.ds(pl.multiple_of(high * 256, 256), 256)


def once(dims):
    return pl.BlockSpec(dims, lambda *_: (0,) * len(dims), pipeline_mode=pl.Buffered(1))


def weight_once(at):
    return pl.BlockSpec((BLOCKS, 32, 1024), lambda *_: (0, at, 0), pipeline_mode=pl.Buffered(1))


class Gather:
    def __init__(self, me, g, shift, local_sem, out_sem, in_sem):
        self.me, self.g, self.shift = me, g, shift
        self.local_sem, self.out_sem, self.in_sem = local_sem, out_sem, in_sem
        self.c, self.x, self.y = [lax.rem(lax.div(me, bit), 2) for bit in (CORE, XBIT, YBIT)]
        self.z = lax.div(me, NEAR)
        self.ticks = g.shape[4] // PAIR

    @staticmethod
    def scratch(ticks):
        return [pltpu.SemaphoreType.DMA((ticks,)), pltpu.SemaphoreType.DMA((8, ticks)), pltpu.SemaphoreType.DMA((8, ticks))]

    def rows(self, p):
        return pl.ds(pl.multiple_of(lax.rem(p + self.shift, self.ticks) * PAIR, PAIR), PAIR)

    def half(self, p, h):
        return pl.ds(pl.multiple_of(lax.rem(p + self.shift, self.ticks) * PAIR + h * HALF, HALF), HALF)

    def mine(self, p):
        return self.g.at[self.z, self.y, self.x, self.c, self.rows(p)]

    def local(self, p, src):
        return pltpu.make_async_copy(src, self.mine(p), self.local_sem.at[p])

    def hop(self, stage, p):
        g, every = self.g, slice(None)
        if stage < 3:
            ref, bits = self.mine(p), (NEAR, FAR, BOTH)[stage]
        elif stage == 3:
            ref, bits = g.at[every, self.y, self.x, self.c, self.half(p, 0)], XBIT
        elif stage == 4:
            ref, bits = g.at[every, self.y, self.x, self.c, self.half(p, 1)], YBIT
        elif stage == 5:
            ref, bits = g.at[every, self.y, every, self.c, self.half(p, 0)], YBIT
        elif stage == 6:
            ref, bits = g.at[every, every, self.x, self.c, self.half(p, 1)], XBIT
        else:
            ref, bits = g.at[every, every, every, self.c, self.rows(p)], CORE
        return remote(ref, ref, self.out_sem.at[stage, p], self.in_sem.at[stage, p], flip(self.me, bits))

    def begin(self, sources):
        for p, src in enumerate(sources):
            self.local(p, src).start()
        greet(self.me)

    def tick(self, t):
        def stage(at):
            return pl.when((t >= at * GATHER_LAG) & (t < self.ticks + at * GATHER_LAG))

        @stage(0)
        def _():
            self.local(t, self.mine(t)).wait()
            for k in (1, 2, 0):
                self.hop(k, t).start()

        @stage(1)
        def _():
            p = t - GATHER_LAG
            for k in range(3):
                self.hop(k, p).wait_recv()
            self.hop(3, p).start()
            self.hop(4, p).start()

        @stage(2)
        def _():
            p = t - 2 * GATHER_LAG
            self.hop(3, p).wait_recv()
            self.hop(5, p).start()
            self.hop(4, p).wait_recv()
            self.hop(6, p).start()

        @stage(3)
        def _():
            p = t - 3 * GATHER_LAG
            self.hop(5, p).wait_recv()
            self.hop(6, p).wait_recv()
            self.hop(7, p).start()

        @stage(4)
        def _():
            self.hop(7, t - 4 * GATHER_LAG).wait_recv()

    def close(self):
        def ended(p, _):
            for stage in range(8):
                self.hop(stage, p).wait_send()
            return 0

        lax.fori_loop(0, self.ticks, ended, 0)


def forward_body(cross_live, self_live, tokens, *refs):
    sources, (inner, outer, memory_in), g = refs[:9], refs[9:12], refs[12]
    outs, held = refs[13:30], refs[30:47]
    weights, vec_rows, memory, load_sem, store_sem = refs[47:52]
    keys, values, q, k, v, mix, summed, first, low, cq, lse, cmix, clse, second_sum, second, second_low, vecs = held
    step = pl.program_id(0)
    me = lax.axis_index("dp").astype(jnp.int32)
    engine = Gather(me, g, 8, *refs[52:])
    count, width = tokens.shape
    pairs = width // 128
    ready = 4 * GATHER_LAG + 1

    def load(at):
        every = slice(None)
        target = vec_rows if at == VEC else weights.at[at if at < VEC else at - 1]
        return pltpu.make_async_copy(g.at[every, every, every, every, engine.rows(at)], target, load_sem.at[at])

    def weight_of(at):
        load(at).wait()
        return weights[at if at < VEC else at - 1].reshape(width, width)

    def load_memory():
        return pltpu.make_async_copy(memory_in, memory, load_sem.at[9])

    def store(*which):
        for at in which:
            pltpu.make_async_copy(held[at], outs[at], store_sem.at[at]).start()

    def on(at):
        return pl.when(step == at)

    @on(0)
    def _():
        load_memory().start()
        parts = [inner.at[:, pl.ds(i, width)] for i in range(0, inner.shape[1], width)]
        parts += [outer.at[pl.ds(i, PAIR)] for i in range(0, outer.shape[0], PAIR)]
        engine.begin(list(sources) + parts)

    tile = 512

    @on(ready)
    def _():
        load_memory().wait()
        factor = weight_of(0)
        for at in range(0, memory.shape[0], tile):
            keys[at : at + tile, :] = nn(memory[at : at + tile, :], factor).astype(BF16)
        store(0)

    @on(ready + 1)
    def _():
        factor = weight_of(1)
        for at in range(0, memory.shape[0], tile):
            values[at : at + tile, :] = nn(memory[at : at + tile, :], factor).astype(BF16)
        store(1)

    for at, rows in ((2, q), (3, k), (4, v)):
        @on(ready + at)
        def _(at=at, rows=rows):
            rows[...] = nn(tokens[...], weight_of(at)).astype(BF16)
            store(at)

    @on(ready + VEC)
    def _():
        load(VEC).wait()
        total = jnp.zeros((16, width), F32)
        for z in range(4):
            for y in range(2):
                for x in range(2):
                    for c in range(2):
                        total = total + vec_rows[z, y, x, c, :16, :].astype(F32)
        vecs[...] = total
        self_attention(self_live[0], q, k, v, mix, lse)
        store(16, 5, 10)

    @on(ready + 6)
    def _():
        total = tokens[...].astype(F32) + nn(mix[...], weight_of(6))
        summed[...] = total
        normal, _ = norm_parts(total)
        rows = normal * vecs[0:1, :] + vecs[1:2, :]
        first[...] = rows
        low[...] = rows.astype(BF16)
        store(6, 7, 8)

    @on(ready + 7)
    def _():
        cq[...] = nn(low[...], weight_of(7)).astype(BF16)
        store(9)

    each = 2
    start = ready + 8

    @pl.when((step >= start) & (step < start + pairs // each))
    def _():
        for part in range(each):
            pair = (step - start) * each + part
            cut = pl.ds(pl.multiple_of(pair * 128, 128), 128)
            cross_body(
                cross_live, cq.at[:, cut], keys.at[:, cut], values.at[:, cut], cmix.at[:, cut], clse.at[pl.ds(pair, 1)]
            )

    @on(start + pairs // each)
    def _():
        second_rows(cmix[...], weight_of(8), first[...], vecs, second_sum, second, second_low)
        store(11, 12, 13, 14, 15)

    engine.tick(step)

    for at in range(9):
        @on(at + 4 * GATHER_LAG)
        def _(at=at):
            load(at).start()

    @on(pl.num_programs(0) - 1)
    def _():
        engine.close()
        for at in range(17):
            pltpu.make_async_copy(held[at], outs[at], store_sem.at[at]).wait()


VEC = 5


def forward_beside(cross_live, self_live, tokens, sources, inner, outer, memory):
    count, width = tokens.shape
    slots = memory.shape[0]
    pairs = width // 128
    rows = PAIR * len(sources) + inner.shape[0] * inner.shape[1] // width + outer.shape[0]
    ticks = rows // PAIR
    low, wide = shape(tokens.shape, BF16), shape(tokens.shape, F32)
    large = shape(memory.shape, BF16)
    parts = [
        large, large, low, low, low, low, wide, wide, low, low, shape((128, count), F32),
        low, shape((pairs, 8, count), F32), wide, wide, low, shape((16, width), F32),
    ]
    scalar = pl.BlockSpec(memory_space=pltpu.SMEM)
    hbm = pl.BlockSpec(memory_space=pl.ANY)
    block = (4, 2, 2, 2)
    out = pl.pallas_call(
        forward_body,
        grid=(ticks + 4 * GATHER_LAG + 1,),
        out_shape=[shape(block + (rows, width), BF16)] + parts,
        in_specs=[scalar, scalar, once(tokens.shape)] + [hbm] * (len(sources) + 3),
        out_specs=[hbm] * (1 + len(parts)),
        scratch_shapes=[pltpu.VMEM(part.shape, part.dtype) for part in parts]
        + [pltpu.VMEM((8,) + block + (PAIR, width), BF16), pltpu.VMEM(block + (PAIR, width), BF16), pltpu.VMEM(memory.shape, BF16)]
        + [pltpu.SemaphoreType.DMA((10,)), pltpu.SemaphoreType.DMA((len(parts),))]
        + Gather.scratch(ticks),
        compiler_params=pltpu.CompilerParams(collective_id=0, has_side_effects=True, vmem_limit_bytes=60 * MIB),
        cost_estimate=pl.CostEstimate(flops=6 * slots * width * width, bytes_accessed=90 * MIB, transcendentals=0),
        name="forward_beside_gather",
    )(cross_live, self_live, tokens, *sources, inner, outer, memory)
    return out[0].reshape(BLOCKS, rows, width), out[1:]


def blocks_of(pay):
    return pay.reshape((4, 2, 2) + pay.shape[1:])


def back_body(
    cross_live, self_live, q, k, v, mixture, lse, vecs, slse, third_grads,
    act_in, go_in, low_in, slope_in, gts_in, second_in, sum_in, sq_in, sk_in, sv_in, smix_in, tokens_in, stack,
    dk_o, dv_o, own, dq_o, gci_o, tokens_grad, self_keep, self_send, *scratch,
):
    refs, scratch = scratch[:8], scratch[8:]
    sent, weights, slopes, hidden, gss, second_sum, first_sum, gfs = scratch[:8]
    go, low, gci, gcm, dq, sq, sk, sv, smix, tokens, gsi, gq, gk, gv = scratch[8:22]
    grads, held, staged, load_sem, store_sem = scratch[22:]
    step = pl.program_id(0)
    me = lax.axis_index("dp").astype(jnp.int32)
    engine = Scatter(me, [], refs, own)
    width = dq.shape[1]
    pairs = width // 128
    first_pair = 4
    after = first_pair + pairs

    def load(at, src, dst):
        return pltpu.make_async_copy(src, dst, load_sem.at[at])

    def store(at, src, dst):
        return pltpu.make_async_copy(src, dst, store_sem.at[at])

    act_load, go_load = load(0, act_in, hidden), load(1, go_in, go)
    ffn_loads = [load(2, low_in, low), load(3, gts_in, gss), load(4, second_in, second_sum)]
    self_loads = [
        load(5 + at, src, dst)
        for at, (src, dst) in enumerate(
            [(sum_in, first_sum), (sq_in, sq), (sk_in, sk), (sv_in, sv), (smix_in, smix), (tokens_in, tokens)]
        )
    ]

    def load_slope(part):
        return load(11 + part % 2, slope_in.at[:, pl.ds(part * width, width)], slopes.at[part % 2])

    def load_outer(part):
        return load(13, stack.at[pl.ds(8 * part, 8), pl.ds(128, 128)], weights.at[0].reshape(8, 128, width))

    def load_square(at, slot):
        return load(13 + slot, stack.at[:, pl.ds(at * 32, 32)], weights.at[slot])

    def on(at):
        return pl.when(step == at)

    def swaps(chunks):
        return [engine.swap(p, sent.at[p % (4 * PARTS)]) for p in range(chunks[0] * PARTS, (chunks[-1] + 1) * PARTS)]

    @on(0)
    def _():
        act_load.start()
        go_load.start()
        load_outer(0).start()
        load_square(0, 1).start()
        for part in range(2):
            load_slope(part).start()
        for copy in ffn_loads + self_loads:
            copy.start()
        greet(me)
        act_load.wait()
        go_load.wait()
        for z in range(4):
            group = flip(lax.div(me, 8), z)
            for part in range(4):
                columns = pl.ds(pl.multiple_of(group * 1024 + part * 256, 256), 256)
                held[pl.ds(part * 256, 256), :] = tn(hidden[:, columns], go[...]).astype(BF16)
            for j in range(8):
                row = pl.multiple_of(flip(lax.rem(me, 8), j) * 128, 128)
                for p in range(4):
                    rows = held[pl.ds(row + p * 32, 32), :]
                    engine.put(sent if j % 2 else engine.keep, p, (z, j // 4, (j // 2) % 2), rows)
        for copy in swaps(range(4)):
            copy.start()

    for at in (1, 2):
        @on(at)
        def _(at=at):
            if at == 1:
                for copy in ffn_loads:
                    copy.wait()
            for part in (2 * at - 2, 2 * at - 1):
                load_outer(part).wait()
                grad = nt(go[...], whole(weights.at[0]))
                if part < 3:
                    load_outer(part + 1).start()
                else:
                    load_square(16, 0).start()
                load_slope(part).wait()
                rows = (grad * slopes[part % 2]).astype(BF16)
                if part < 2:
                    load_slope(part + 2).start()
                hidden[:, part * width : part * width + width] = rows
                load_square(part, 1).wait()
                gss[...] += nt(rows, whole(weights.at[1]))
                load_square(part + 1 if part < 3 else 15, 1).start()
            if at == 2:
                grad, gain, shift = norm_back(second_sum[...], vecs[2:3, :], gss[...])
                gss[...] = grad
                rows = grad.astype(BF16)
                gci[...] = rows
                load_square(16, 0).wait()
                gcm[...] = nt(rows, whole(weights.at[0])).astype(BF16)
                load_square(14, 0).start()
                grads[2:3, :] = gain
                grads[3:4, :] = shift
                grads[4:6, :] = third_grads[0:2, :]
                grads[8:32, :] = jnp.zeros((24, width), F32)
                store(0, gci, gci_o).start()

    @on(3)
    def _():
        for copy in swaps(range(4)):
            copy.wait_send()
        for part in range(4):
            for z in range(4):
                held[:256, :] = tn(low[:, group_at(me, z)], hidden[:, part * width : part * width + width]).astype(BF16)

                def put(y, x, c, rows, z=z, part=part):
                    engine.put(sent if c else engine.keep, part if c else 4 + part, (z, y, x), rows)

                weight_blocks(held, me, put)
        for copy in swaps(range(4, 8)):
            copy.start()

    @pl.when((step >= first_pair) & (step < after))
    def _():
        cut = pl.ds(pl.multiple_of((step - first_pair) * 128, 128), 128)
        cross_back_body(cross_live, q, k, v, gcm.at[:, cut], mixture, lse, dq.at[:, cut], dk_o, dv_o)

    @on(after)
    def _():
        store(1, dq, dq_o).start()
        for copy in self_loads:
            copy.wait()
        load_square(15, 1).wait()
        load_square(14, 0).wait()
        self_back_body(
            self_live, gss, dq, weights.at[1], first_sum, weights.at[0], vecs, sq, sk, sv, smix, slse,
            gfs, gsi, gq, gk, gv, second_sum.at[pl.ds(0, 8)],
        )
        grads[0:2, :] = second_sum[0:2, :]
        load_square(10, 0).start()
        load_square(11, 1).start()

    def stores(z):
        return [store(2 + 2 * (z % 2) + c, staged.at[z % 2, c], (self_send if c else self_keep).at[z]) for c in range(2)]

    for z in range(4):
        @on(after + 1 + z // 2)
        def _(z=z):
            if z >= 2:
                for copy in stores(z - 2):
                    copy.wait()
            columns = group_at(me, z)
            for at, (rows, grad) in enumerate([(tokens, gq), (tokens, gk), (tokens, gv), (smix, gsi)]):
                held[:256, :] = tn(rows[:, columns], grad[...]).astype(BF16)

                def put(y, x, c, rows, at=at):
                    staged[z % 2, c, y, x, at * 32 : at * 32 + 32, :] = rows

                weight_blocks(held, me, put)
            rows = grads[...].astype(BF16)
            for y in range(2):
                for x in range(2):
                    for c in range(2):
                        staged[z % 2, c, y, x, 128:160, :] = rows
            for copy in stores(z):
                copy.start()
            if z == 0:
                load_square(10, 0).wait()
                gfs[...] += nt(gq[...], whole(weights.at[0]))
                load_square(12, 0).start()
            if z == 1:
                load_square(11, 1).wait()
                gfs[...] += nt(gk[...], whole(weights.at[1]))
            if z == 2:
                load_square(12, 0).wait()
                gfs[...] += nt(gv[...], whole(weights.at[0]))
                store(6, gfs, tokens_grad).start()

    @pl.when((step < first_pair) | (step >= after) | (lax.rem(step, 2) == 1))
    def _():
        engine.ticks_of(step - jnp.clip(lax.div(step - first_pair + 1, 2), 0, pairs // 2))

    @on(pl.num_programs(0) - 1)
    def _():
        engine.close(4 * PARTS)
        for copy in [store(0, gci, gci_o), store(1, dq, dq_o), store(6, gfs, tokens_grad)] + stores(2) + stores(3):
            copy.wait()


def backward_beside(
    cross_live, self_live, q, k, v, mixture, lse, vecs, slse, third_grads,
    act, go, low, slope, gts, second_sum, first_sum, sq, sk, sv, smix, tokens, stack,
):
    count, width = q.shape
    slots = k.shape[0]
    last = width // 128 - 1

    def pair(i):
        return jnp.clip(i - 4, 0, last)

    ticks = 8
    small = pl.BlockSpec((count, 128), lambda i: (0, pair(i)))
    large = pl.BlockSpec((slots, 128), lambda i: (0, pair(i)))
    scalar = pl.BlockSpec(memory_space=pltpu.SMEM)
    hbm = pl.BlockSpec(memory_space=pl.ANY)
    pay_shape = shape((4, 2, 2, 160, width), BF16)
    wide = pltpu.VMEM(q.shape, F32)
    thin = pltpu.VMEM(q.shape, BF16)
    dk, dv, own, dq, gci, tokens_grad, self_keep, self_send = pl.pallas_call(
        back_body,
        grid=(last + 1 + 7,),
        out_shape=[
            shape(k.shape, BF16), shape(k.shape, BF16), shape((ticks * PAIR, width), F32),
            shape(q.shape, BF16), shape(q.shape, BF16), shape(q.shape, F32), pay_shape, pay_shape,
        ],
        in_specs=[
            scalar, scalar, small, large, large, small, pl.BlockSpec((1, 8, count), lambda i: (pair(i), 0, 0)),
            once(vecs.shape), once(slse.shape), once(third_grads.shape),
        ] + [hbm] * 13,
        out_specs=[large, large, full((ticks * PAIR, width))] + [hbm] * 5,
        scratch_shapes=Scatter.scratch(ticks * PARTS, width // PARTS)
        + [
            pltpu.VMEM((4 * PARTS, 4, 2, 2, PAIR, width // PARTS), BF16), pltpu.VMEM((2, BLOCKS, 32, width), BF16),
            pltpu.VMEM((2, count, width), F32), pltpu.VMEM(act.shape, BF16),
        ]
        + [wide] * 4 + [thin] * 14
        + [
            pltpu.VMEM((32, width), F32), pltpu.VMEM((1024, width), BF16), pltpu.VMEM((2, 2, 2, 2, 160, width), BF16),
            pltpu.SemaphoreType.DMA((15,)), pltpu.SemaphoreType.DMA((7,)),
        ],
        compiler_params=pltpu.CompilerParams(collective_id=1, has_side_effects=True, vmem_limit_bytes=63 * MIB),
        cost_estimate=pl.CostEstimate(flops=70 * count * slots * width, bytes_accessed=80 * MIB, transcendentals=0),
        name="backward_beside_sum",
    )(
        cross_live, self_live, q, k, v, mixture, lse, vecs, slse, third_grads,
        act, go, low, slope, gts, second_sum, first_sum, sq, sk, sv, smix, tokens, stack,
    )
    return dq, dk, dv, gci, tokens_grad, (self_keep, self_send), own


def finish_body(
    first_low, dq, mixture, gci, memory_in, dk_in, dv_in, stack, self_keep, self_send, memory_grad, own, *scratch
):
    refs, (sent, held, memory, dk, dv, weights, load_sem) = scratch[:8], scratch[8:]
    step = pl.program_id(0)
    me = lax.axis_index("dp").astype(jnp.int32)
    engine = Scatter(me, [(self_keep, self_send)], refs, own)
    early = engine.loads // PARTS
    tile = memory_grad.shape[0]
    loads = [
        pltpu.make_async_copy(src, dst, load_sem.at[at])
        for at, (src, dst) in enumerate(
            [(memory_in, memory), (dk_in, dk), (dv_in, dv)]
            + [(stack.at[:, pl.ds((8 + slot) * 32, 32)], weights.at[slot]) for slot in range(2)]
        )
    ]

    def on(at):
        return pl.when(step == at)

    @on(0)
    def _():
        engine.begin()
        for load in loads:
            load.start()

    def weight(w, rows, grad, groups):
        for z in groups:
            held[...] = tn(rows[:, group_at(me, z)], grad[...])

            def put(y, x, c, rows, z=z):
                engine.put(sent if c else engine.keep, w if c else early + w, (z, y, x), rows)

            weight_blocks(held, me, put)

    def swap(w):
        for part in range(PARTS):
            engine.swap((early + w) * PARTS + part, sent.at[w * PARTS + part]).start()

    for w, rows, grad in ((0, first_low, dq), (1, mixture, gci)):
        @on(w)
        def _(w=w, rows=rows, grad=grad):
            weight(w, rows, grad, range(4))
            swap(w)

    for w, rows, grad in ((2, memory, dk), (3, memory, dv)):
        for z in range(4):
            @on((w - 2) * 4 + z + 1)
            def _(w=w, rows=rows, grad=grad, z=z):
                if z == 0:
                    for load in loads[:2] if w == 2 else loads[2:]:
                        load.wait()
                weight(w, rows, grad, (z,))
                if z == 3:
                    swap(w)

    @pl.when((step >= FIRST_TILE) & (step < FIRST_TILE + dk.shape[0] // tile))
    def _():
        at = pl.ds(pl.multiple_of((step - FIRST_TILE) * tile, tile), tile)
        memory_grad[...] = nt(dk[at, :], whole(weights.at[0])) + nt(dv[at, :], whole(weights.at[1]))

    engine.ticks_of(step)

    @on(pl.num_programs(0) - 1)
    def _():
        engine.close()


def finish(memory, dk, dv, first_low, dq, mixture, gci, stack, self_pay):
    slots, width = memory.shape
    tile = 512
    tiles = slots // tile
    ticks = self_pay[0].shape[3] // PAIR + 4
    hbm = pl.BlockSpec(memory_space=pl.ANY)
    square = once(dq.shape)
    large = pltpu.VMEM(memory.shape, BF16)
    return pl.pallas_call(
        finish_body,
        grid=(max(FIRST_TILE + tiles, ticks + -(-3 * LAG // PARTS)),),
        out_shape=[shape(memory.shape, F32), shape((ticks * PAIR, width), F32)],
        in_specs=[square, square, square, square] + [hbm] * 6,
        out_specs=[pl.BlockSpec((tile, width), lambda i: (jnp.clip(i - FIRST_TILE, 0, tiles - 1), 0)), full((ticks * PAIR, width))],
        scratch_shapes=Scatter.scratch(ticks * PARTS, width // PARTS)
        + [pltpu.VMEM((4 * PARTS, 4, 2, 2, PAIR, width // PARTS), BF16), pltpu.VMEM((256, width), F32), large, large, large]
        + [pltpu.VMEM((2, BLOCKS, 32, width), BF16), pltpu.SemaphoreType.DMA((5,))],
        compiler_params=pltpu.CompilerParams(collective_id=2, has_side_effects=True, vmem_limit_bytes=62 * MIB),
        cost_estimate=pl.CostEstimate(flops=8 * slots * width * width, bytes_accessed=60 * MIB, transcendentals=0),
        name="finish_beside_sum",
    )(first_low, dq, mixture, gci, memory, dk, dv, stack, *self_pay)


def unpack_body(memory_in, tokens_in, ffn, owned, memory_grad, tokens_grad, outer, inner, *squares):
    memory_grad[...] = memory_in[...]

    @pl.when(pl.program_id(0) == 0)
    def _():
        width = ffn.shape[1]
        tokens_grad[...] = tokens_in[...]
        outer[...] = ffn[:128, :]
        for part in range(4):
            inner[:, part * width : part * width + width] = ffn[128 + part * 32 : 160 + part * 32, :]
        for at, square in zip(OWNED, squares):
            square[...] = owned[at : at + 32, :]


def unpack(memory_grad, tokens_grad, ffn, owned):
    width = ffn.shape[1]
    tile = 256
    wide = pl.BlockSpec((tile, width), lambda i: (i, 0))
    outs = [(128, width), (32, 4 * width)] + [(32, width)] * len(OWNED)
    return call(
        unpack_body, "unpack",
        [shape(memory_grad.shape, F32), shape(tokens_grad.shape, F32)] + [shape(dims, F32) for dims in outs],
        (memory_grad.shape[0] // tile,),
        [wide, once(tokens_grad.shape), once(ffn.shape), once(owned.shape)],
        [wide, full(tokens_grad.shape)] + [full(dims) for dims in outs],
        flops=0, moved=22 * MIB,
    )(memory_grad, tokens_grad, ffn, owned)


OWNED = (0, 32, 64, 96, 160, 224, 256, 192)


def absolute(keep, send):
    return jnp.stack([keep, send], axis=1).reshape((BLOCKS,) + keep.shape[1:])


def gather(rows):
    return lax.all_gather(rows, "dp", axis=0, tiled=True)


def on_device(
    devices, tokens, memory, target_lengths, memory_lengths, cotangent,
    self_query, self_key, self_value, self_output, first_gain, first_shift,
    cross_query, cross_key, cross_value, cross_output, second_gain, second_shift,
    inner_weight, outer_weight, third_gain, third_shift,
):
    width = tokens.shape[1]
    hidden = inner_weight.shape[1]
    direct = devices == BLOCKS
    squares = [cross_key, cross_value, self_query, self_key, self_value, self_output, cross_query, cross_output]
    vectors = [first_gain, first_shift, second_gain, second_shift, third_gain, third_shift]
    if direct:
        place_of = lax.axis_index("dp").astype(jnp.int32)
        me = place_of.reshape(1)
        own = lax.dynamic_update_slice(jnp.zeros((32, width), BF16), jnp.stack(vectors), (0, place_of * 32))
        stack, parts = forward_beside(
            memory_lengths, target_lengths, tokens, squares[:VEC] + [own] + squares[VEC:], inner_weight, outer_weight, memory
        )
        (keys, values, q, k, v, mixture, first_sum, first_out, first_low, cross_q, lse,
         cross_mixture, cross_lse, second_sum, second, second_low, vecs) = parts
    else:
        me = jnp.zeros((1,), jnp.int32)
        inner_full = gather(inner_weight)
        parts = [inner_full[:, i : i + width].reshape(BLOCKS, 32, width) for i in range(0, hidden, width)]
        parts.append(gather(outer_weight).reshape(BLOCKS, 128, width))
        parts += [gather(w).reshape(BLOCKS, 32, width) for w in squares[:VEC]] + [jnp.zeros((BLOCKS, 32, width), BF16)]
        parts += [gather(w).reshape(BLOCKS, 32, width) for w in squares[VEC:]]
        stack = jnp.concatenate(parts, axis=1)
        vecs = jnp.pad(jnp.stack([gather(v) for v in vectors]), ((0, 10), (0, 0))).astype(F32)
        keys, values = kv_project(memory, stack, 8, 9)
        q, k, v, mixture, first_sum, first_out, first_low, cross_q, lse = self_forward(
            target_lengths, tokens, stack, (10, 11, 12, 14, 15), vecs
        )
        cross_mixture, cross_lse = cross_forward(memory_lengths, cross_q, keys, values)
        second_sum, second, second_low = second_norm(cross_mixture, stack, 16, first_out, vecs)

    act, slope, output_rows, gts, go, third_grads = ffn_forward(second_low, second, stack, cotangent, vecs)
    if direct:
        dq, dk, dv, gci, tokens_grad, self_pay, ffn_own = backward_beside(
            memory_lengths, target_lengths, cross_q, keys, values, cross_mixture, cross_lse, vecs, lse, third_grads,
            act, go, second_low, slope, gts, second_sum, first_sum, q, k, v, mixture, tokens, stack,
        )
        memory_grad, owned = finish(memory, dk, dv, first_low, dq, cross_mixture, gci, stack, self_pay)
        vec_rows = lax.dynamic_slice(owned, (128, me[0] * 32), (6, 32))
        vec_own = [vec_rows[i] for i in range(6)]
        memory_grad, tokens_grad, outer_own, inner_own, *squares_own = unpack(memory_grad, tokens_grad, ffn_own, owned)
        self_own, cross_own = squares_own[:4], squares_own[4:]
    else:
        gi, gss, gci, gcm, second_grads = ffn_backward(go, gts, slope, stack, second_sum, stack, 16, vecs)
        ffn_pay = ffn_weights(me, act, go, second_low, gi)
        dq, dk, dv = cross_backward(memory_lengths, cross_q, keys, values, gcm, cross_mixture, cross_lse)
        cross_pay = square_weights(
            me, [(first_low, dq), (memory, dk), (memory, dv), (cross_mixture, gci)], "cross_weights"
        )
        gfs, gsi, gq, gk, gv, first_grads = self_backward(
            target_lengths, gss, dq, stack, 15, 14, first_sum, vecs, q, k, v, mixture, lse
        )
        self_pay = square_weights(me, [(tokens, gq), (tokens, gk), (tokens, gv), (mixture, gsi)], "self_weights")
        memory_grad = memory_gradient(dk, dv, stack, 8, 9)
        tokens_grad = tokens_gradient(gfs, gq, gk, gv, stack, (10, 11, 12))

        def summed(rows):
            return lax.psum_scatter(rows.astype(F32), "dp", scatter_dimension=0, tiled=True)

        ffn_rows, cross_rows, self_rows = absolute(*ffn_pay), absolute(*cross_pay), absolute(*self_pay)
        outer_own = summed(ffn_rows[:, :128].reshape(-1, width))
        inner_own = summed(
            jnp.concatenate([ffn_rows[:, i : i + 32].reshape(-1, width) for i in range(128, 256, 32)], axis=1)
        )
        cross_own = [summed(cross_rows[:, i : i + 32].reshape(-1, width)) for i in range(0, 128, 32)]
        self_own = [summed(self_rows[:, i : i + 32].reshape(-1, width)) for i in range(0, 128, 32)]
        vec_own = [summed(rows[i]) for rows in (first_grads, second_grads, third_grads) for i in range(2)]

    return (
        output_rows, tokens_grad, memory_grad,
        *self_own, vec_own[0], vec_own[1],
        *cross_own, vec_own[2], vec_own[3],
        inner_own, outer_own, vec_own[4], vec_own[5],
    )


def solution(mesh):
    rows, line = P("dp", None), P("dp")
    block = [rows] * 4 + [line] * 2
    placed = (rows, rows, line, line, rows, *block, *block, rows, rows, line, line)
    return jax.shard_map(
        functools.partial(on_device, mesh.shape["dp"]),
        mesh=mesh,
        in_specs=placed,
        out_specs=(rows, rows, rows, *block, *block, rows, rows, line, line),
        check_vma=False,
    )
```

```python
import functools
import math

import jax
import jax.numpy as jnp
from jax import lax
from jax.experimental import pallas as pl
from jax.experimental.pallas import tpu as pltpu
from jax.sharding import PartitionSpec as P

HEAD = 64
EPS = 1e-05
SCALE = 1.0 / math.sqrt(HEAD)
LOG2E = 1.4426950408889634
BLOCKS = 32
MIB = 1024 * 1024
F32 = jnp.float32
BF16 = jnp.bfloat16
PAIR, HALF = 32, 16
CORE, XBIT, YBIT, NEAR, FAR, BOTH = PARTNERS = (1, 2, 4, 8, 16, 24)
LAG = 2
PARTS = 2
GATHER_LAG = 1
FIRST_TILE = 7


def nn(a, b):
    return jnp.dot(a, b, preferred_element_type=F32)


def nt(a, b):
    return lax.dot_general(a, b, (((1,), (1,)), ((), ())), preferred_element_type=F32)


def tn(a, b):
    return lax.dot_general(a, b, (((0,), (0,)), ((), ())), preferred_element_type=F32)


def whole(ref):
    return ref[...].reshape(-1, ref.shape[-1])


def call(body, name, out, grid=(), ins=None, outs=None, scratch=(), prefetch=0, limit=56, flops=0, moved=0):
    return pl.pallas_call(
        body,
        out_shape=out,
        grid_spec=pltpu.PrefetchScalarGridSpec(
            num_scalar_prefetch=prefetch,
            grid=grid,
            in_specs=ins,
            out_specs=outs,
            scratch_shapes=scratch,
        ),
        compiler_params=pltpu.CompilerParams(vmem_limit_bytes=limit * MIB),
        cost_estimate=pl.CostEstimate(flops=flops, bytes_accessed=moved, transcendentals=0),
        name=name,
    )


def full(shape):
    return pl.BlockSpec(shape, lambda *_: (0,) * len(shape))


def weight(at):
    return pl.BlockSpec((BLOCKS, 32, 1024), lambda *_: (0, at, 0))


def shape(dims, dtype):
    return jax.ShapeDtypeStruct(dims, dtype)


def norm_parts(summed):
    average = jnp.mean(summed, axis=-1, keepdims=True)
    centred = summed - average
    spread = jnp.mean(centred * centred, axis=-1, keepdims=True)
    scale = lax.rsqrt(spread + EPS)
    return centred * scale, scale


def norm_back(summed, gain, upstream):
    normal, scale = norm_parts(summed)
    grad_gain = jnp.sum(upstream * normal, axis=0, keepdims=True)
    grad_shift = jnp.sum(upstream, axis=0, keepdims=True)
    scaled = upstream * gain
    first = jnp.mean(scaled, axis=-1, keepdims=True)
    second = jnp.mean(scaled * normal, axis=-1, keepdims=True)
    return scale * (scaled - first - normal * second), grad_gain, grad_shift


def lanes(rows):
    return lax.broadcasted_iota(jnp.int32, (rows, 128), 1)


def stack_pair(rows):
    low = lanes(rows.shape[0]) < HEAD
    zero = jnp.zeros_like(rows)
    return jnp.concatenate([jnp.where(low, rows, zero), jnp.where(low, zero, rows)], axis=0)


def unstack_pair(stacked):
    half = stacked.shape[0] // 2
    return jnp.where(lanes(half) < HEAD, stacked[:half], stacked[half:])


def pair_forward(stacked, keys, values, mask):
    scores = nt(stacked, keys)
    if mask is not None:
        scores = mask(scores)
    peak = jnp.max(scores, axis=-1, keepdims=True)
    raised = jnp.exp2((scores - peak) * (SCALE * LOG2E))
    total = jnp.sum(raised, axis=-1, keepdims=True)
    mixed = nn(raised.astype(BF16), values) / total
    return mixed, peak * SCALE + jnp.log(total)


def pair_tile_back(q2, g2, keys, values, totals, inner, mask):
    scores = nt(keys, q2)
    probs = jnp.exp2(scores * (SCALE * LOG2E) - totals)
    if mask is not None:
        probs = mask(probs)
    grad_probs = nt(values, g2)
    grad_scores = (probs * (grad_probs - inner)).astype(BF16)
    grad_values = nn(probs.astype(BF16), g2)
    grad_keys = nn(grad_scores, q2) * SCALE
    grad_queries = tn(keys, grad_scores)
    return grad_queries, grad_keys, grad_values


def pair_inner(mixture, grad):
    product = mixture.astype(F32) * grad.astype(F32)
    half = jnp.where(
        (lax.broadcasted_iota(jnp.int32, (8, 128), 1) // HEAD)
        == lax.broadcasted_iota(jnp.int32, (8, 128), 0),
        1.0,
        0.0,
    ).astype(F32)
    sums = lax.dot_general(
        half, product, (((1,), (1,)), ((), ())),
        preferred_element_type=F32, precision=lax.Precision.HIGHEST,
    )
    return jnp.concatenate([sums[0:1], sums[1:2]], axis=1)


def join_grad_queries(grad):
    count = grad.shape[1] // 2
    joined = jnp.concatenate([grad[:HEAD, :count], grad[HEAD:, count:]], axis=0) * SCALE
    return joined.T.astype(BF16)


def kv_body(memory, wk, wv, keys, values):
    rows = memory[...]
    keys[...] = nn(rows, whole(wk)).astype(BF16)
    values[...] = nn(rows, whole(wv)).astype(BF16)


def kv_project(memory, stack, at_k, at_v):
    count, width = memory.shape
    tile = 512
    spec = pl.BlockSpec((tile, width), lambda i: (i, 0))
    return call(
        kv_body, "cross_kv", [shape(memory.shape, BF16)] * 2, (count // tile,),
        [spec, weight(at_k), weight(at_v)], [spec, spec],
        flops=4 * count * width * width, moved=12 * MIB + 4 * MIB,
    )(memory, stack, stack)


def self_attention(live, q_o, k_o, v_o, mix_o, lse_o):
    count, width = q_o.shape
    at_q = lax.rem(lax.broadcasted_iota(jnp.int32, (2 * count, count), 0), count)
    at_k = lax.broadcasted_iota(jnp.int32, (2 * count, count), 1)
    allowed = (at_k <= at_q) & (at_k < live)
    column = lanes(count)
    totals = jnp.zeros((count, 128), F32)
    for pair in range(width // 128):
        cut = slice(pair * 128, pair * 128 + 128)
        mixed, log_total = pair_forward(
            stack_pair(q_o[:, cut]), k_o[:, cut], v_o[:, cut],
            lambda scores: jnp.where(allowed, scores, -1e30),
        )
        mix_o[:, cut] = unstack_pair(mixed).astype(BF16)
        totals = jnp.where(column == 2 * pair, log_total[:count], totals)
        totals = jnp.where(column == 2 * pair + 1, log_total[count:], totals)
    lse_o[...] = totals.T


def self_body(length, tokens, wq, wk, wv, wo, wcq, vecs, q_o, k_o, v_o, mix_o, sum_o, first_o, low_o, cq_o, lse_o):
    rows = tokens[...]
    count, width = rows.shape
    q_o[...] = nn(rows, whole(wq)).astype(BF16)
    k_o[...] = nn(rows, whole(wk)).astype(BF16)
    v_o[...] = nn(rows, whole(wv)).astype(BF16)
    self_attention(length[0], q_o, k_o, v_o, mix_o, lse_o)
    summed = rows.astype(F32) + nn(mix_o[...], whole(wo))
    sum_o[...] = summed
    normal, _ = norm_parts(summed)
    first = normal * vecs[0:1] + vecs[1:2]
    first_o[...] = first
    low = first.astype(BF16)
    low_o[...] = low
    cq_o[...] = nn(low, whole(wcq)).astype(BF16)


def self_forward(length, tokens, stack, at, vecs):
    count, width = tokens.shape
    low = shape(tokens.shape, BF16)
    wide = shape(tokens.shape, F32)
    spec = full(tokens.shape)
    return call(
        self_body, "self_forward",
        [low, low, low, low, wide, wide, low, low, shape((128, count), F32)], (1,),
        [spec] + [weight(k) for k in at] + [full(vecs.shape)],
        [spec] * 8 + [full((128, count))], prefetch=1,
        flops=10 * count * width * width, moved=16 * MIB,
    )(length, tokens, stack, stack, stack, stack, stack, vecs)


def cross_body(length, q, k, v, mix_o, lse_o):
    count = q.shape[0]
    slots = k.shape[0]
    live = length[0]
    q2 = stack_pair(q[...])
    keys = k[...]
    values = v[...]
    half = slots // 2
    tile = 128
    column = lax.broadcasted_iota(jnp.int32, (tile, slots - half), 1) + half

    def mask(scores):
        upper = jnp.where(column < live, scores[:, half:], -1e30)
        return jnp.concatenate([scores[:, :half], upper], axis=1)

    mixes, logs = [], []
    for at in range(0, 2 * count, tile):
        mixed, log_total = pair_forward(q2[at : at + tile], keys, values, mask)
        mixes.append(mixed)
        logs.append(log_total)
    mix_o[...] = unstack_pair(jnp.concatenate(mixes, axis=0)).astype(BF16)
    logs = jnp.concatenate(logs, axis=0)
    column = lanes(count)
    totals = jnp.where(column == 0, logs[:count], jnp.where(column == 1, logs[count:], 0.0))
    lse_o[0] = totals.T[:8]


def cross_forward(length, q, k, v):
    count, width = q.shape
    slots = k.shape[0]
    pairs = width // 128
    return call(
        cross_body, "cross_forward",
        [shape(q.shape, BF16), shape((pairs, 8, count), F32)], (pairs,),
        [pl.BlockSpec((count, 128), lambda i, _: (0, i))]
        + [pl.BlockSpec((slots, 128), lambda i, _: (0, i))] * 2,
        [pl.BlockSpec((count, 128), lambda i, _: (0, i)), pl.BlockSpec((1, 8, count), lambda i, _: (i, 0, 0))],
        prefetch=1, flops=16 * count * slots * width, moved=10 * MIB,
    )(length, q, k, v)


def second_rows(mixture, wo, first, vecs, sum_o, second_o, low_o):
    summed = first + nn(mixture, wo)
    sum_o[...] = summed
    normal, _ = norm_parts(summed)
    second = normal * vecs[2:3, :] + vecs[3:4, :]
    second_o[...] = second
    low_o[...] = second.astype(BF16)


def second_body(mixture, wo, first, vecs, sum_o, second_o, low_o):
    second_rows(mixture[...], whole(wo), first[...], vecs, sum_o, second_o, low_o)


def second_norm(mixture, stack, at, first, vecs):
    spec = full(mixture.shape)
    return call(
        second_body, "second_norm",
        [shape(mixture.shape, F32), shape(mixture.shape, F32), shape(mixture.shape, BF16)], (1,),
        [spec, weight(at), spec, full(vecs.shape)], [spec] * 3,
        flops=MIB * 512, moved=6 * MIB,
    )(mixture, stack, first, vecs)


def erf(x):
    return lax.erf(x)


def ffn_body(low, second, inner, outer, cot, vecs, act_o, slope_o, out_o, gts_o, go_o, grads_o, total):
    step = pl.program_id(0)
    pre = nn(low[...], whole(inner))
    half = 0.5 * (1.0 + erf(pre * math.sqrt(0.5)))
    active = (pre * half).astype(BF16)
    act_o[...] = active
    slope_o[...] = half + pre * (jnp.exp(-0.5 * pre * pre) * (1.0 / math.sqrt(2.0 * math.pi)))
    part = nn(active, whole(outer))

    @pl.when(step == 0)
    def _():
        total[...] = second[...] + part

    @pl.when(step > 0)
    def _():
        total[...] += part

    @pl.when(step == pl.num_programs(0) - 1)
    def _():
        summed = total[...]
        normal, _ = norm_parts(summed)
        out_o[...] = (normal * vecs[4:5] + vecs[5:6]).astype(BF16)
        grad, gain, shift = norm_back(summed, vecs[4:5], cot[...].astype(F32))
        gts_o[...] = grad
        go_o[...] = grad.astype(BF16)
        grads_o[...] = jnp.concatenate([gain, shift] + [jnp.zeros_like(gain)] * 6, axis=0)


def ffn_forward(low, second, stack, cot, vecs):
    count, width = low.shape
    spec = full(low.shape)
    wide = pl.BlockSpec((count, 1024), lambda i: (0, i))
    return call(
        ffn_body, "ffn_forward",
        [shape((count, 4096), BF16), shape((count, 4096), F32), shape(low.shape, BF16), shape(low.shape, F32), shape(low.shape, BF16), shape((8, width), F32)],
        (4,),
        [spec, spec, pl.BlockSpec((BLOCKS, 32, 1024), lambda i: (0, i, 0)), pl.BlockSpec((8, 128, 1024), lambda i: (i, 1, 0)), spec, full(vecs.shape)],
        [wide, wide, spec, spec, spec, full((8, width))],
        scratch=[pltpu.VMEM(low.shape, F32)],
        flops=16 * count * width * width, moved=24 * MIB,
    )(low, second, stack, stack, cot, vecs)


def ffn_back_body(go, gts, slope, inner, outer, summed, wo, vecs, gi_o, gss_o, gci_o, gcm_o, grads_o, total):
    step = pl.program_id(0)
    grad = nt(go[...], whole(outer))
    low = (grad * slope[...]).astype(BF16)
    gi_o[...] = low
    part = nt(low, whole(inner))

    @pl.when(step == 0)
    def _():
        total[...] = gts[...] + part

    @pl.when(step > 0)
    def _():
        total[...] += part

    @pl.when(step == pl.num_programs(0) - 1)
    def _():
        grad, gain, shift = norm_back(summed[...], vecs[2:3], total[...])
        gss_o[...] = grad
        low = grad.astype(BF16)
        gci_o[...] = low
        gcm_o[...] = nt(low, whole(wo)).astype(BF16)
        grads_o[...] = jnp.concatenate([gain, shift] + [jnp.zeros_like(gain)] * 6, axis=0)


def ffn_backward(go, gts, slope, stack, summed, squares, at, vecs):
    count, width = go.shape
    spec = full(go.shape)
    wide = pl.BlockSpec((count, 1024), lambda i: (0, i))
    low = shape(go.shape, BF16)
    return call(
        ffn_back_body, "ffn_backward",
        [shape((count, 4096), BF16), shape(go.shape, F32), low, low, shape((8, width), F32)],
        (4,),
        [spec, spec, wide, pl.BlockSpec((BLOCKS, 32, 1024), lambda i: (0, i, 0)), pl.BlockSpec((8, 128, 1024), lambda i: (i, 1, 0)), spec, weight(at), full(vecs.shape)],
        [wide, spec, spec, spec, full((8, width))],
        scratch=[pltpu.VMEM(go.shape, F32)],
        flops=18 * count * width * width, moved=26 * MIB,
    )(go, gts, slope, stack, stack, summed, squares, vecs)


def cross_back_body(length, q, k, v, g, mixture, lse, dq_o, dk_o, dv_o):
    live = length[0]
    slots = k.shape[0]
    count = q.shape[0]
    q2 = stack_pair(q[...])
    g2 = stack_pair(g[...])
    totals = jnp.concatenate([lse[0, 0:1], lse[0, 1:2]], axis=1) * LOG2E
    inner = pair_inner(mixture[...], g[...])
    tile = 256
    grad_q = jnp.zeros((128, 2 * count), F32)
    for at in range(0, slots, tile):
        mask = None
        if at + tile > slots // 2:
            row = lax.broadcasted_iota(jnp.int32, (tile, 2 * count), 0) + at

            def mask(probs, row=row):
                return jnp.where(row < live, probs, 0.0)

        cut = slice(at, at + tile)
        dq, dk, dv = pair_tile_back(q2, g2, k[cut], v[cut], totals, inner, mask)
        grad_q = grad_q + dq
        dk_o[cut] = dk.astype(BF16)
        dv_o[cut] = dv.astype(BF16)
    dq_o[...] = join_grad_queries(grad_q)


def cross_backward(length, q, k, v, g, mixture, lse):
    count, width = q.shape
    slots = k.shape[0]
    pairs = width // 128
    small = pl.BlockSpec((count, 128), lambda i, _: (0, i))
    large = pl.BlockSpec((slots, 128), lambda i, _: (0, i))
    return call(
        cross_back_body, "cross_backward",
        [shape(q.shape, BF16), shape(k.shape, BF16), shape(k.shape, BF16)], (pairs,),
        [small, large, large, small, small, pl.BlockSpec((1, 8, count), lambda i, _: (i, 0, 0))],
        [small, large, large], prefetch=1,
        flops=40 * count * slots * width, moved=18 * MIB,
    )(length, q, k, v, g, mixture, lse)


def memory_grad_body(dk, dv, wk, wv, out):
    out[...] = nt(dk[...], whole(wk)) + nt(dv[...], whole(wv))


def memory_gradient(dk, dv, stack, at_k, at_v):
    count, width = dk.shape
    tile = 512
    spec = pl.BlockSpec((tile, width), lambda i: (i, 0))
    return call(
        memory_grad_body, "memory_grad", shape(dk.shape, F32), (count // tile,),
        [spec, spec, weight(at_k), weight(at_v)], spec,
        flops=4 * count * width * width, moved=20 * MIB,
    )(dk, dv, stack, stack)


def self_back_body(length, gss, dcq, wcq, summed, wo, vecs, q, k, v, mixture, lse, gfs_o, gsi_o, gq_o, gk_o, gv_o, grads_o):
    live = length[0]
    count, width = gss.shape
    upstream = gss[...] + nt(dcq[...], whole(wcq))
    grad, gain, shift = norm_back(summed[...], vecs[0:1], upstream)
    gfs_o[...] = grad
    grads_o[...] = jnp.concatenate([gain, shift] + [jnp.zeros_like(gain)] * 6, axis=0)
    low = grad.astype(BF16)
    gsi_o[...] = low
    mix_grad = nt(low, whole(wo)).astype(BF16)
    at_k = lax.broadcasted_iota(jnp.int32, (count, 2 * count), 0)
    at_q = lax.rem(lax.broadcasted_iota(jnp.int32, (count, 2 * count), 1), count)
    allowed = (at_k <= at_q) & (at_k < live)
    for pair in range(width // 128):
        cut = slice(pair * 128, pair * 128 + 128)
        g = mix_grad[:, cut]
        totals = jnp.concatenate([lse[2 * pair : 2 * pair + 1], lse[2 * pair + 1 : 2 * pair + 2]], axis=1) * LOG2E
        scores_back = pair_tile_back(
            stack_pair(q[:, cut]), stack_pair(g), k[:, cut], v[:, cut], totals,
            pair_inner(mixture[:, cut], g),
            lambda probs: jnp.where(allowed, probs, 0.0),
        )
        dq, dk, dv = scores_back
        gq_o[:, cut] = join_grad_queries(dq)
        gk_o[:, cut] = dk.astype(BF16)
        gv_o[:, cut] = dv.astype(BF16)


def self_backward(length, gss, dcq, stack, at_cq, at_o, summed, vecs, q, k, v, mixture, lse):
    count, width = q.shape
    spec = full(q.shape)
    low = shape(q.shape, BF16)
    return call(
        self_back_body, "self_backward",
        [shape(q.shape, F32), low, low, low, low, shape((8, width), F32)], (1,),
        [spec, spec, weight(at_cq), spec, weight(at_o), full(vecs.shape), spec, spec, spec, spec, full(lse.shape)],
        [spec] * 5 + [full((8, width))], prefetch=1,
        flops=8 * count * width * width, moved=12 * MIB,
    )(length, gss, dcq, stack, summed, stack, vecs, q, k, v, mixture, lse)


def tokens_grad_body(gfs, gq, gk, gv, wq, wk, wv, out):
    out[...] = gfs[...] + nt(gq[...], whole(wq)) + nt(gk[...], whole(wk)) + nt(gv[...], whole(wv))


def tokens_gradient(gfs, gq, gk, gv, stack, at):
    spec = full(gfs.shape)
    return call(
        tokens_grad_body, "tokens_grad", shape(gfs.shape, F32), (1,),
        [spec] * 4 + [weight(k) for k in at], spec,
        flops=6 * MIB * 256, moved=10 * MIB,
    )(gfs, gq, gk, gv, stack, stack, stack)


def place(keep, send, at, size, pieces, me):
    low = lax.rem(me, 8)
    for j in range(8):
        rows = pieces(lax.bitwise_xor(low, j))
        target = send if j % 2 else keep
        target[j // 2, at : at + size, :] = rows.astype(BF16)


def group_of(step, me):
    return lax.bitwise_xor(step, lax.div(me[0], 8))


def payload(rows, width):
    out = [shape((16, rows, width), BF16)] * 2
    spec = [pl.BlockSpec((4, rows, width), lambda i, _: (i, 0, 0))] * 2
    return out, spec


def ffn_weights_body(me, act, go, low, gi, keep, send, held):
    step = pl.program_id(0)

    @pl.when(step < 4)
    def _():
        held[...] = tn(act[...], go[...])
        place(keep, send, 0, 128, lambda d: held[pl.ds(pl.multiple_of(d * 128, 128), 128), :], me[0])

    @pl.when(step >= 4)
    def _():
        for part in range(4):
            held[:256, :] = tn(low[...], gi[:, part * 1024 : part * 1024 + 1024])
            place(keep, send, part * 32, 32, lambda d: held[pl.ds(pl.multiple_of(d * 32, 32), 32), :], me[0])


def ffn_weights(me, act, go, low, gi):
    count, width = go.shape
    spec = pl.BlockSpec((4, 128, width), lambda i, me: (lax.rem(i, 4), lax.div(i, 4), 0))
    return call(
        ffn_weights_body, "ffn_weights", [shape((16, 256, width), BF16)] * 2, (8,),
        [
            pl.BlockSpec((count, 1024), lambda i, me: (0, group_of(jnp.minimum(i, 3), me))),
            full(go.shape),
            pl.BlockSpec((count, 256), lambda i, me: (0, group_of(jnp.maximum(i - 4, 0), me))),
            full(gi.shape),
        ],
        [spec, spec], [pltpu.VMEM((1024, width), F32)], 1,
        flops=16 * count * width * width, moved=22 * MIB,
    )(me, act, go, low, gi)


def square_body(me, *refs):
    count = (len(refs) - 3) // 2
    keep, send, held = refs[-3:]
    for at in range(count):
        held[...] = tn(refs[2 * at][...], refs[2 * at + 1][...])
        place(keep, send, at * 32, 32, lambda d: held[pl.ds(pl.multiple_of(d * 32, 32), 32), :], me[0])


def square_weights(me, pairs, name):
    width = pairs[0][0].shape[1]
    out, spec = payload(128, width)
    ins, operands, flops = [], [], 0
    for rows, grads in pairs:
        ins.append(pl.BlockSpec((rows.shape[0], 256), lambda i, me: (0, group_of(i, me))))
        ins.append(full(grads.shape))
        operands += [rows, grads]
        flops += 2 * rows.shape[0] * width * width
    return call(
        square_body, name, out, (4,), ins, spec,
        [pltpu.VMEM((256, width), F32)], 1, flops=flops, moved=20 * MIB,
    )(me, *operands)


def flip(me, bits):
    for bit in (1, 2, 4, 8, 16):
        if bits & bit:
            me = me + bit - 2 * bit * lax.rem(lax.div(me, bit), 2)
    return me


def remote(src, dst, out_sem, in_sem, to):
    return pltpu.make_async_remote_copy(
        src_ref=src, dst_ref=dst, send_sem=out_sem, recv_sem=in_sem,
        device_id=(to,), device_id_type=pl.DeviceIdType.MESH,
    )


def greet(me):
    barrier = pltpu.get_barrier_semaphore()
    for bit in PARTNERS:
        pl.semaphore_signal(barrier, inc=1, device_id=(flip(me, bit),), device_id_type=pl.DeviceIdType.MESH)
    pl.semaphore_wait(barrier, len(PARTNERS))


class Scatter:
    def __init__(self, me, pays, refs, out, swapped=0):
        self.me, self.pays, self.out, self.swapped = me, pays, out, swapped
        (self.keep, self.came0, self.came1, self.came2, self.came3,
         self.load_sem, self.out_sem, self.in_sem) = refs
        self.ticks = self.keep.shape[0]
        self.loads = sum(kept.shape[3] for kept, _ in pays) // PAIR * PARTS
        self.part_width = self.keep.shape[5]

    @staticmethod
    def scratch(ticks, width):
        def held(*dims):
            return pltpu.VMEM((ticks,) + dims + (width,), BF16)

        return [
            held(4, 2, 2, PAIR), held(4, 2, 2, PAIR), held(2, 4, 2, HALF), held(2, 4, HALF), held(3, PAIR),
            pltpu.SemaphoreType.DMA((ticks,)), pltpu.SemaphoreType.DMA((8, ticks)), pltpu.SemaphoreType.DMA((8, ticks)),
        ]

    def link(self, stage, p, src, dst, bit):
        return remote(src, dst, self.out_sem.at[stage, p], self.in_sem.at[stage, p], flip(self.me, bit))

    def load(self, p, kept, at):
        return pltpu.make_async_copy(
            kept.at[:, :, :, pl.ds(at, PAIR), pl.ds((p % PARTS) * self.part_width, self.part_width)], self.keep.at[p], self.load_sem.at[p]
        )

    def loaded(self, p):
        return pltpu.make_async_copy(self.came0.at[p], self.keep.at[p], self.load_sem.at[p])

    def put(self, target, p, block, rows):
        for part in range(PARTS):
            target.at[(p * PARTS + part, *block)][...] = rows[:, part * self.part_width : (part + 1) * self.part_width]

    def swap(self, p, sent):
        return self.link(0, p, sent, self.came0.at[p], CORE)

    def hop(self, stage, p):
        keep, up, down = self.keep, pl.ds(0, HALF), pl.ds(HALF, HALF)
        if stage == 1:
            return self.link(1, p, keep.at[p, :, :, 1, up], self.came1.at[p, 0], XBIT)
        if stage == 2:
            return self.link(2, p, keep.at[p, :, 1, :, down], self.came1.at[p, 1], YBIT)
        if stage == 3:
            return self.link(3, p, keep.at[p, :, 1, 0, up], self.came2.at[p, 0], YBIT)
        if stage == 4:
            return self.link(4, p, keep.at[p, :, 0, 1, down], self.came2.at[p, 1], XBIT)
        z = stage - 4
        return self.link(stage, p, keep.at[p, z, 0, 0], self.came3.at[p, z - 1], (NEAR, FAR, BOTH)[z - 1])

    def begin(self):
        greet(self.me)
        p = 0
        for kept, sent in self.pays:
            for at in range(0, kept.shape[3] * PARTS, PAIR):
                row = at // (PAIR * PARTS) * PAIR
                self.load(p, kept, row).start()
                cut = pl.ds((p % PARTS) * self.part_width, self.part_width)
                self.swap(p, sent.at[:, :, :, pl.ds(row, PAIR), cut]).start()
                p += 1

    def total(self, p, z, y, x, h, depth):
        cut = slice(h * HALF, h * HALF + HALF)
        sum_ = self.keep[p, z, y, x, cut, :].astype(F32) + self.came0[p, z, y, x, cut, :].astype(F32)
        if depth > 1:
            sum_ = sum_ + self.came1[p, h, z, y if h == 0 else x].astype(F32)
        if depth > 2:
            sum_ = sum_ + self.came2[p, h, z].astype(F32)
        if depth > 3:
            for other in range(3):
                sum_ = sum_ + self.came3[p, other, cut, :].astype(F32)
        return sum_

    def sums(self, p, blocks, h, depth):
        for z, y, x in blocks:
            self.keep[p, z, y, x, h * HALF : h * HALF + HALF, :] = self.total(p, z, y, x, h, depth).astype(BF16)

    def ticks_of(self, t):
        def one(i, _):
            self.tick(t * PARTS + i)
            return 0

        lax.fori_loop(0, PARTS, one, 0)

    def tick(self, t):
        ticks = self.ticks

        def stage(at):
            return pl.when((t >= at * LAG) & (t < ticks + at * LAG))

        if self.pays:
            @pl.when((t >= 0) & (t < self.loads))
            def _():
                self.loaded(t).wait()

        @stage(0)
        def _():
            self.swap(t, self.came0.at[t]).wait_recv()
            self.sums(t, [(z, y, 1) for z in range(4) for y in range(2)], 0, 1)
            self.hop(1, t).start()
            self.sums(t, [(z, 1, x) for z in range(4) for x in range(2)], 1, 1)
            self.hop(2, t).start()

        @stage(1)
        def _():
            p = t - 1 * LAG
            self.hop(1, p).wait_recv()
            self.sums(p, [(z, 1, 0) for z in range(4)], 0, 2)
            self.hop(3, p).start()
            self.hop(2, p).wait_recv()
            self.sums(p, [(z, 0, 1) for z in range(4)], 1, 2)
            self.hop(4, p).start()

        @stage(2)
        def _():
            p = t - 2 * LAG
            self.hop(3, p).wait_recv()
            self.hop(4, p).wait_recv()
            for z in (2, 3, 1):
                for h in range(2):
                    self.sums(p, [(z, 0, 0)], h, 3)
                self.hop(4 + z, p).start()

        @stage(3)
        def _():
            p = t - 3 * LAG
            for z in (1, 2, 3):
                self.hop(4 + z, p).wait_recv()
            for z in range(1, 8):
                self.hop(z, p).wait_send()

            @pl.when(p >= self.swapped)
            def _():
                self.swap(p, self.came0.at[p]).wait_send()

            for h in range(2):
                at = pl.ds(pl.multiple_of(lax.div(p, PARTS) * PAIR + h * HALF, HALF), HALF)
                cut = pl.ds(pl.multiple_of(lax.rem(p, PARTS) * self.part_width, 128), self.part_width)
                self.out[at, cut] = self.total(p, 0, 0, 0, h, 4)


def weight_blocks(held, me, store):
    low = lax.rem(me, 8)
    for j in range(8):
        rows = held[pl.ds(pl.multiple_of(flip(low, j) * 32, 32), 32), :].astype(BF16)
        store(j // 4, (j // 2) % 2, j % 2, rows)


def group_at(me, z):
    high = flip(lax.div(me, 8), z)
    return pl.ds(pl.multiple_of(high * 256, 256), 256)


def once(dims):
    return pl.BlockSpec(dims, lambda *_: (0,) * len(dims), pipeline_mode=pl.Buffered(1))


def weight_once(at):
    return pl.BlockSpec((BLOCKS, 32, 1024), lambda *_: (0, at, 0), pipeline_mode=pl.Buffered(1))


class Gather:
    def __init__(self, me, g, shift, own, own_sem, local_sem, out_sem, in_sem):
        self.me, self.g, self.shift, self.own = me, g, shift, own
        self.own_sem, self.local_sem, self.out_sem, self.in_sem = own_sem, local_sem, out_sem, in_sem
        self.c, self.x, self.y = [lax.rem(lax.div(me, bit), 2) for bit in (CORE, XBIT, YBIT)]
        self.z = lax.div(me, NEAR)
        self.ticks = g.shape[4] // PAIR

    @staticmethod
    def scratch(ticks, width):
        return [pltpu.VMEM((ticks, PAIR, width), BF16)] + [pltpu.SemaphoreType.DMA((ticks,))] * 2 + [pltpu.SemaphoreType.DMA((8, ticks)), pltpu.SemaphoreType.DMA((8, ticks))]

    def rows(self, p):
        return pl.ds(pl.multiple_of(lax.rem(p + self.shift, self.ticks) * PAIR, PAIR), PAIR)

    def half(self, p, h):
        return pl.ds(pl.multiple_of(lax.rem(p + self.shift, self.ticks) * PAIR + h * HALF, HALF), HALF)

    def mine(self, p):
        return self.g.at[self.z, self.y, self.x, self.c, self.rows(p)]

    def load(self, p, src):
        return pltpu.make_async_copy(src, self.own.at[p], self.own_sem.at[p])

    def local(self, p):
        return pltpu.make_async_copy(self.own.at[p], self.mine(p), self.local_sem.at[p])

    def hop(self, stage, p):
        g, every = self.g, slice(None)
        if stage < 3:
            to = flip(self.me, (NEAR, FAR, BOTH)[stage])
            return remote(self.own.at[p], self.mine(p), self.out_sem.at[stage, p], self.in_sem.at[stage, p], to)
        if stage == 3:
            ref, bits = g.at[every, self.y, self.x, self.c, self.half(p, 0)], XBIT
        elif stage == 4:
            ref, bits = g.at[every, self.y, self.x, self.c, self.half(p, 1)], YBIT
        elif stage == 5:
            ref, bits = g.at[every, self.y, every, self.c, self.half(p, 0)], YBIT
        elif stage == 6:
            ref, bits = g.at[every, every, self.x, self.c, self.half(p, 1)], XBIT
        else:
            ref, bits = g.at[every, every, every, self.c, self.rows(p)], CORE
        return remote(ref, ref, self.out_sem.at[stage, p], self.in_sem.at[stage, p], flip(self.me, bits))

    def begin(self, sources):
        for p, src in enumerate(sources):
            self.load(p, src).start()
        greet(self.me)

    def tick(self, t):
        def stage(at):
            return pl.when((t >= at * GATHER_LAG) & (t < self.ticks + at * GATHER_LAG))

        @stage(0)
        def _():
            self.load(t, self.mine(t)).wait()
            for k in (1, 2, 0):
                self.hop(k, t).start()
            self.local(t).start()

        @stage(1)
        def _():
            p = t - GATHER_LAG
            for k in range(3):
                self.hop(k, p).wait_recv()
            self.local(p).wait()
            self.hop(3, p).start()
            self.hop(4, p).start()

        @stage(2)
        def _():
            p = t - 2 * GATHER_LAG
            self.hop(3, p).wait_recv()
            self.hop(5, p).start()
            self.hop(4, p).wait_recv()
            self.hop(6, p).start()

        @stage(3)
        def _():
            p = t - 3 * GATHER_LAG
            self.hop(5, p).wait_recv()
            self.hop(6, p).wait_recv()
            self.hop(7, p).start()

        @stage(4)
        def _():
            p = t - 4 * GATHER_LAG
            self.hop(7, p).wait_recv()
            for k in range(8):
                self.hop(k, p).wait_send()


def forward_body(cross_live, self_live, tokens, *refs):
    sources, (inner, outer, memory_in), g = refs[:9], refs[9:12], refs[12]
    outs, held = refs[13:30], refs[30:47]
    weights, vec_rows, memory, load_sem, store_sem = refs[47:52]
    keys, values, q, k, v, mix, summed, first, low, cq, lse, cmix, clse, second_sum, second, second_low, vecs = held
    step = pl.program_id(0)
    me = lax.axis_index("dp").astype(jnp.int32)
    engine = Gather(me, g, 8, *refs[52:])
    count, width = tokens.shape
    pairs = width // 128
    ready = 4 * GATHER_LAG + 1

    def load(at):
        every = slice(None)
        target = vec_rows if at == VEC else weights.at[at if at < VEC else at - 1]
        return pltpu.make_async_copy(g.at[every, every, every, every, engine.rows(at)], target, load_sem.at[at])

    def weight_of(at):
        load(at).wait()
        return weights[at if at < VEC else at - 1].reshape(width, width)

    def load_memory():
        return pltpu.make_async_copy(memory_in, memory, load_sem.at[9])

    def store(*which):
        for at in which:
            pltpu.make_async_copy(held[at], outs[at], store_sem.at[at]).start()

    def on(at):
        return pl.when(step == at)

    @on(0)
    def _():
        load_memory().start()
        parts = [inner.at[:, pl.ds(i, width)] for i in range(0, inner.shape[1], width)]
        parts += [outer.at[pl.ds(i, PAIR)] for i in range(0, outer.shape[0], PAIR)]
        engine.begin(list(sources) + parts)

    tile = 512

    @on(ready)
    def _():
        load_memory().wait()
        factor = weight_of(0)
        for at in range(0, memory.shape[0], tile):
            keys[at : at + tile, :] = nn(memory[at : at + tile, :], factor).astype(BF16)
        store(0)

    @on(ready + 1)
    def _():
        factor = weight_of(1)
        for at in range(0, memory.shape[0], tile):
            values[at : at + tile, :] = nn(memory[at : at + tile, :], factor).astype(BF16)
        store(1)

    for at, rows in ((2, q), (3, k), (4, v)):
        @on(ready + at)
        def _(at=at, rows=rows):
            rows[...] = nn(tokens[...], weight_of(at)).astype(BF16)
            store(at)

    @on(ready + VEC)
    def _():
        load(VEC).wait()
        total = jnp.zeros((16, width), F32)
        for z in range(4):
            for y in range(2):
                for x in range(2):
                    for c in range(2):
                        total = total + vec_rows[z, y, x, c, :16, :].astype(F32)
        vecs[...] = total
        self_attention(self_live[0], q, k, v, mix, lse)
        store(16, 5, 10)

    @on(ready + 6)
    def _():
        total = tokens[...].astype(F32) + nn(mix[...], weight_of(6))
        summed[...] = total
        normal, _ = norm_parts(total)
        rows = normal * vecs[0:1, :] + vecs[1:2, :]
        first[...] = rows
        low[...] = rows.astype(BF16)
        store(6, 7, 8)

    @on(ready + 7)
    def _():
        cq[...] = nn(low[...], weight_of(7)).astype(BF16)
        store(9)

    each = 2
    start = ready + 8

    @pl.when((step >= start) & (step < start + pairs // each))
    def _():
        for part in range(each):
            pair = (step - start) * each + part
            cut = pl.ds(pl.multiple_of(pair * 128, 128), 128)
            cross_body(
                cross_live, cq.at[:, cut], keys.at[:, cut], values.at[:, cut], cmix.at[:, cut], clse.at[pl.ds(pair, 1)]
            )

    @on(start + pairs // each)
    def _():
        second_rows(cmix[...], weight_of(8), first[...], vecs, second_sum, second, second_low)
        store(11, 12, 13, 14, 15)

    engine.tick(step)

    for at in range(9):
        @on(at + 4 * GATHER_LAG)
        def _(at=at):
            load(at).start()

    @on(pl.num_programs(0) - 1)
    def _():
        for at in range(17):
            pltpu.make_async_copy(held[at], outs[at], store_sem.at[at]).wait()


VEC = 5


def forward_beside(cross_live, self_live, tokens, sources, inner, outer, memory):
    count, width = tokens.shape
    slots = memory.shape[0]
    pairs = width // 128
    rows = PAIR * len(sources) + inner.shape[0] * inner.shape[1] // width + outer.shape[0]
    ticks = rows // PAIR
    low, wide = shape(tokens.shape, BF16), shape(tokens.shape, F32)
    large = shape(memory.shape, BF16)
    parts = [
        large, large, low, low, low, low, wide, wide, low, low, shape((128, count), F32),
        low, shape((pairs, 8, count), F32), wide, wide, low, shape((16, width), F32),
    ]
    scalar = pl.BlockSpec(memory_space=pltpu.SMEM)
    hbm = pl.BlockSpec(memory_space=pl.ANY)
    block = (4, 2, 2, 2)
    out = pl.pallas_call(
        forward_body,
        grid=(ticks + 4 * GATHER_LAG + 1,),
        out_shape=[shape(block + (rows, width), BF16)] + parts,
        in_specs=[scalar, scalar, once(tokens.shape)] + [hbm] * (len(sources) + 3),
        out_specs=[hbm] * (1 + len(parts)),
        scratch_shapes=[pltpu.VMEM(part.shape, part.dtype) for part in parts]
        + [pltpu.VMEM((8,) + block + (PAIR, width), BF16), pltpu.VMEM(block + (PAIR, width), BF16), pltpu.VMEM(memory.shape, BF16)]
        + [pltpu.SemaphoreType.DMA((10,)), pltpu.SemaphoreType.DMA((len(parts),))]
        + Gather.scratch(ticks, width),
        compiler_params=pltpu.CompilerParams(collective_id=0, has_side_effects=True, vmem_limit_bytes=60 * MIB),
        cost_estimate=pl.CostEstimate(flops=6 * slots * width * width, bytes_accessed=90 * MIB, transcendentals=0),
        name="forward_beside_gather",
    )(cross_live, self_live, tokens, *sources, inner, outer, memory)
    return out[0].reshape(BLOCKS, rows, width), out[1:]


def blocks_of(pay):
    return pay.reshape((4, 2, 2) + pay.shape[1:])


def back_body(
    cross_live, self_live, q, k, v, mixture, lse, vecs, slse, third_grads,
    act_in, go_in, low_in, slope_in, gts_in, second_in, sum_in, sq_in, sk_in, sv_in, smix_in, tokens_in, stack,
    dk_o, dv_o, own, dq_o, gci_o, tokens_grad, self_keep, self_send, *scratch,
):
    refs, scratch = scratch[:8], scratch[8:]
    sent, weights, slopes, hidden, gss, second_sum, first_sum, gfs = scratch[:8]
    go, low, gci, gcm, dq, sq, sk, sv, smix, tokens, gsi, gq, gk, gv = scratch[8:22]
    grads, held, staged, load_sem, store_sem = scratch[22:]
    step = pl.program_id(0)
    me = lax.axis_index("dp").astype(jnp.int32)
    engine = Scatter(me, [], refs, own, 4 * PARTS)
    width = dq.shape[1]
    pairs = width // 128
    first_pair = 4
    after = first_pair + pairs

    def load(at, src, dst):
        return pltpu.make_async_copy(src, dst, load_sem.at[at])

    def store(at, src, dst):
        return pltpu.make_async_copy(src, dst, store_sem.at[at])

    act_load, go_load = load(0, act_in, hidden), load(1, go_in, go)
    ffn_loads = [load(2, low_in, low), load(3, gts_in, gss), load(4, second_in, second_sum)]
    self_loads = [
        load(5 + at, src, dst)
        for at, (src, dst) in enumerate(
            [(sum_in, first_sum), (sq_in, sq), (sk_in, sk), (sv_in, sv), (smix_in, smix), (tokens_in, tokens)]
        )
    ]

    def load_slope(part):
        return load(11 + part % 2, slope_in.at[:, pl.ds(part * width, width)], slopes.at[part % 2])

    def load_outer(part):
        return load(13, stack.at[pl.ds(8 * part, 8), pl.ds(128, 128)], weights.at[0].reshape(8, 128, width))

    def load_square(at, slot):
        return load(13 + slot, stack.at[:, pl.ds(at * 32, 32)], weights.at[slot])

    def on(at):
        return pl.when(step == at)

    def swaps(chunks):
        return [engine.swap(p, sent.at[p % (4 * PARTS)]) for p in range(chunks[0] * PARTS, (chunks[-1] + 1) * PARTS)]

    @on(0)
    def _():
        act_load.start()
        go_load.start()
        load_outer(0).start()
        load_square(0, 1).start()
        for part in range(2):
            load_slope(part).start()
        for copy in ffn_loads + self_loads:
            copy.start()
        greet(me)
        act_load.wait()
        go_load.wait()
        for z in range(4):
            group = flip(lax.div(me, 8), z)
            for part in range(4):
                columns = pl.ds(pl.multiple_of(group * 1024 + part * 256, 256), 256)
                held[pl.ds(part * 256, 256), :] = tn(hidden[:, columns], go[...]).astype(BF16)
            for j in range(8):
                row = pl.multiple_of(flip(lax.rem(me, 8), j) * 128, 128)
                for p in range(4):
                    rows = held[pl.ds(row + p * 32, 32), :]
                    engine.put(sent if j % 2 else engine.keep, p, (z, j // 4, (j // 2) % 2), rows)
        for copy in swaps(range(4)):
            copy.start()

    for at in (1, 2):
        @on(at)
        def _(at=at):
            if at == 1:
                for copy in ffn_loads:
                    copy.wait()
            for part in (2 * at - 2, 2 * at - 1):
                load_outer(part).wait()
                grad = nt(go[...], whole(weights.at[0]))
                if part < 3:
                    load_outer(part + 1).start()
                else:
                    load_square(16, 0).start()
                load_slope(part).wait()
                rows = (grad * slopes[part % 2]).astype(BF16)
                if part < 2:
                    load_slope(part + 2).start()
                hidden[:, part * width : part * width + width] = rows
                load_square(part, 1).wait()
                gss[...] += nt(rows, whole(weights.at[1]))
                load_square(part + 1 if part < 3 else 15, 1).start()
            if at == 2:
                grad, gain, shift = norm_back(second_sum[...], vecs[2:3, :], gss[...])
                gss[...] = grad
                rows = grad.astype(BF16)
                gci[...] = rows
                load_square(16, 0).wait()
                gcm[...] = nt(rows, whole(weights.at[0])).astype(BF16)
                load_square(14, 0).start()
                grads[2:3, :] = gain
                grads[3:4, :] = shift
                grads[4:6, :] = third_grads[0:2, :]
                grads[8:32, :] = jnp.zeros((24, width), F32)
                store(0, gci, gci_o).start()

    @on(3)
    def _():
        for copy in swaps(range(4)):
            copy.wait_send()
        for part in range(4):
            for z in range(4):
                held[:256, :] = tn(low[:, group_at(me, z)], hidden[:, part * width : part * width + width]).astype(BF16)

                def put(y, x, c, rows, z=z, part=part):
                    engine.put(sent if c else engine.keep, part if c else 4 + part, (z, y, x), rows)

                weight_blocks(held, me, put)
        for copy in swaps(range(4, 8)):
            copy.start()

    @pl.when((step >= first_pair) & (step < after))
    def _():
        cut = pl.ds(pl.multiple_of((step - first_pair) * 128, 128), 128)
        cross_back_body(cross_live, q, k, v, gcm.at[:, cut], mixture, lse, dq.at[:, cut], dk_o, dv_o)

    @on(after)
    def _():
        store(1, dq, dq_o).start()
        for copy in self_loads:
            copy.wait()
        load_square(15, 1).wait()
        load_square(14, 0).wait()
        self_back_body(
            self_live, gss, dq, weights.at[1], first_sum, weights.at[0], vecs, sq, sk, sv, smix, slse,
            gfs, gsi, gq, gk, gv, second_sum.at[pl.ds(0, 8)],
        )
        grads[0:2, :] = second_sum[0:2, :]
        load_square(10, 0).start()
        load_square(11, 1).start()

    def stores(z):
        return [store(2 + 2 * (z % 2) + c, staged.at[z % 2, c], (self_send if c else self_keep).at[z]) for c in range(2)]

    for z in range(4):
        @on(after + 1 + z // 2)
        def _(z=z):
            if z >= 2:
                for copy in stores(z - 2):
                    copy.wait()
            columns = group_at(me, z)
            for at, (rows, grad) in enumerate([(tokens, gq), (tokens, gk), (tokens, gv), (smix, gsi)]):
                held[:256, :] = tn(rows[:, columns], grad[...]).astype(BF16)

                def put(y, x, c, rows, at=at):
                    staged[z % 2, c, y, x, at * 32 : at * 32 + 32, :] = rows

                weight_blocks(held, me, put)
            rows = grads[...].astype(BF16)
            for y in range(2):
                for x in range(2):
                    for c in range(2):
                        staged[z % 2, c, y, x, 128:160, :] = rows
            for copy in stores(z):
                copy.start()
            if z == 0:
                load_square(10, 0).wait()
                gfs[...] += nt(gq[...], whole(weights.at[0]))
                load_square(12, 0).start()
            if z == 1:
                load_square(11, 1).wait()
                gfs[...] += nt(gk[...], whole(weights.at[1]))
            if z == 2:
                load_square(12, 0).wait()
                gfs[...] += nt(gv[...], whole(weights.at[0]))
                store(6, gfs, tokens_grad).start()

    @pl.when((step < first_pair) | (step >= after) | (lax.rem(step, 2) == 1))
    def _():
        engine.ticks_of(step - jnp.clip(lax.div(step - first_pair + 1, 2), 0, pairs // 2))

    @on(pl.num_programs(0) - 1)
    def _():
        for copy in [store(0, gci, gci_o), store(1, dq, dq_o), store(6, gfs, tokens_grad)] + stores(2) + stores(3):
            copy.wait()


def backward_beside(
    cross_live, self_live, q, k, v, mixture, lse, vecs, slse, third_grads,
    act, go, low, slope, gts, second_sum, first_sum, sq, sk, sv, smix, tokens, stack,
):
    count, width = q.shape
    slots = k.shape[0]
    last = width // 128 - 1

    def pair(i):
        return jnp.clip(i - 4, 0, last)

    ticks = 8
    small = pl.BlockSpec((count, 128), lambda i: (0, pair(i)))
    large = pl.BlockSpec((slots, 128), lambda i: (0, pair(i)))
    scalar = pl.BlockSpec(memory_space=pltpu.SMEM)
    hbm = pl.BlockSpec(memory_space=pl.ANY)
    pay_shape = shape((4, 2, 2, 160, width), BF16)
    wide = pltpu.VMEM(q.shape, F32)
    thin = pltpu.VMEM(q.shape, BF16)
    dk, dv, own, dq, gci, tokens_grad, self_keep, self_send = pl.pallas_call(
        back_body,
        grid=(last + 1 + 7,),
        out_shape=[
            shape(k.shape, BF16), shape(k.shape, BF16), shape((ticks * PAIR, width), F32),
            shape(q.shape, BF16), shape(q.shape, BF16), shape(q.shape, F32), pay_shape, pay_shape,
        ],
        in_specs=[
            scalar, scalar, small, large, large, small, pl.BlockSpec((1, 8, count), lambda i: (pair(i), 0, 0)),
            once(vecs.shape), once(slse.shape), once(third_grads.shape),
        ] + [hbm] * 13,
        out_specs=[large, large, full((ticks * PAIR, width))] + [hbm] * 5,
        scratch_shapes=Scatter.scratch(ticks * PARTS, width // PARTS)
        + [
            pltpu.VMEM((4 * PARTS, 4, 2, 2, PAIR, width // PARTS), BF16), pltpu.VMEM((2, BLOCKS, 32, width), BF16),
            pltpu.VMEM((2, count, width), F32), pltpu.VMEM(act.shape, BF16),
        ]
        + [wide] * 4 + [thin] * 14
        + [
            pltpu.VMEM((32, width), F32), pltpu.VMEM((1024, width), BF16), pltpu.VMEM((2, 2, 2, 2, 160, width), BF16),
            pltpu.SemaphoreType.DMA((15,)), pltpu.SemaphoreType.DMA((7,)),
        ],
        compiler_params=pltpu.CompilerParams(collective_id=1, has_side_effects=True, vmem_limit_bytes=63 * MIB),
        cost_estimate=pl.CostEstimate(flops=70 * count * slots * width, bytes_accessed=80 * MIB, transcendentals=0),
        name="backward_beside_sum",
    )(
        cross_live, self_live, q, k, v, mixture, lse, vecs, slse, third_grads,
        act, go, low, slope, gts, second_sum, first_sum, sq, sk, sv, smix, tokens, stack,
    )
    return dq, dk, dv, gci, tokens_grad, (self_keep, self_send), own


def finish_body(
    first_low, dq, mixture, gci, memory_in, dk_in, dv_in, stack, self_keep, self_send, memory_grad, own, *scratch
):
    refs, (sent, held, memory, dk, dv, weights, load_sem) = scratch[:8], scratch[8:]
    step = pl.program_id(0)
    me = lax.axis_index("dp").astype(jnp.int32)
    engine = Scatter(me, [(self_keep, self_send)], refs, own)
    early = engine.loads // PARTS
    tile = memory_grad.shape[0]
    loads = [
        pltpu.make_async_copy(src, dst, load_sem.at[at])
        for at, (src, dst) in enumerate(
            [(memory_in, memory), (dk_in, dk), (dv_in, dv)]
            + [(stack.at[:, pl.ds((8 + slot) * 32, 32)], weights.at[slot]) for slot in range(2)]
        )
    ]

    def on(at):
        return pl.when(step == at)

    @on(0)
    def _():
        engine.begin()
        for load in loads:
            load.start()

    def weight(w, rows, grad, groups):
        for z in groups:
            held[...] = tn(rows[:, group_at(me, z)], grad[...])

            def put(y, x, c, rows, z=z):
                engine.put(sent if c else engine.keep, w if c else early + w, (z, y, x), rows)

            weight_blocks(held, me, put)

    def swap(w):
        for part in range(PARTS):
            engine.swap((early + w) * PARTS + part, sent.at[w * PARTS + part]).start()

    for w, rows, grad in ((0, first_low, dq), (1, mixture, gci)):
        @on(w)
        def _(w=w, rows=rows, grad=grad):
            weight(w, rows, grad, range(4))
            swap(w)

    for w, rows, grad in ((2, memory, dk), (3, memory, dv)):
        for z in range(4):
            @on((w - 2) * 4 + z + 1)
            def _(w=w, rows=rows, grad=grad, z=z):
                if z == 0:
                    for load in loads[:2] if w == 2 else loads[2:]:
                        load.wait()
                weight(w, rows, grad, (z,))
                if z == 3:
                    swap(w)

    @pl.when((step >= FIRST_TILE) & (step < FIRST_TILE + dk.shape[0] // tile))
    def _():
        at = pl.ds(pl.multiple_of((step - FIRST_TILE) * tile, tile), tile)
        memory_grad[...] = nt(dk[at, :], whole(weights.at[0])) + nt(dv[at, :], whole(weights.at[1]))

    engine.ticks_of(step)


def finish(memory, dk, dv, first_low, dq, mixture, gci, stack, self_pay):
    slots, width = memory.shape
    tile = 512
    tiles = slots // tile
    ticks = self_pay[0].shape[3] // PAIR + 4
    hbm = pl.BlockSpec(memory_space=pl.ANY)
    square = once(dq.shape)
    large = pltpu.VMEM(memory.shape, BF16)
    return pl.pallas_call(
        finish_body,
        grid=(max(FIRST_TILE + tiles, ticks + -(-3 * LAG // PARTS)),),
        out_shape=[shape(memory.shape, F32), shape((ticks * PAIR, width), F32)],
        in_specs=[square, square, square, square] + [hbm] * 6,
        out_specs=[pl.BlockSpec((tile, width), lambda i: (jnp.clip(i - FIRST_TILE, 0, tiles - 1), 0)), full((ticks * PAIR, width))],
        scratch_shapes=Scatter.scratch(ticks * PARTS, width // PARTS)
        + [pltpu.VMEM((4 * PARTS, 4, 2, 2, PAIR, width // PARTS), BF16), pltpu.VMEM((256, width), F32), large, large, large]
        + [pltpu.VMEM((2, BLOCKS, 32, width), BF16), pltpu.SemaphoreType.DMA((5,))],
        compiler_params=pltpu.CompilerParams(collective_id=2, has_side_effects=True, vmem_limit_bytes=62 * MIB),
        cost_estimate=pl.CostEstimate(flops=8 * slots * width * width, bytes_accessed=60 * MIB, transcendentals=0),
        name="finish_beside_sum",
    )(first_low, dq, mixture, gci, memory, dk, dv, stack, *self_pay)


def unpack_body(memory_in, tokens_in, ffn, owned, memory_grad, tokens_grad, outer, inner, *squares):
    memory_grad[...] = memory_in[...]

    @pl.when(pl.program_id(0) == 0)
    def _():
        width = ffn.shape[1]
        tokens_grad[...] = tokens_in[...]
        outer[...] = ffn[:128, :]
        for part in range(4):
            inner[:, part * width : part * width + width] = ffn[128 + part * 32 : 160 + part * 32, :]
        for at, square in zip(OWNED, squares):
            square[...] = owned[at : at + 32, :]


def unpack(memory_grad, tokens_grad, ffn, owned):
    width = ffn.shape[1]
    tile = 256
    wide = pl.BlockSpec((tile, width), lambda i: (i, 0))
    outs = [(128, width), (32, 4 * width)] + [(32, width)] * len(OWNED)
    return call(
        unpack_body, "unpack",
        [shape(memory_grad.shape, F32), shape(tokens_grad.shape, F32)] + [shape(dims, F32) for dims in outs],
        (memory_grad.shape[0] // tile,),
        [wide, once(tokens_grad.shape), once(ffn.shape), once(owned.shape)],
        [wide, full(tokens_grad.shape)] + [full(dims) for dims in outs],
        flops=0, moved=22 * MIB,
    )(memory_grad, tokens_grad, ffn, owned)


OWNED = (0, 32, 64, 96, 160, 224, 256, 192)


def absolute(keep, send):
    return jnp.stack([keep, send], axis=1).reshape((BLOCKS,) + keep.shape[1:])


def gather(rows):
    return lax.all_gather(rows, "dp", axis=0, tiled=True)


def on_device(
    devices, tokens, memory, target_lengths, memory_lengths, cotangent,
    self_query, self_key, self_value, self_output, first_gain, first_shift,
    cross_query, cross_key, cross_value, cross_output, second_gain, second_shift,
    inner_weight, outer_weight, third_gain, third_shift,
):
    width = tokens.shape[1]
    hidden = inner_weight.shape[1]
    direct = devices == BLOCKS
    squares = [cross_key, cross_value, self_query, self_key, self_value, self_output, cross_query, cross_output]
    vectors = [first_gain, first_shift, second_gain, second_shift, third_gain, third_shift]
    if direct:
        place_of = lax.axis_index("dp").astype(jnp.int32)
        me = place_of.reshape(1)
        own = lax.dynamic_update_slice(jnp.zeros((32, width), BF16), jnp.stack(vectors), (0, place_of * 32))
        stack, parts = forward_beside(
            memory_lengths, target_lengths, tokens, squares[:VEC] + [own] + squares[VEC:], inner_weight, outer_weight, memory
        )
        (keys, values, q, k, v, mixture, first_sum, first_out, first_low, cross_q, lse,
         cross_mixture, cross_lse, second_sum, second, second_low, vecs) = parts
    else:
        me = jnp.zeros((1,), jnp.int32)
        inner_full = gather(inner_weight)
        parts = [inner_full[:, i : i + width].reshape(BLOCKS, 32, width) for i in range(0, hidden, width)]
        parts.append(gather(outer_weight).reshape(BLOCKS, 128, width))
        parts += [gather(w).reshape(BLOCKS, 32, width) for w in squares[:VEC]] + [jnp.zeros((BLOCKS, 32, width), BF16)]
        parts += [gather(w).reshape(BLOCKS, 32, width) for w in squares[VEC:]]
        stack = jnp.concatenate(parts, axis=1)
        vecs = jnp.pad(jnp.stack([gather(v) for v in vectors]), ((0, 10), (0, 0))).astype(F32)
        keys, values = kv_project(memory, stack, 8, 9)
        q, k, v, mixture, first_sum, first_out, first_low, cross_q, lse = self_forward(
            target_lengths, tokens, stack, (10, 11, 12, 14, 15), vecs
        )
        cross_mixture, cross_lse = cross_forward(memory_lengths, cross_q, keys, values)
        second_sum, second, second_low = second_norm(cross_mixture, stack, 16, first_out, vecs)

    act, slope, output_rows, gts, go, third_grads = ffn_forward(second_low, second, stack, cotangent, vecs)
    if direct:
        dq, dk, dv, gci, tokens_grad, self_pay, ffn_own = backward_beside(
            memory_lengths, target_lengths, cross_q, keys, values, cross_mixture, cross_lse, vecs, lse, third_grads,
            act, go, second_low, slope, gts, second_sum, first_sum, q, k, v, mixture, tokens, stack,
        )
        memory_grad, owned = finish(memory, dk, dv, first_low, dq, cross_mixture, gci, stack, self_pay)
        vec_rows = lax.dynamic_slice(owned, (128, me[0] * 32), (6, 32))
        vec_own = [vec_rows[i] for i in range(6)]
        memory_grad, tokens_grad, outer_own, inner_own, *squares_own = unpack(memory_grad, tokens_grad, ffn_own, owned)
        self_own, cross_own = squares_own[:4], squares_own[4:]
    else:
        gi, gss, gci, gcm, second_grads = ffn_backward(go, gts, slope, stack, second_sum, stack, 16, vecs)
        ffn_pay = ffn_weights(me, act, go, second_low, gi)
        dq, dk, dv = cross_backward(memory_lengths, cross_q, keys, values, gcm, cross_mixture, cross_lse)
        cross_pay = square_weights(
            me, [(first_low, dq), (memory, dk), (memory, dv), (cross_mixture, gci)], "cross_weights"
        )
        gfs, gsi, gq, gk, gv, first_grads = self_backward(
            target_lengths, gss, dq, stack, 15, 14, first_sum, vecs, q, k, v, mixture, lse
        )
        self_pay = square_weights(me, [(tokens, gq), (tokens, gk), (tokens, gv), (mixture, gsi)], "self_weights")
        memory_grad = memory_gradient(dk, dv, stack, 8, 9)
        tokens_grad = tokens_gradient(gfs, gq, gk, gv, stack, (10, 11, 12))

        def summed(rows):
            return lax.psum_scatter(rows.astype(F32), "dp", scatter_dimension=0, tiled=True)

        ffn_rows, cross_rows, self_rows = absolute(*ffn_pay), absolute(*cross_pay), absolute(*self_pay)
        outer_own = summed(ffn_rows[:, :128].reshape(-1, width))
        inner_own = summed(
            jnp.concatenate([ffn_rows[:, i : i + 32].reshape(-1, width) for i in range(128, 256, 32)], axis=1)
        )
        cross_own = [summed(cross_rows[:, i : i + 32].reshape(-1, width)) for i in range(0, 128, 32)]
        self_own = [summed(self_rows[:, i : i + 32].reshape(-1, width)) for i in range(0, 128, 32)]
        vec_own = [summed(rows[i]) for rows in (first_grads, second_grads, third_grads) for i in range(2)]

    return (
        output_rows, tokens_grad, memory_grad,
        *self_own, vec_own[0], vec_own[1],
        *cross_own, vec_own[2], vec_own[3],
        inner_own, outer_own, vec_own[4], vec_own[5],
    )


def solution(mesh):
    rows, line = P("dp", None), P("dp")
    block = [rows] * 4 + [line] * 2
    placed = (rows, rows, line, line, rows, *block, *block, rows, rows, line, line)
    return jax.shard_map(
        functools.partial(on_device, mesh.shape["dp"]),
        mesh=mesh,
        in_specs=placed,
        out_specs=(rows, rows, rows, *block, *block, rows, rows, line, line),
        check_vma=False,
    )
```

```python
import functools
import math

import jax
import jax.numpy as jnp
from jax import lax
from jax.experimental import pallas as pl
from jax.experimental.pallas import tpu as pltpu
from jax.sharding import PartitionSpec as P

HEAD = 64
EPS = 1e-05
SCALE = 1.0 / math.sqrt(HEAD)
LOG2E = 1.4426950408889634
BLOCKS = 32
MIB = 1024 * 1024
F32 = jnp.float32
BF16 = jnp.bfloat16
PAIR, HALF = 32, 16
CORE, XBIT, YBIT, NEAR, FAR, BOTH = PARTNERS = (1, 2, 4, 8, 16, 24)
LAG = 2
PARTS = 2
GATHER_LAG = 1
FIRST_TILE = 7


def nn(a, b):
    return jnp.dot(a, b, preferred_element_type=F32)


def nt(a, b):
    return lax.dot_general(a, b, (((1,), (1,)), ((), ())), preferred_element_type=F32)


def tn(a, b):
    return lax.dot_general(a, b, (((0,), (0,)), ((), ())), preferred_element_type=F32)


def whole(ref):
    return ref[...].reshape(-1, ref.shape[-1])


def call(body, name, out, grid=(), ins=None, outs=None, scratch=(), prefetch=0, limit=56, flops=0, moved=0):
    return pl.pallas_call(
        body,
        out_shape=out,
        grid_spec=pltpu.PrefetchScalarGridSpec(
            num_scalar_prefetch=prefetch,
            grid=grid,
            in_specs=ins,
            out_specs=outs,
            scratch_shapes=scratch,
        ),
        compiler_params=pltpu.CompilerParams(vmem_limit_bytes=limit * MIB),
        cost_estimate=pl.CostEstimate(flops=flops, bytes_accessed=moved, transcendentals=0),
        name=name,
    )


def full(shape):
    return pl.BlockSpec(shape, lambda *_: (0,) * len(shape))


def weight(at):
    return pl.BlockSpec((BLOCKS, 32, 1024), lambda *_: (0, at, 0))


def shape(dims, dtype):
    return jax.ShapeDtypeStruct(dims, dtype)


def norm_parts(summed):
    average = jnp.mean(summed, axis=-1, keepdims=True)
    centred = summed - average
    spread = jnp.mean(centred * centred, axis=-1, keepdims=True)
    scale = lax.rsqrt(spread + EPS)
    return centred * scale, scale


def norm_back(summed, gain, upstream):
    normal, scale = norm_parts(summed)
    grad_gain = jnp.sum(upstream * normal, axis=0, keepdims=True)
    grad_shift = jnp.sum(upstream, axis=0, keepdims=True)
    scaled = upstream * gain
    first = jnp.mean(scaled, axis=-1, keepdims=True)
    second = jnp.mean(scaled * normal, axis=-1, keepdims=True)
    return scale * (scaled - first - normal * second), grad_gain, grad_shift


def lanes(rows):
    return lax.broadcasted_iota(jnp.int32, (rows, 128), 1)


def stack_pair(rows):
    low = lanes(rows.shape[0]) < HEAD
    zero = jnp.zeros_like(rows)
    return jnp.concatenate([jnp.where(low, rows, zero), jnp.where(low, zero, rows)], axis=0)


def unstack_pair(stacked):
    half = stacked.shape[0] // 2
    return jnp.where(lanes(half) < HEAD, stacked[:half], stacked[half:])


def pair_forward(stacked, keys, values, mask):
    scores = nt(stacked, keys)
    if mask is not None:
        scores = mask(scores)
    peak = jnp.max(scores, axis=-1, keepdims=True)
    raised = jnp.exp2((scores - peak) * (SCALE * LOG2E))
    total = jnp.sum(raised, axis=-1, keepdims=True)
    mixed = nn(raised.astype(BF16), values) / total
    return mixed, peak * SCALE + jnp.log(total)


def pair_tile_back(q2, g2, keys, values, totals, inner, mask):
    scores = nt(keys, q2)
    probs = jnp.exp2(scores * (SCALE * LOG2E) - totals)
    if mask is not None:
        probs = mask(probs)
    grad_probs = nt(values, g2)
    grad_scores = (probs * (grad_probs - inner)).astype(BF16)
    grad_values = nn(probs.astype(BF16), g2)
    grad_keys = nn(grad_scores, q2) * SCALE
    grad_queries = tn(keys, grad_scores)
    return grad_queries, grad_keys, grad_values


def pair_inner(mixture, grad):
    product = mixture.astype(F32) * grad.astype(F32)
    half = jnp.where(
        (lax.broadcasted_iota(jnp.int32, (8, 128), 1) // HEAD)
        == lax.broadcasted_iota(jnp.int32, (8, 128), 0),
        1.0,
        0.0,
    ).astype(F32)
    sums = lax.dot_general(
        half, product, (((1,), (1,)), ((), ())),
        preferred_element_type=F32, precision=lax.Precision.HIGHEST,
    )
    return jnp.concatenate([sums[0:1], sums[1:2]], axis=1)


def join_grad_queries(grad):
    count = grad.shape[1] // 2
    joined = jnp.concatenate([grad[:HEAD, :count], grad[HEAD:, count:]], axis=0) * SCALE
    return joined.T.astype(BF16)


def kv_body(memory, wk, wv, keys, values):
    rows = memory[...]
    keys[...] = nn(rows, whole(wk)).astype(BF16)
    values[...] = nn(rows, whole(wv)).astype(BF16)


def kv_project(memory, stack, at_k, at_v):
    count, width = memory.shape
    tile = 512
    spec = pl.BlockSpec((tile, width), lambda i: (i, 0))
    return call(
        kv_body, "cross_kv", [shape(memory.shape, BF16)] * 2, (count // tile,),
        [spec, weight(at_k), weight(at_v)], [spec, spec],
        flops=4 * count * width * width, moved=12 * MIB + 4 * MIB,
    )(memory, stack, stack)


def self_attention(live, q_o, k_o, v_o, mix_o, lse_o):
    count, width = q_o.shape
    at_q = lax.rem(lax.broadcasted_iota(jnp.int32, (2 * count, count), 0), count)
    at_k = lax.broadcasted_iota(jnp.int32, (2 * count, count), 1)
    allowed = (at_k <= at_q) & (at_k < live)
    column = lanes(count)
    totals = jnp.zeros((count, 128), F32)
    for pair in range(width // 128):
        cut = slice(pair * 128, pair * 128 + 128)
        mixed, log_total = pair_forward(
            stack_pair(q_o[:, cut]), k_o[:, cut], v_o[:, cut],
            lambda scores: jnp.where(allowed, scores, -1e30),
        )
        mix_o[:, cut] = unstack_pair(mixed).astype(BF16)
        totals = jnp.where(column == 2 * pair, log_total[:count], totals)
        totals = jnp.where(column == 2 * pair + 1, log_total[count:], totals)
    lse_o[...] = totals.T


def self_body(length, tokens, wq, wk, wv, wo, wcq, vecs, q_o, k_o, v_o, mix_o, sum_o, first_o, low_o, cq_o, lse_o):
    rows = tokens[...]
    count, width = rows.shape
    q_o[...] = nn(rows, whole(wq)).astype(BF16)
    k_o[...] = nn(rows, whole(wk)).astype(BF16)
    v_o[...] = nn(rows, whole(wv)).astype(BF16)
    self_attention(length[0], q_o, k_o, v_o, mix_o, lse_o)
    summed = rows.astype(F32) + nn(mix_o[...], whole(wo))
    sum_o[...] = summed
    normal, _ = norm_parts(summed)
    first = normal * vecs[0:1] + vecs[1:2]
    first_o[...] = first
    low = first.astype(BF16)
    low_o[...] = low
    cq_o[...] = nn(low, whole(wcq)).astype(BF16)


def self_forward(length, tokens, stack, at, vecs):
    count, width = tokens.shape
    low = shape(tokens.shape, BF16)
    wide = shape(tokens.shape, F32)
    spec = full(tokens.shape)
    return call(
        self_body, "self_forward",
        [low, low, low, low, wide, wide, low, low, shape((128, count), F32)], (1,),
        [spec] + [weight(k) for k in at] + [full(vecs.shape)],
        [spec] * 8 + [full((128, count))], prefetch=1,
        flops=10 * count * width * width, moved=16 * MIB,
    )(length, tokens, stack, stack, stack, stack, stack, vecs)


def cross_body(length, q, k, v, mix_o, lse_o):
    count = q.shape[0]
    slots = k.shape[0]
    live = length[0]
    q2 = stack_pair(q[...])
    keys = k[...]
    values = v[...]
    half = slots // 2
    tile = 128
    column = lax.broadcasted_iota(jnp.int32, (tile, slots - half), 1) + half

    def mask(scores):
        upper = jnp.where(column < live, scores[:, half:], -1e30)
        return jnp.concatenate([scores[:, :half], upper], axis=1)

    mixes, logs = [], []
    for at in range(0, 2 * count, tile):
        mixed, log_total = pair_forward(q2[at : at + tile], keys, values, mask)
        mixes.append(mixed)
        logs.append(log_total)
    mix_o[...] = unstack_pair(jnp.concatenate(mixes, axis=0)).astype(BF16)
    logs = jnp.concatenate(logs, axis=0)
    column = lanes(count)
    totals = jnp.where(column == 0, logs[:count], jnp.where(column == 1, logs[count:], 0.0))
    lse_o[0] = totals.T[:8]


def cross_forward(length, q, k, v):
    count, width = q.shape
    slots = k.shape[0]
    pairs = width // 128
    return call(
        cross_body, "cross_forward",
        [shape(q.shape, BF16), shape((pairs, 8, count), F32)], (pairs,),
        [pl.BlockSpec((count, 128), lambda i, _: (0, i))]
        + [pl.BlockSpec((slots, 128), lambda i, _: (0, i))] * 2,
        [pl.BlockSpec((count, 128), lambda i, _: (0, i)), pl.BlockSpec((1, 8, count), lambda i, _: (i, 0, 0))],
        prefetch=1, flops=16 * count * slots * width, moved=10 * MIB,
    )(length, q, k, v)


def second_rows(mixture, wo, first, vecs, sum_o, second_o, low_o):
    summed = first + nn(mixture, wo)
    sum_o[...] = summed
    normal, _ = norm_parts(summed)
    second = normal * vecs[2:3, :] + vecs[3:4, :]
    second_o[...] = second
    low_o[...] = second.astype(BF16)


def second_body(mixture, wo, first, vecs, sum_o, second_o, low_o):
    second_rows(mixture[...], whole(wo), first[...], vecs, sum_o, second_o, low_o)


def second_norm(mixture, stack, at, first, vecs):
    spec = full(mixture.shape)
    return call(
        second_body, "second_norm",
        [shape(mixture.shape, F32), shape(mixture.shape, F32), shape(mixture.shape, BF16)], (1,),
        [spec, weight(at), spec, full(vecs.shape)], [spec] * 3,
        flops=MIB * 512, moved=6 * MIB,
    )(mixture, stack, first, vecs)


def erf(x):
    return lax.erf(x)


def ffn_body(low, second, inner, outer, cot, vecs, act_o, slope_o, out_o, gts_o, go_o, grads_o, total):
    step = pl.program_id(0)
    pre = nn(low[...], whole(inner))
    half = 0.5 * (1.0 + erf(pre * math.sqrt(0.5)))
    active = (pre * half).astype(BF16)
    act_o[...] = active
    slope_o[...] = half + pre * (jnp.exp(-0.5 * pre * pre) * (1.0 / math.sqrt(2.0 * math.pi)))
    part = nn(active, whole(outer))

    @pl.when(step == 0)
    def _():
        total[...] = second[...] + part

    @pl.when(step > 0)
    def _():
        total[...] += part

    @pl.when(step == pl.num_programs(0) - 1)
    def _():
        summed = total[...]
        normal, _ = norm_parts(summed)
        out_o[...] = (normal * vecs[4:5] + vecs[5:6]).astype(BF16)
        grad, gain, shift = norm_back(summed, vecs[4:5], cot[...].astype(F32))
        gts_o[...] = grad
        go_o[...] = grad.astype(BF16)
        grads_o[...] = jnp.concatenate([gain, shift] + [jnp.zeros_like(gain)] * 6, axis=0)


def ffn_forward(low, second, stack, cot, vecs):
    count, width = low.shape
    spec = full(low.shape)
    wide = pl.BlockSpec((count, 1024), lambda i: (0, i))
    return call(
        ffn_body, "ffn_forward",
        [shape((count, 4096), BF16), shape((count, 4096), F32), shape(low.shape, BF16), shape(low.shape, F32), shape(low.shape, BF16), shape((8, width), F32)],
        (4,),
        [spec, spec, pl.BlockSpec((BLOCKS, 32, 1024), lambda i: (0, i, 0)), pl.BlockSpec((8, 128, 1024), lambda i: (i, 1, 0)), spec, full(vecs.shape)],
        [wide, wide, spec, spec, spec, full((8, width))],
        scratch=[pltpu.VMEM(low.shape, F32)],
        flops=16 * count * width * width, moved=24 * MIB,
    )(low, second, stack, stack, cot, vecs)


def ffn_back_body(go, gts, slope, inner, outer, summed, wo, vecs, gi_o, gss_o, gci_o, gcm_o, grads_o, total):
    step = pl.program_id(0)
    grad = nt(go[...], whole(outer))
    low = (grad * slope[...]).astype(BF16)
    gi_o[...] = low
    part = nt(low, whole(inner))

    @pl.when(step == 0)
    def _():
        total[...] = gts[...] + part

    @pl.when(step > 0)
    def _():
        total[...] += part

    @pl.when(step == pl.num_programs(0) - 1)
    def _():
        grad, gain, shift = norm_back(summed[...], vecs[2:3], total[...])
        gss_o[...] = grad
        low = grad.astype(BF16)
        gci_o[...] = low
        gcm_o[...] = nt(low, whole(wo)).astype(BF16)
        grads_o[...] = jnp.concatenate([gain, shift] + [jnp.zeros_like(gain)] * 6, axis=0)


def ffn_backward(go, gts, slope, stack, summed, squares, at, vecs):
    count, width = go.shape
    spec = full(go.shape)
    wide = pl.BlockSpec((count, 1024), lambda i: (0, i))
    low = shape(go.shape, BF16)
    return call(
        ffn_back_body, "ffn_backward",
        [shape((count, 4096), BF16), shape(go.shape, F32), low, low, shape((8, width), F32)],
        (4,),
        [spec, spec, wide, pl.BlockSpec((BLOCKS, 32, 1024), lambda i: (0, i, 0)), pl.BlockSpec((8, 128, 1024), lambda i: (i, 1, 0)), spec, weight(at), full(vecs.shape)],
        [wide, spec, spec, spec, full((8, width))],
        scratch=[pltpu.VMEM(go.shape, F32)],
        flops=18 * count * width * width, moved=26 * MIB,
    )(go, gts, slope, stack, stack, summed, squares, vecs)


def cross_back_body(length, q, k, v, g, mixture, lse, dq_o, dk_o, dv_o):
    live = length[0]
    slots = k.shape[0]
    count = q.shape[0]
    q2 = stack_pair(q[...])
    g2 = stack_pair(g[...])
    totals = jnp.concatenate([lse[0, 0:1], lse[0, 1:2]], axis=1) * LOG2E
    inner = pair_inner(mixture[...], g[...])
    tile = 256
    grad_q = jnp.zeros((128, 2 * count), F32)
    for at in range(0, slots, tile):
        mask = None
        if at + tile > slots // 2:
            row = lax.broadcasted_iota(jnp.int32, (tile, 2 * count), 0) + at

            def mask(probs, row=row):
                return jnp.where(row < live, probs, 0.0)

        cut = slice(at, at + tile)
        dq, dk, dv = pair_tile_back(q2, g2, k[cut], v[cut], totals, inner, mask)
        grad_q = grad_q + dq
        dk_o[cut] = dk.astype(BF16)
        dv_o[cut] = dv.astype(BF16)
    dq_o[...] = join_grad_queries(grad_q)


def cross_backward(length, q, k, v, g, mixture, lse):
    count, width = q.shape
    slots = k.shape[0]
    pairs = width // 128
    small = pl.BlockSpec((count, 128), lambda i, _: (0, i))
    large = pl.BlockSpec((slots, 128), lambda i, _: (0, i))
    return call(
        cross_back_body, "cross_backward",
        [shape(q.shape, BF16), shape(k.shape, BF16), shape(k.shape, BF16)], (pairs,),
        [small, large, large, small, small, pl.BlockSpec((1, 8, count), lambda i, _: (i, 0, 0))],
        [small, large, large], prefetch=1,
        flops=40 * count * slots * width, moved=18 * MIB,
    )(length, q, k, v, g, mixture, lse)


def memory_grad_body(dk, dv, wk, wv, out):
    out[...] = nt(dk[...], whole(wk)) + nt(dv[...], whole(wv))


def memory_gradient(dk, dv, stack, at_k, at_v):
    count, width = dk.shape
    tile = 512
    spec = pl.BlockSpec((tile, width), lambda i: (i, 0))
    return call(
        memory_grad_body, "memory_grad", shape(dk.shape, F32), (count // tile,),
        [spec, spec, weight(at_k), weight(at_v)], spec,
        flops=4 * count * width * width, moved=20 * MIB,
    )(dk, dv, stack, stack)


def self_back_body(length, gss, dcq, wcq, summed, wo, vecs, q, k, v, mixture, lse, gfs_o, gsi_o, gq_o, gk_o, gv_o, grads_o):
    live = length[0]
    count, width = gss.shape
    upstream = gss[...] + nt(dcq[...], whole(wcq))
    grad, gain, shift = norm_back(summed[...], vecs[0:1], upstream)
    gfs_o[...] = grad
    grads_o[...] = jnp.concatenate([gain, shift] + [jnp.zeros_like(gain)] * 6, axis=0)
    low = grad.astype(BF16)
    gsi_o[...] = low
    mix_grad = nt(low, whole(wo)).astype(BF16)
    at_k = lax.broadcasted_iota(jnp.int32, (count, 2 * count), 0)
    at_q = lax.rem(lax.broadcasted_iota(jnp.int32, (count, 2 * count), 1), count)
    allowed = (at_k <= at_q) & (at_k < live)
    for pair in range(width // 128):
        cut = slice(pair * 128, pair * 128 + 128)
        g = mix_grad[:, cut]
        totals = jnp.concatenate([lse[2 * pair : 2 * pair + 1], lse[2 * pair + 1 : 2 * pair + 2]], axis=1) * LOG2E
        scores_back = pair_tile_back(
            stack_pair(q[:, cut]), stack_pair(g), k[:, cut], v[:, cut], totals,
            pair_inner(mixture[:, cut], g),
            lambda probs: jnp.where(allowed, probs, 0.0),
        )
        dq, dk, dv = scores_back
        gq_o[:, cut] = join_grad_queries(dq)
        gk_o[:, cut] = dk.astype(BF16)
        gv_o[:, cut] = dv.astype(BF16)


def self_backward(length, gss, dcq, stack, at_cq, at_o, summed, vecs, q, k, v, mixture, lse):
    count, width = q.shape
    spec = full(q.shape)
    low = shape(q.shape, BF16)
    return call(
        self_back_body, "self_backward",
        [shape(q.shape, F32), low, low, low, low, shape((8, width), F32)], (1,),
        [spec, spec, weight(at_cq), spec, weight(at_o), full(vecs.shape), spec, spec, spec, spec, full(lse.shape)],
        [spec] * 5 + [full((8, width))], prefetch=1,
        flops=8 * count * width * width, moved=12 * MIB,
    )(length, gss, dcq, stack, summed, stack, vecs, q, k, v, mixture, lse)


def tokens_grad_body(gfs, gq, gk, gv, wq, wk, wv, out):
    out[...] = gfs[...] + nt(gq[...], whole(wq)) + nt(gk[...], whole(wk)) + nt(gv[...], whole(wv))


def tokens_gradient(gfs, gq, gk, gv, stack, at):
    spec = full(gfs.shape)
    return call(
        tokens_grad_body, "tokens_grad", shape(gfs.shape, F32), (1,),
        [spec] * 4 + [weight(k) for k in at], spec,
        flops=6 * MIB * 256, moved=10 * MIB,
    )(gfs, gq, gk, gv, stack, stack, stack)


def place(keep, send, at, size, pieces, me):
    low = lax.rem(me, 8)
    for j in range(8):
        rows = pieces(lax.bitwise_xor(low, j))
        target = send if j % 2 else keep
        target[j // 2, at : at + size, :] = rows.astype(BF16)


def group_of(step, me):
    return lax.bitwise_xor(step, lax.div(me[0], 8))


def payload(rows, width):
    out = [shape((16, rows, width), BF16)] * 2
    spec = [pl.BlockSpec((4, rows, width), lambda i, _: (i, 0, 0))] * 2
    return out, spec


def ffn_weights_body(me, act, go, low, gi, keep, send, held):
    step = pl.program_id(0)

    @pl.when(step < 4)
    def _():
        held[...] = tn(act[...], go[...])
        place(keep, send, 0, 128, lambda d: held[pl.ds(pl.multiple_of(d * 128, 128), 128), :], me[0])

    @pl.when(step >= 4)
    def _():
        for part in range(4):
            held[:256, :] = tn(low[...], gi[:, part * 1024 : part * 1024 + 1024])
            place(keep, send, part * 32, 32, lambda d: held[pl.ds(pl.multiple_of(d * 32, 32), 32), :], me[0])


def ffn_weights(me, act, go, low, gi):
    count, width = go.shape
    spec = pl.BlockSpec((4, 128, width), lambda i, me: (lax.rem(i, 4), lax.div(i, 4), 0))
    return call(
        ffn_weights_body, "ffn_weights", [shape((16, 256, width), BF16)] * 2, (8,),
        [
            pl.BlockSpec((count, 1024), lambda i, me: (0, group_of(jnp.minimum(i, 3), me))),
            full(go.shape),
            pl.BlockSpec((count, 256), lambda i, me: (0, group_of(jnp.maximum(i - 4, 0), me))),
            full(gi.shape),
        ],
        [spec, spec], [pltpu.VMEM((1024, width), F32)], 1,
        flops=16 * count * width * width, moved=22 * MIB,
    )(me, act, go, low, gi)


def square_body(me, *refs):
    count = (len(refs) - 3) // 2
    keep, send, held = refs[-3:]
    for at in range(count):
        held[...] = tn(refs[2 * at][...], refs[2 * at + 1][...])
        place(keep, send, at * 32, 32, lambda d: held[pl.ds(pl.multiple_of(d * 32, 32), 32), :], me[0])


def square_weights(me, pairs, name):
    width = pairs[0][0].shape[1]
    out, spec = payload(128, width)
    ins, operands, flops = [], [], 0
    for rows, grads in pairs:
        ins.append(pl.BlockSpec((rows.shape[0], 256), lambda i, me: (0, group_of(i, me))))
        ins.append(full(grads.shape))
        operands += [rows, grads]
        flops += 2 * rows.shape[0] * width * width
    return call(
        square_body, name, out, (4,), ins, spec,
        [pltpu.VMEM((256, width), F32)], 1, flops=flops, moved=20 * MIB,
    )(me, *operands)


def flip(me, bits):
    for bit in (1, 2, 4, 8, 16):
        if bits & bit:
            me = me + bit - 2 * bit * lax.rem(lax.div(me, bit), 2)
    return me


def remote(src, dst, out_sem, in_sem, to):
    return pltpu.make_async_remote_copy(
        src_ref=src, dst_ref=dst, send_sem=out_sem, recv_sem=in_sem,
        device_id=(to,), device_id_type=pl.DeviceIdType.MESH,
    )


def greet(me):
    barrier = pltpu.get_barrier_semaphore()
    for bit in PARTNERS:
        pl.semaphore_signal(barrier, inc=1, device_id=(flip(me, bit),), device_id_type=pl.DeviceIdType.MESH)
    pl.semaphore_wait(barrier, len(PARTNERS))


class Scatter:
    def __init__(self, me, pays, refs, out, swapped=0):
        self.me, self.pays, self.out, self.swapped = me, pays, out, swapped
        (self.keep, self.came0, self.came1, self.came2, self.came3,
         self.load_sem, self.out_sem, self.in_sem) = refs
        self.ticks = self.keep.shape[0]
        self.loads = sum(kept.shape[3] for kept, _ in pays) // PAIR * PARTS
        self.part_width = self.keep.shape[5]

    @staticmethod
    def scratch(ticks, width):
        def held(*dims):
            return pltpu.VMEM((ticks,) + dims + (width,), BF16)

        return [
            held(4, 2, 2, PAIR), held(4, 2, 2, PAIR), held(2, 4, 2, HALF), held(2, 4, HALF), held(3, PAIR),
            pltpu.SemaphoreType.DMA((ticks,)), pltpu.SemaphoreType.DMA((8, ticks)), pltpu.SemaphoreType.DMA((8, ticks)),
        ]

    def link(self, stage, p, src, dst, bit):
        return remote(src, dst, self.out_sem.at[stage, p], self.in_sem.at[stage, p], flip(self.me, bit))

    def load(self, p, kept, at):
        return pltpu.make_async_copy(
            kept.at[:, :, :, pl.ds(at, PAIR), pl.ds((p % PARTS) * self.part_width, self.part_width)], self.keep.at[p], self.load_sem.at[p]
        )

    def loaded(self, p):
        return pltpu.make_async_copy(self.came0.at[p], self.keep.at[p], self.load_sem.at[p])

    def put(self, target, p, block, rows):
        for part in range(PARTS):
            target.at[(p * PARTS + part, *block)][...] = rows[:, part * self.part_width : (part + 1) * self.part_width]

    def swap(self, p, sent):
        return self.link(0, p, sent, self.came0.at[p], CORE)

    def hop(self, stage, p):
        keep, up, down = self.keep, pl.ds(0, HALF), pl.ds(HALF, HALF)
        if stage == 1:
            return self.link(1, p, keep.at[p, :, :, 1, up], self.came1.at[p, 0], XBIT)
        if stage == 2:
            return self.link(2, p, keep.at[p, :, 1, :, down], self.came1.at[p, 1], YBIT)
        if stage == 3:
            return self.link(3, p, keep.at[p, :, 1, 0, up], self.came2.at[p, 0], YBIT)
        if stage == 4:
            return self.link(4, p, keep.at[p, :, 0, 1, down], self.came2.at[p, 1], XBIT)
        z = stage - 4
        return self.link(stage, p, keep.at[p, z, 0, 0], self.came3.at[p, z - 1], (NEAR, FAR, BOTH)[z - 1])

    def begin(self):
        greet(self.me)
        p = 0
        for kept, sent in self.pays:
            for at in range(0, kept.shape[3] * PARTS, PAIR):
                row = at // (PAIR * PARTS) * PAIR
                self.load(p, kept, row).start()
                cut = pl.ds((p % PARTS) * self.part_width, self.part_width)
                self.swap(p, sent.at[:, :, :, pl.ds(row, PAIR), cut]).start()
                p += 1

    def total(self, p, z, y, x, h, depth):
        cut = slice(h * HALF, h * HALF + HALF)
        sum_ = self.keep[p, z, y, x, cut, :].astype(F32) + self.came0[p, z, y, x, cut, :].astype(F32)
        if depth > 1:
            sum_ = sum_ + self.came1[p, h, z, y if h == 0 else x].astype(F32)
        if depth > 2:
            sum_ = sum_ + self.came2[p, h, z].astype(F32)
        if depth > 3:
            for other in range(3):
                sum_ = sum_ + self.came3[p, other, cut, :].astype(F32)
        return sum_

    def sums(self, p, blocks, h, depth):
        for z, y, x in blocks:
            self.keep[p, z, y, x, h * HALF : h * HALF + HALF, :] = self.total(p, z, y, x, h, depth).astype(BF16)

    def ticks_of(self, t):
        def one(i, _):
            self.tick(t * PARTS + i)
            return 0

        lax.fori_loop(0, PARTS, one, 0)

    def tick(self, t):
        ticks = self.ticks

        def stage(at):
            return pl.when((t >= at * LAG) & (t < ticks + at * LAG))

        if self.pays:
            @pl.when((t >= 0) & (t < self.loads))
            def _():
                self.loaded(t).wait()

        @stage(0)
        def _():
            self.swap(t, self.came0.at[t]).wait_recv()
            self.sums(t, [(z, y, 1) for z in range(4) for y in range(2)], 0, 1)
            self.hop(1, t).start()
            self.sums(t, [(z, 1, x) for z in range(4) for x in range(2)], 1, 1)
            self.hop(2, t).start()

        @stage(1)
        def _():
            p = t - 1 * LAG
            self.hop(1, p).wait_recv()
            self.sums(p, [(z, 1, 0) for z in range(4)], 0, 2)
            self.hop(3, p).start()
            self.hop(2, p).wait_recv()
            self.sums(p, [(z, 0, 1) for z in range(4)], 1, 2)
            self.hop(4, p).start()

        @stage(2)
        def _():
            p = t - 2 * LAG
            self.hop(3, p).wait_recv()
            self.hop(4, p).wait_recv()
            for z in (2, 3, 1):
                for h in range(2):
                    self.sums(p, [(z, 0, 0)], h, 3)
                self.hop(4 + z, p).start()

        @stage(3)
        def _():
            p = t - 3 * LAG
            for z in (1, 2, 3):
                self.hop(4 + z, p).wait_recv()
            for z in range(1, 8):
                self.hop(z, p).wait_send()

            @pl.when(p >= self.swapped)
            def _():
                self.swap(p, self.came0.at[p]).wait_send()

            for h in range(2):
                at = pl.ds(pl.multiple_of(lax.div(p, PARTS) * PAIR + h * HALF, HALF), HALF)
                cut = pl.ds(pl.multiple_of(lax.rem(p, PARTS) * self.part_width, 128), self.part_width)
                self.out[at, cut] = self.total(p, 0, 0, 0, h, 4)


def weight_blocks(held, me, store):
    low = lax.rem(me, 8)
    for j in range(8):
        rows = held[pl.ds(pl.multiple_of(flip(low, j) * 32, 32), 32), :].astype(BF16)
        store(j // 4, (j // 2) % 2, j % 2, rows)


def group_at(me, z):
    high = flip(lax.div(me, 8), z)
    return pl.ds(pl.multiple_of(high * 256, 256), 256)


def once(dims):
    return pl.BlockSpec(dims, lambda *_: (0,) * len(dims), pipeline_mode=pl.Buffered(1))


def weight_once(at):
    return pl.BlockSpec((BLOCKS, 32, 1024), lambda *_: (0, at, 0), pipeline_mode=pl.Buffered(1))


class Gather:
    def __init__(self, me, g, shift, own, own_sem, local_sem, out_sem, in_sem):
        self.me, self.g, self.shift, self.own = me, g, shift, own
        self.own_sem, self.local_sem, self.out_sem, self.in_sem = own_sem, local_sem, out_sem, in_sem
        self.c, self.x, self.y = [lax.rem(lax.div(me, bit), 2) for bit in (CORE, XBIT, YBIT)]
        self.z = lax.div(me, NEAR)
        self.ticks = g.shape[4] // PAIR

    @staticmethod
    def scratch(ticks, width):
        return [pltpu.VMEM((ticks, PAIR, width), BF16)] + [pltpu.SemaphoreType.DMA((ticks,))] * 2 + [pltpu.SemaphoreType.DMA((8, ticks)), pltpu.SemaphoreType.DMA((8, ticks))]

    def rows(self, p):
        return pl.ds(pl.multiple_of(lax.rem(p + self.shift, self.ticks) * PAIR, PAIR), PAIR)

    def half(self, p, h):
        return pl.ds(pl.multiple_of(lax.rem(p + self.shift, self.ticks) * PAIR + h * HALF, HALF), HALF)

    def mine(self, p):
        return self.g.at[self.z, self.y, self.x, self.c, self.rows(p)]

    def load(self, p, src):
        return pltpu.make_async_copy(src, self.own.at[p], self.own_sem.at[p])

    def local(self, p):
        return pltpu.make_async_copy(self.own.at[p], self.mine(p), self.local_sem.at[p])

    def hop(self, stage, p):
        g, every = self.g, slice(None)
        if stage < 3:
            to = flip(self.me, (NEAR, FAR, BOTH)[stage])
            return remote(self.own.at[p], self.mine(p), self.out_sem.at[stage, p], self.in_sem.at[stage, p], to)
        if stage == 3:
            ref, bits = g.at[every, self.y, self.x, self.c, self.half(p, 0)], XBIT
        elif stage == 4:
            ref, bits = g.at[every, self.y, self.x, self.c, self.half(p, 1)], YBIT
        elif stage == 5:
            ref, bits = g.at[every, self.y, every, self.c, self.half(p, 0)], YBIT
        elif stage == 6:
            ref, bits = g.at[every, every, self.x, self.c, self.half(p, 1)], XBIT
        else:
            ref, bits = g.at[every, every, every, self.c, self.rows(p)], CORE
        return remote(ref, ref, self.out_sem.at[stage, p], self.in_sem.at[stage, p], flip(self.me, bits))

    def begin(self, sources):
        for p, src in enumerate(sources):
            self.load(p, src).start()
        greet(self.me)

    def tick(self, t):
        def stage(at):
            return pl.when((t >= at * GATHER_LAG) & (t < self.ticks + at * GATHER_LAG))

        @stage(0)
        def _():
            self.load(t, self.mine(t)).wait()
            for k in (1, 2, 0):
                self.hop(k, t).start()
            self.local(t).start()

        @stage(1)
        def _():
            p = t - GATHER_LAG
            for k in range(3):
                self.hop(k, p).wait_recv()
            self.local(p).wait()
            self.hop(3, p).start()
            self.hop(4, p).start()

        @stage(2)
        def _():
            p = t - 2 * GATHER_LAG
            self.hop(3, p).wait_recv()
            self.hop(5, p).start()
            self.hop(4, p).wait_recv()
            self.hop(6, p).start()

        @stage(3)
        def _():
            p = t - 3 * GATHER_LAG
            self.hop(5, p).wait_recv()
            self.hop(6, p).wait_recv()
            self.hop(7, p).start()

        @stage(4)
        def _():
            p = t - 4 * GATHER_LAG
            self.hop(7, p).wait_recv()
            for k in range(8):
                self.hop(k, p).wait_send()


def forward_body(cross_live, self_live, tokens, *refs):
    sources, (inner, outer, memory_in), g = refs[:9], refs[9:12], refs[12]
    outs, held = refs[13:30], refs[30:47]
    weights, vec_rows, memory, load_sem, store_sem = refs[47:52]
    keys, values, q, k, v, mix, summed, first, low, cq, lse, cmix, clse, second_sum, second, second_low, vecs = held
    step = pl.program_id(0)
    me = lax.axis_index("dp").astype(jnp.int32)
    engine = Gather(me, g, 8, *refs[52:])
    count, width = tokens.shape
    pairs = width // 128
    ready = 4 * GATHER_LAG + 1

    def load(at):
        every = slice(None)
        target = vec_rows if at == VEC else weights.at[at if at < VEC else at - 1]
        return pltpu.make_async_copy(g.at[every, every, every, every, engine.rows(at)], target, load_sem.at[at])

    def weight_of(at):
        load(at).wait()
        return weights[at if at < VEC else at - 1].reshape(width, width)

    def load_memory():
        return pltpu.make_async_copy(memory_in, memory, load_sem.at[9])

    def store(*which):
        for at in which:
            pltpu.make_async_copy(held[at], outs[at], store_sem.at[at]).start()

    def on(at):
        return pl.when(step == at)

    @on(0)
    def _():
        load_memory().start()
        parts = [inner.at[:, pl.ds(i, width)] for i in range(0, inner.shape[1], width)]
        parts += [outer.at[pl.ds(i, PAIR)] for i in range(0, outer.shape[0], PAIR)]
        engine.begin(list(sources) + parts)

    tile = 512

    @on(ready)
    def _():
        load_memory().wait()
        factor = weight_of(0)
        for at in range(0, memory.shape[0], tile):
            keys[at : at + tile, :] = nn(memory[at : at + tile, :], factor).astype(BF16)
        store(0)

    @on(ready + 1)
    def _():
        factor = weight_of(1)
        for at in range(0, memory.shape[0], tile):
            values[at : at + tile, :] = nn(memory[at : at + tile, :], factor).astype(BF16)
        store(1)

    for at, rows in ((2, q), (3, k), (4, v)):
        @on(ready + at)
        def _(at=at, rows=rows):
            rows[...] = nn(tokens[...], weight_of(at)).astype(BF16)
            store(at)

    @on(ready + VEC)
    def _():
        load(VEC).wait()
        total = jnp.zeros((16, width), F32)
        for z in range(4):
            for y in range(2):
                for x in range(2):
                    for c in range(2):
                        total = total + vec_rows[z, y, x, c, :16, :].astype(F32)
        vecs[...] = total
        self_attention(self_live[0], q, k, v, mix, lse)
        store(16, 5, 10)

    @on(ready + 6)
    def _():
        total = tokens[...].astype(F32) + nn(mix[...], weight_of(6))
        summed[...] = total
        normal, _ = norm_parts(total)
        rows = normal * vecs[0:1, :] + vecs[1:2, :]
        first[...] = rows
        low[...] = rows.astype(BF16)
        store(6, 7, 8)

    @on(ready + 7)
    def _():
        cq[...] = nn(low[...], weight_of(7)).astype(BF16)
        store(9)

    each = 2
    start = ready + 8

    @pl.when((step >= start) & (step < start + pairs // each))
    def _():
        for part in range(each):
            pair = (step - start) * each + part
            cut = pl.ds(pl.multiple_of(pair * 128, 128), 128)
            cross_body(
                cross_live, cq.at[:, cut], keys.at[:, cut], values.at[:, cut], cmix.at[:, cut], clse.at[pl.ds(pair, 1)]
            )

    @on(start + pairs // each)
    def _():
        second_rows(cmix[...], weight_of(8), first[...], vecs, second_sum, second, second_low)
        store(11, 12, 13, 14, 15)

    engine.tick(step)

    for at in range(9):
        @on(at + 4 * GATHER_LAG)
        def _(at=at):
            load(at).start()

    @on(pl.num_programs(0) - 1)
    def _():
        for at in range(17):
            pltpu.make_async_copy(held[at], outs[at], store_sem.at[at]).wait()


VEC = 5


def forward_beside(cross_live, self_live, tokens, sources, inner, outer, memory):
    count, width = tokens.shape
    slots = memory.shape[0]
    pairs = width // 128
    rows = PAIR * len(sources) + inner.shape[0] * inner.shape[1] // width + outer.shape[0]
    ticks = rows // PAIR
    low, wide = shape(tokens.shape, BF16), shape(tokens.shape, F32)
    large = shape(memory.shape, BF16)
    parts = [
        large, large, low, low, low, low, wide, wide, low, low, shape((128, count), F32),
        low, shape((pairs, 8, count), F32), wide, wide, low, shape((16, width), F32),
    ]
    scalar = pl.BlockSpec(memory_space=pltpu.SMEM)
    hbm = pl.BlockSpec(memory_space=pl.ANY)
    block = (4, 2, 2, 2)
    out = pl.pallas_call(
        forward_body,
        grid=(ticks + 4 * GATHER_LAG + 1,),
        out_shape=[shape(block + (rows, width), BF16)] + parts,
        in_specs=[scalar, scalar, once(tokens.shape)] + [hbm] * (len(sources) + 3),
        out_specs=[hbm] * (1 + len(parts)),
        scratch_shapes=[pltpu.VMEM(part.shape, part.dtype) for part in parts]
        + [pltpu.VMEM((8,) + block + (PAIR, width), BF16), pltpu.VMEM(block + (PAIR, width), BF16), pltpu.VMEM(memory.shape, BF16)]
        + [pltpu.SemaphoreType.DMA((10,)), pltpu.SemaphoreType.DMA((len(parts),))]
        + Gather.scratch(ticks, width),
        compiler_params=pltpu.CompilerParams(collective_id=0, has_side_effects=True, vmem_limit_bytes=60 * MIB),
        cost_estimate=pl.CostEstimate(flops=6 * slots * width * width, bytes_accessed=90 * MIB, transcendentals=0),
        name="forward_beside_gather",
    )(cross_live, self_live, tokens, *sources, inner, outer, memory)
    return out[0].reshape(BLOCKS, rows, width), out[1:]


def blocks_of(pay):
    return pay.reshape((4, 2, 2) + pay.shape[1:])


def back_body(
    cross_live, self_live, q, k, v, mixture, lse, vecs, slse, third_grads,
    act_in, go_in, low_in, slope_in, gts_in, second_in, sum_in, sq_in, sk_in, sv_in, smix_in, tokens_in, stack,
    dk_o, dv_o, own, dq_o, gci_o, tokens_grad, self_keep, self_send, *scratch,
):
    refs, scratch = scratch[:8], scratch[8:]
    sent, weights, slopes, hidden, gss, second_sum, first_sum, gfs = scratch[:8]
    go, low, gci, gcm, dq, sq, sk, sv, smix, tokens, gsi, gq, gk, gv = scratch[8:22]
    grads, held, staged, load_sem, store_sem = scratch[22:]
    step = pl.program_id(0)
    me = lax.axis_index("dp").astype(jnp.int32)
    engine = Scatter(me, [], refs, own, 4 * PARTS)
    width = dq.shape[1]
    pairs = width // 128
    first_pair = 4
    after = first_pair + pairs

    def load(at, src, dst):
        return pltpu.make_async_copy(src, dst, load_sem.at[at])

    def store(at, src, dst):
        return pltpu.make_async_copy(src, dst, store_sem.at[at])

    act_load, go_load = load(0, act_in, hidden), load(1, go_in, go)
    ffn_loads = [load(2, low_in, low), load(3, gts_in, gss), load(4, second_in, second_sum)]
    self_loads = [
        load(5 + at, src, dst)
        for at, (src, dst) in enumerate(
            [(sum_in, first_sum), (sq_in, sq), (sk_in, sk), (sv_in, sv), (smix_in, smix), (tokens_in, tokens)]
        )
    ]

    def load_slope(part):
        return load(11 + part % 2, slope_in.at[:, pl.ds(part * width, width)], slopes.at[part % 2])

    def load_outer(part):
        return load(13, stack.at[pl.ds(8 * part, 8), pl.ds(128, 128)], weights.at[0].reshape(8, 128, width))

    def load_square(at, slot):
        return load(13 + slot, stack.at[:, pl.ds(at * 32, 32)], weights.at[slot])

    def on(at):
        return pl.when(step == at)

    def swaps(chunks):
        return [engine.swap(p, sent.at[p % (4 * PARTS)]) for p in range(chunks[0] * PARTS, (chunks[-1] + 1) * PARTS)]

    @on(0)
    def _():
        act_load.start()
        go_load.start()
        load_outer(0).start()
        load_square(0, 1).start()
        for part in range(2):
            load_slope(part).start()
        for copy in ffn_loads + self_loads:
            copy.start()
        greet(me)
        act_load.wait()
        go_load.wait()
        for z in range(4):
            group = flip(lax.div(me, 8), z)
            for part in range(4):
                columns = pl.ds(pl.multiple_of(group * 1024 + part * 256, 256), 256)
                held[pl.ds(part * 256, 256), :] = tn(hidden[:, columns], go[...]).astype(BF16)
            for j in range(8):
                row = pl.multiple_of(flip(lax.rem(me, 8), j) * 128, 128)
                for p in range(4):
                    rows = held[pl.ds(row + p * 32, 32), :]
                    engine.put(sent if j % 2 else engine.keep, p, (z, j // 4, (j // 2) % 2), rows)
        for copy in swaps(range(4)):
            copy.start()

    for at in (1, 2):
        @on(at)
        def _(at=at):
            if at == 1:
                for copy in ffn_loads:
                    copy.wait()
            for part in (2 * at - 2, 2 * at - 1):
                load_outer(part).wait()
                grad = nt(go[...], whole(weights.at[0]))
                if part < 3:
                    load_outer(part + 1).start()
                else:
                    load_square(16, 0).start()
                load_slope(part).wait()
                rows = (grad * slopes[part % 2]).astype(BF16)
                if part < 2:
                    load_slope(part + 2).start()
                hidden[:, part * width : part * width + width] = rows
                load_square(part, 1).wait()
                gss[...] += nt(rows, whole(weights.at[1]))
                load_square(part + 1 if part < 3 else 15, 1).start()
            if at == 2:
                grad, gain, shift = norm_back(second_sum[...], vecs[2:3, :], gss[...])
                gss[...] = grad
                rows = grad.astype(BF16)
                gci[...] = rows
                load_square(16, 0).wait()
                gcm[...] = nt(rows, whole(weights.at[0])).astype(BF16)
                load_square(14, 0).start()
                grads[2:3, :] = gain
                grads[3:4, :] = shift
                grads[4:6, :] = third_grads[0:2, :]
                grads[8:32, :] = jnp.zeros((24, width), F32)
                store(0, gci, gci_o).start()

    @on(3)
    def _():
        for copy in swaps(range(4)):
            copy.wait_send()
        for part in range(4):
            for z in range(4):
                held[:256, :] = tn(low[:, group_at(me, z)], hidden[:, part * width : part * width + width]).astype(BF16)

                def put(y, x, c, rows, z=z, part=part):
                    engine.put(sent if c else engine.keep, part if c else 4 + part, (z, y, x), rows)

                weight_blocks(held, me, put)
        for copy in swaps(range(4, 8)):
            copy.start()

    @pl.when((step >= first_pair) & (step < after))
    def _():
        cut = pl.ds(pl.multiple_of((step - first_pair) * 128, 128), 128)
        cross_back_body(cross_live, q, k, v, gcm.at[:, cut], mixture, lse, dq.at[:, cut], dk_o, dv_o)

    @on(after)
    def _():
        store(1, dq, dq_o).start()
        for copy in self_loads:
            copy.wait()
        load_square(15, 1).wait()
        load_square(14, 0).wait()
        self_back_body(
            self_live, gss, dq, weights.at[1], first_sum, weights.at[0], vecs, sq, sk, sv, smix, slse,
            gfs, gsi, gq, gk, gv, second_sum.at[pl.ds(0, 8)],
        )
        grads[0:2, :] = second_sum[0:2, :]
        load_square(10, 0).start()
        load_square(11, 1).start()

    def stores(z):
        return [store(2 + 2 * (z % 2) + c, staged.at[z % 2, c], (self_send if c else self_keep).at[z]) for c in range(2)]

    for z in range(4):
        @on(after + 1 + z // 2)
        def _(z=z):
            if z >= 2:
                for copy in stores(z - 2):
                    copy.wait()
            columns = group_at(me, z)
            for at, (rows, grad) in enumerate([(tokens, gq), (tokens, gk), (tokens, gv), (smix, gsi)]):
                held[:256, :] = tn(rows[:, columns], grad[...]).astype(BF16)

                def put(y, x, c, rows, at=at):
                    staged[z % 2, c, y, x, at * 32 : at * 32 + 32, :] = rows

                weight_blocks(held, me, put)
            rows = grads[...].astype(BF16)
            for y in range(2):
                for x in range(2):
                    for c in range(2):
                        staged[z % 2, c, y, x, 128:160, :] = rows
            for copy in stores(z):
                copy.start()
            if z == 0:
                load_square(10, 0).wait()
                gfs[...] += nt(gq[...], whole(weights.at[0]))
                load_square(12, 0).start()
            if z == 1:
                load_square(11, 1).wait()
                gfs[...] += nt(gk[...], whole(weights.at[1]))
            if z == 2:
                load_square(12, 0).wait()
                gfs[...] += nt(gv[...], whole(weights.at[0]))
                store(6, gfs, tokens_grad).start()

    @pl.when((step < first_pair) | (step >= after) | (lax.rem(step, 2) == 1))
    def _():
        engine.ticks_of(step - jnp.clip(lax.div(step - first_pair + 1, 2), 0, pairs // 2))

    @on(pl.num_programs(0) - 1)
    def _():
        for copy in [store(0, gci, gci_o), store(1, dq, dq_o), store(6, gfs, tokens_grad)] + stores(2) + stores(3):
            copy.wait()


def backward_beside(
    cross_live, self_live, q, k, v, mixture, lse, vecs, slse, third_grads,
    act, go, low, slope, gts, second_sum, first_sum, sq, sk, sv, smix, tokens, stack,
):
    count, width = q.shape
    slots = k.shape[0]
    last = width // 128 - 1

    def pair(i):
        return jnp.clip(i - 4, 0, last)

    ticks = 8
    small = pl.BlockSpec((count, 128), lambda i: (0, pair(i)))
    large = pl.BlockSpec((slots, 128), lambda i: (0, pair(i)))
    scalar = pl.BlockSpec(memory_space=pltpu.SMEM)
    hbm = pl.BlockSpec(memory_space=pl.ANY)
    pay_shape = shape((4, 2, 2, 160, width), BF16)
    wide = pltpu.VMEM(q.shape, F32)
    thin = pltpu.VMEM(q.shape, BF16)
    dk, dv, own, dq, gci, tokens_grad, self_keep, self_send = pl.pallas_call(
        back_body,
        grid=(last + 1 + 7,),
        out_shape=[
            shape(k.shape, BF16), shape(k.shape, BF16), shape((ticks * PAIR, width), F32),
            shape(q.shape, BF16), shape(q.shape, BF16), shape(q.shape, F32), pay_shape, pay_shape,
        ],
        in_specs=[
            scalar, scalar, small, large, large, small, pl.BlockSpec((1, 8, count), lambda i: (pair(i), 0, 0)),
            once(vecs.shape), once(slse.shape), once(third_grads.shape),
        ] + [hbm] * 13,
        out_specs=[large, large, full((ticks * PAIR, width))] + [hbm] * 5,
        scratch_shapes=Scatter.scratch(ticks * PARTS, width // PARTS)
        + [
            pltpu.VMEM((4 * PARTS, 4, 2, 2, PAIR, width // PARTS), BF16), pltpu.VMEM((2, BLOCKS, 32, width), BF16),
            pltpu.VMEM((2, count, width), F32), pltpu.VMEM(act.shape, BF16),
        ]
        + [wide] * 4 + [thin] * 14
        + [
            pltpu.VMEM((32, width), F32), pltpu.VMEM((1024, width), BF16), pltpu.VMEM((2, 2, 2, 2, 160, width), BF16),
            pltpu.SemaphoreType.DMA((15,)), pltpu.SemaphoreType.DMA((7,)),
        ],
        compiler_params=pltpu.CompilerParams(collective_id=1, has_side_effects=True, vmem_limit_bytes=63 * MIB),
        cost_estimate=pl.CostEstimate(flops=70 * count * slots * width, bytes_accessed=80 * MIB, transcendentals=0),
        name="backward_beside_sum",
    )(
        cross_live, self_live, q, k, v, mixture, lse, vecs, slse, third_grads,
        act, go, low, slope, gts, second_sum, first_sum, sq, sk, sv, smix, tokens, stack,
    )
    return dq, dk, dv, gci, tokens_grad, (self_keep, self_send), own


def finish_body(
    first_low, dq, mixture, gci, memory_in, dk_in, dv_in, stack, self_keep, self_send, memory_grad, own, *scratch
):
    refs, (sent, held, memory, dk, dv, weights, load_sem) = scratch[:8], scratch[8:]
    step = pl.program_id(0)
    me = lax.axis_index("dp").astype(jnp.int32)
    engine = Scatter(me, [(self_keep, self_send)], refs, own)
    early = engine.loads // PARTS
    tile = memory_grad.shape[0]
    loads = [
        pltpu.make_async_copy(src, dst, load_sem.at[at])
        for at, (src, dst) in enumerate(
            [(memory_in, memory), (dk_in, dk), (dv_in, dv)]
            + [(stack.at[:, pl.ds((8 + slot) * 32, 32)], weights.at[slot]) for slot in range(2)]
        )
    ]

    def on(at):
        return pl.when(step == at)

    @on(0)
    def _():
        engine.begin()
        for load in loads:
            load.start()

    def weight(w, rows, grad, groups):
        for z in groups:
            held[...] = tn(rows[:, group_at(me, z)], grad[...])

            def put(y, x, c, rows, z=z):
                engine.put(sent if c else engine.keep, w if c else early + w, (z, y, x), rows)

            weight_blocks(held, me, put)

    def swap(w):
        for part in range(PARTS):
            engine.swap((early + w) * PARTS + part, sent.at[w * PARTS + part]).start()

    for w, rows, grad in ((0, first_low, dq), (1, mixture, gci)):
        @on(w)
        def _(w=w, rows=rows, grad=grad):
            weight(w, rows, grad, range(4))
            swap(w)

    for w, rows, grad in ((2, memory, dk), (3, memory, dv)):
        for z in range(4):
            @on((w - 2) * 4 + z + 1)
            def _(w=w, rows=rows, grad=grad, z=z):
                if z == 0:
                    for load in loads[:2] if w == 2 else loads[2:]:
                        load.wait()
                weight(w, rows, grad, (z,))
                if z == 3:
                    swap(w)

    @pl.when((step >= FIRST_TILE) & (step < FIRST_TILE + dk.shape[0] // tile))
    def _():
        at = pl.ds(pl.multiple_of((step - FIRST_TILE) * tile, tile), tile)
        memory_grad[...] = nt(dk[at, :], whole(weights.at[0])) + nt(dv[at, :], whole(weights.at[1]))

    engine.ticks_of(step)


def finish(memory, dk, dv, first_low, dq, mixture, gci, stack, self_pay):
    slots, width = memory.shape
    tile = 512
    tiles = slots // tile
    ticks = self_pay[0].shape[3] // PAIR + 4
    hbm = pl.BlockSpec(memory_space=pl.ANY)
    square = once(dq.shape)
    large = pltpu.VMEM(memory.shape, BF16)
    return pl.pallas_call(
        finish_body,
        grid=(max(FIRST_TILE + tiles, ticks + -(-3 * LAG // PARTS)),),
        out_shape=[shape(memory.shape, F32), shape((ticks * PAIR, width), F32)],
        in_specs=[square, square, square, square] + [hbm] * 6,
        out_specs=[pl.BlockSpec((tile, width), lambda i: (jnp.clip(i - FIRST_TILE, 0, tiles - 1), 0)), full((ticks * PAIR, width))],
        scratch_shapes=Scatter.scratch(ticks * PARTS, width // PARTS)
        + [pltpu.VMEM((4 * PARTS, 4, 2, 2, PAIR, width // PARTS), BF16), pltpu.VMEM((256, width), F32), large, large, large]
        + [pltpu.VMEM((2, BLOCKS, 32, width), BF16), pltpu.SemaphoreType.DMA((5,))],
        compiler_params=pltpu.CompilerParams(collective_id=2, has_side_effects=True, vmem_limit_bytes=62 * MIB),
        cost_estimate=pl.CostEstimate(flops=8 * slots * width * width, bytes_accessed=60 * MIB, transcendentals=0),
        name="finish_beside_sum",
    )(first_low, dq, mixture, gci, memory, dk, dv, stack, *self_pay)


def unpack_body(memory_in, tokens_in, ffn, owned, memory_grad, tokens_grad, outer, inner, *squares):
    memory_grad[...] = memory_in[...]

    @pl.when(pl.program_id(0) == 0)
    def _():
        width = ffn.shape[1]
        tokens_grad[...] = tokens_in[...]
        outer[...] = ffn[:128, :]
        for part in range(4):
            inner[:, part * width : part * width + width] = ffn[128 + part * 32 : 160 + part * 32, :]
        for at, square in zip(OWNED, squares):
            square[...] = owned[at : at + 32, :]


def unpack(memory_grad, tokens_grad, ffn, owned):
    width = ffn.shape[1]
    tile = 512
    wide = pl.BlockSpec((tile, width), lambda i: (i, 0))
    outs = [(128, width), (32, 4 * width)] + [(32, width)] * len(OWNED)
    return call(
        unpack_body, "unpack",
        [shape(memory_grad.shape, F32), shape(tokens_grad.shape, F32)] + [shape(dims, F32) for dims in outs],
        (memory_grad.shape[0] // tile,),
        [wide, once(tokens_grad.shape), once(ffn.shape), once(owned.shape)],
        [wide, full(tokens_grad.shape)] + [full(dims) for dims in outs],
        flops=0, moved=22 * MIB,
    )(memory_grad, tokens_grad, ffn, owned)


OWNED = (0, 32, 64, 96, 160, 224, 256, 192)


def absolute(keep, send):
    return jnp.stack([keep, send], axis=1).reshape((BLOCKS,) + keep.shape[1:])


def gather(rows):
    return lax.all_gather(rows, "dp", axis=0, tiled=True)


def on_device(
    devices, tokens, memory, target_lengths, memory_lengths, cotangent,
    self_query, self_key, self_value, self_output, first_gain, first_shift,
    cross_query, cross_key, cross_value, cross_output, second_gain, second_shift,
    inner_weight, outer_weight, third_gain, third_shift,
):
    width = tokens.shape[1]
    hidden = inner_weight.shape[1]
    direct = devices == BLOCKS
    squares = [cross_key, cross_value, self_query, self_key, self_value, self_output, cross_query, cross_output]
    vectors = [first_gain, first_shift, second_gain, second_shift, third_gain, third_shift]
    if direct:
        place_of = lax.axis_index("dp").astype(jnp.int32)
        me = place_of.reshape(1)
        own = lax.dynamic_update_slice(jnp.zeros((32, width), BF16), jnp.stack(vectors), (0, place_of * 32))
        stack, parts = forward_beside(
            memory_lengths, target_lengths, tokens, squares[:VEC] + [own] + squares[VEC:], inner_weight, outer_weight, memory
        )
        (keys, values, q, k, v, mixture, first_sum, first_out, first_low, cross_q, lse,
         cross_mixture, cross_lse, second_sum, second, second_low, vecs) = parts
    else:
        me = jnp.zeros((1,), jnp.int32)
        inner_full = gather(inner_weight)
        parts = [inner_full[:, i : i + width].reshape(BLOCKS, 32, width) for i in range(0, hidden, width)]
        parts.append(gather(outer_weight).reshape(BLOCKS, 128, width))
        parts += [gather(w).reshape(BLOCKS, 32, width) for w in squares[:VEC]] + [jnp.zeros((BLOCKS, 32, width), BF16)]
        parts += [gather(w).reshape(BLOCKS, 32, width) for w in squares[VEC:]]
        stack = jnp.concatenate(parts, axis=1)
        vecs = jnp.pad(jnp.stack([gather(v) for v in vectors]), ((0, 10), (0, 0))).astype(F32)
        keys, values = kv_project(memory, stack, 8, 9)
        q, k, v, mixture, first_sum, first_out, first_low, cross_q, lse = self_forward(
            target_lengths, tokens, stack, (10, 11, 12, 14, 15), vecs
        )
        cross_mixture, cross_lse = cross_forward(memory_lengths, cross_q, keys, values)
        second_sum, second, second_low = second_norm(cross_mixture, stack, 16, first_out, vecs)

    act, slope, output_rows, gts, go, third_grads = ffn_forward(second_low, second, stack, cotangent, vecs)
    if direct:
        dq, dk, dv, gci, tokens_grad, self_pay, ffn_own = backward_beside(
            memory_lengths, target_lengths, cross_q, keys, values, cross_mixture, cross_lse, vecs, lse, third_grads,
            act, go, second_low, slope, gts, second_sum, first_sum, q, k, v, mixture, tokens, stack,
        )
        memory_grad, owned = finish(memory, dk, dv, first_low, dq, cross_mixture, gci, stack, self_pay)
        vec_rows = lax.dynamic_slice(owned, (128, me[0] * 32), (6, 32))
        vec_own = [vec_rows[i] for i in range(6)]
        memory_grad, tokens_grad, outer_own, inner_own, *squares_own = unpack(memory_grad, tokens_grad, ffn_own, owned)
        self_own, cross_own = squares_own[:4], squares_own[4:]
    else:
        gi, gss, gci, gcm, second_grads = ffn_backward(go, gts, slope, stack, second_sum, stack, 16, vecs)
        ffn_pay = ffn_weights(me, act, go, second_low, gi)
        dq, dk, dv = cross_backward(memory_lengths, cross_q, keys, values, gcm, cross_mixture, cross_lse)
        cross_pay = square_weights(
            me, [(first_low, dq), (memory, dk), (memory, dv), (cross_mixture, gci)], "cross_weights"
        )
        gfs, gsi, gq, gk, gv, first_grads = self_backward(
            target_lengths, gss, dq, stack, 15, 14, first_sum, vecs, q, k, v, mixture, lse
        )
        self_pay = square_weights(me, [(tokens, gq), (tokens, gk), (tokens, gv), (mixture, gsi)], "self_weights")
        memory_grad = memory_gradient(dk, dv, stack, 8, 9)
        tokens_grad = tokens_gradient(gfs, gq, gk, gv, stack, (10, 11, 12))

        def summed(rows):
            return lax.psum_scatter(rows.astype(F32), "dp", scatter_dimension=0, tiled=True)

        ffn_rows, cross_rows, self_rows = absolute(*ffn_pay), absolute(*cross_pay), absolute(*self_pay)
        outer_own = summed(ffn_rows[:, :128].reshape(-1, width))
        inner_own = summed(
            jnp.concatenate([ffn_rows[:, i : i + 32].reshape(-1, width) for i in range(128, 256, 32)], axis=1)
        )
        cross_own = [summed(cross_rows[:, i : i + 32].reshape(-1, width)) for i in range(0, 128, 32)]
        self_own = [summed(self_rows[:, i : i + 32].reshape(-1, width)) for i in range(0, 128, 32)]
        vec_own = [summed(rows[i]) for rows in (first_grads, second_grads, third_grads) for i in range(2)]

    return (
        output_rows, tokens_grad, memory_grad,
        *self_own, vec_own[0], vec_own[1],
        *cross_own, vec_own[2], vec_own[3],
        inner_own, outer_own, vec_own[4], vec_own[5],
    )


def solution(mesh):
    rows, line = P("dp", None), P("dp")
    block = [rows] * 4 + [line] * 2
    placed = (rows, rows, line, line, rows, *block, *block, rows, rows, line, line)
    return jax.shard_map(
        functools.partial(on_device, mesh.shape["dp"]),
        mesh=mesh,
        in_specs=placed,
        out_specs=(rows, rows, rows, *block, *block, rows, rows, line, line),
        check_vma=False,
    )
```
